512 devices in a mesh: ctx: 16 (over x, z_hi), dp: 8 (over y), tp: 4 (over z_lo, core).
Axes of the slice: x: 4, y: 8, z: 8 (z_hi: 4, z_lo: 2; z = z_hi * 2 + z_lo), core: 2. Of those that a mesh axis runs over, the one named last changes fastest.
Arguments:
- token_ids: int32 [4, 16], replicated, may hold values from 0 to 50279
- decode_prompt: int32 [16], replicated, may hold values from 0 to 15, as said below
- embedding: bfloat16 [50280, 4096], P('dp', ('ctx', 'tp')), may hold values from -6 to 6
- norm_gain: float32 [4096], replicated, may hold values from 0.1 to 1.9
- w_zx: bfloat16 [2, 128, 64, 4096], P(None, ('tp', 'ctx')), may hold values from -0.09375 to 0.09375
- w_bcdt: bfloat16 [4096, 384], P(None, ('ctx', 'tp')), may hold values from -0.09375 to 0.09375
- conv_x_weight: float32 [4, 128, 64], P(None, ('tp', 'ctx')), may hold values from -3 to 3
- conv_x_bias: float32 [128, 64], P(('tp', 'ctx')), may hold values from -3 to 3
- conv_bc_weight: float32 [4, 256], replicated, may hold values from -3 to 3
- conv_bc_bias: float32 [256], replicated, may hold values from -3 to 3
- dt_bias: float32 [128], P(('tp', 'ctx')), may hold values from -4 to -1
- a_log: float32 [128], P(('tp', 'ctx')), may hold values from 0 to 2.7
- d_skip: float32 [128], P(('tp', 'ctx')), may hold values from 0.5 to 1.5
- gate_norm_gain: float32 [128, 64], P(('tp', 'ctx')), may hold values from 0.1 to 1.9
- w_out: bfloat16 [128, 64, 4096], P(('tp', 'ctx')), may hold values from -0.0625 to 0.0625
- state_parts: bfloat16 [16, 16, 128, 64, 128], P('ctx', 'dp', 'tp'), may hold values from -6 to 6
- seg_rate: float32 [16, 16, 128], P('ctx', 'dp', 'tp'), may hold values from 0 to 2
- x_tail: bfloat16 [16, 3, 128, 64], P('dp', None, ('tp', 'ctx')), may hold values from -6 to 6
- bc_tail: bfloat16 [16, 3, 256], P('dp'), may hold values from -6 to 6
Outputs:
- mixer_out: bfloat16 [4, 16, 4096], P(None, 'dp', ('ctx', 'tp'))
- final_state: float32 [16, 128, 64, 128], P('dp', ('tp', 'ctx'))
The draws below stay inside these ranges and needn't reach their ends.
Inputs may be any that keep to these rules, and one draw needn't show every extreme that they name: decode_prompt is a permutation of the prompts; slot s is decoded by dp group s // 2, and prompt q is held by dp group q // 2; the 2 prompts held by one dp group are decoded by 2 different dp groups.
All inputs are finite; a program needn't handle non-finite values.
Results may differ from the reference program's by a relative error of at most 0.02.
Values may be sent and summed in bfloat16 or wider, within the bound.
No kernel may reach another device: no remote copies, remote signals or barrier semaphores. Data moves between devices by JAX's collectives and lax.ppermute only.
A program may use at most 64 MiB of HBM per device.

```python
import math
import jax
import jax.numpy as jnp
import numpy as np
from jax import lax

D = 4096
HEADS = 128
HEAD_DIM = 64
STATE = 128
VOCAB = 50280
CONV = 4
STEPS = 4
PR_DEV = 2
PROMPTS = 16
PREFILL_SEGMENTS = 16
N_DP = 8


def draw_decode_prompt(key, part):
    base = jax.random.fold_in(key, 11)
    key_label, key_offset, key_link, key_slot = jax.random.split(base, 4)
    label = jax.random.permutation(key_label, N_DP).astype(jnp.int32)
    owner = jnp.argsort(label).astype(jnp.int32)
    offsets = jax.random.permutation(key_offset, N_DP)[:PR_DEV].astype(jnp.int32)
    link_prompt = jax.vmap(lambda single: jax.random.permutation(single, PR_DEV))(jax.random.split(key_link, N_DP)).astype(jnp.int32)
    slot_order = jax.vmap(lambda single: jax.random.permutation(single, PR_DEV))(jax.random.split(key_slot, N_DP)).astype(jnp.int32)
    source = owner[(label[:, None] - offsets[None, :]) % N_DP]
    links = jnp.arange(PR_DEV, dtype=jnp.int32)[None, :]
    prompt = source * PR_DEV + link_prompt[source, links]
    slots = jnp.arange(N_DP, dtype=jnp.int32)[:, None] * PR_DEV + slot_order
    return jnp.zeros((N_DP * PR_DEV,), jnp.int32).at[slots.reshape(-1)].set(prompt.reshape(-1).astype(jnp.int32))


def draw_seg_rate(key, part):
    root_random_key = jax.random.fold_in(key, 23)
    plateau_random_key, quick_random_key, choose_random_key, jitter_random_key, spike_random_key, length_random_key = jax.random.split(root_random_key, 6)
    leading = (PROMPTS, HEADS)
    complete_shape = (PREFILL_SEGMENTS, PROMPTS, HEADS)
    slow_low, slow_high, fast_share, rough_low, rough_high = (0.1, 1.5, 0.25, 0.5, 1.5)
    slow_rate = jnp.exp(jax.random.uniform(plateau_random_key, leading, jnp.float32, math.log(slow_low), math.log(slow_high)))
    fast_rate = jnp.exp(jax.random.uniform(quick_random_key, leading, jnp.float32, math.log(2.0), math.log(5.0)))
    chosen = jax.random.uniform(choose_random_key, leading, jnp.float32) < fast_share
    plateau_rate = jnp.where(chosen, fast_rate, slow_rate) / PREFILL_SEGMENTS
    jitter_amount = jax.random.uniform(jitter_random_key, complete_shape, jnp.float32, rough_low, rough_high)
    spike_events = jax.random.uniform(spike_random_key, complete_shape, jnp.float32) < 1.0 / PREFILL_SEGMENTS
    spike_length = jax.random.uniform(length_random_key, complete_shape, jnp.float32, 0.22, 0.69)
    return (plateau_rate[None] * jitter_amount + jnp.where(spike_events, spike_length, 0.0)).astype(jnp.float32)


def touch_ends(drawn, stream_key, least, largest):
    index_at = [jax.random.randint(jax.random.fold_in(stream_key, axis), (), 0, length) for axis, length in enumerate(drawn.shape)]
    main_axis = drawn.shape.index(max(drawn.shape))
    beside = index_at[:main_axis] + [(index_at[main_axis] + 1) % drawn.shape[main_axis]] + index_at[main_axis + 1:]
    return drawn.at[tuple(index_at)].set(least).at[tuple(beside)].set(largest)


def spiked(result, key, source, target, parts, factor):
    owner, partner = [(jnp.arange(result.shape[axis_at]) // (result.shape[axis_at] // parts)).reshape([-1 if axis == axis_at else 1 for axis in range(result.ndim)]) for axis_at in (source, target)]
    chosen = jax.random.permutation(key, parts)[partner]
    strong = (owner == chosen) | (owner == (partner + parts // 2) % parts)
    return jnp.where(strong, factor * result, result)


def levels(key, extent, cuts, low, largest):
    level = 1.0
    for axis_at, parts in cuts:
        steps = jax.random.uniform(jax.random.fold_in(jax.random.fold_in(key, 6), axis_at), (parts,), jnp.float32, low / len(cuts), largest / len(cuts))
        level = level * jnp.repeat(jnp.exp(steps), extent[axis_at] // parts).reshape((-1,) + (1,) * (len(extent) - 1 - axis_at))
    return level


def rank_bounds(number_of, skew):
    weights = [(1 << 20) // math.isqrt(grade ** skew) + 1 for grade in range(1, number_of + 1)]
    width = 1 + sum(weights) // (1 << 30)
    return np.cumsum(np.array([max(1, weight // width) for weight in weights]))


def ranked_ids(stream_key, shape, amount, skew):
    listing = rank_bounds(amount, skew)
    pick = jax.random.randint(jax.random.fold_in(stream_key, 1), shape, 0, int(listing[amount - 1]))
    rank = jnp.searchsorted(jnp.asarray(listing, jnp.int32), pick, side="right")
    return jax.random.permutation(jax.random.fold_in(stream_key, 2), amount)[rank].astype(jnp.int32)


def gaussian(rng, shape, scale, most, pieces=(), kind=jnp.bfloat16):
    drawn = scale * jax.random.normal(rng, shape, jnp.float32)
    if pieces:
        drawn = drawn * levels(rng, shape, pieces, -0.22, 0.18)
    return jnp.clip(drawn, -most, most).astype(kind)


def gaussian_with(stream_key, dims, width, limit, shards, heavy, kind=jnp.bfloat16):
    entries = width * jax.random.normal(stream_key, dims, jnp.float32)
    if shards:
        entries = entries * levels(stream_key, dims, shards, -0.22, 0.18)
    return jnp.clip(spiked(entries, jax.random.fold_in(stream_key, 3), *heavy), -limit, limit).astype(kind)


def setup_inputs(seed: int = 0) -> dict:
    key_list = jax.random.split(jax.random.key(seed), 20)
    return {
        "token_ids": touch_ends(ranked_ids(key_list[0], (STEPS, PROMPTS), VOCAB, 2), jax.random.fold_in(key_list[0], 3), 0, VOCAB - 1).astype(jnp.int32),
        "decode_prompt": draw_decode_prompt(jax.random.fold_in(key_list[19], 71), 0),
        "embedding": gaussian(key_list[2], (VOCAB, D), 1.0, 6.0, ((0, 8), (1, 64))),
        "norm_gain": jnp.clip(1.0 + 0.18 * jax.random.normal(key_list[3], (D,), jnp.float32), 0.1, 1.9),
        "w_zx": gaussian(key_list[4], (2, HEADS, HEAD_DIM, D), D ** -0.5, 0.09375, ((1, 64),)),
        "w_bcdt": gaussian(key_list[5], (D, 2 * STATE + HEADS), D ** -0.5, 0.09375, ((1, 64),)),
        "conv_x_weight": gaussian(key_list[6], (CONV, HEADS, HEAD_DIM), CONV ** -0.5, 3.0, ((1, 64),), jnp.float32),
        "conv_x_bias": gaussian(key_list[7], (HEADS, HEAD_DIM), 0.5, 3.0, ((0, 64),), jnp.float32),
        "conv_bc_weight": gaussian(key_list[8], (CONV, 2 * STATE), CONV ** -0.5, 3.0, (), jnp.float32),
        "conv_bc_bias": gaussian(key_list[9], (2 * STATE,), 0.5, 3.0, (), jnp.float32),
        "dt_bias": jnp.clip(-4.0 + 3.0 * jax.random.uniform(key_list[10], (HEADS,), jnp.float32) ** levels(key_list[10], (HEADS,), ((0, 64),), -0.2, 0.2), -4.0, -1.0),
        "a_log": jnp.clip(2.7 * jax.random.uniform(key_list[11], (HEADS,), jnp.float32) ** levels(key_list[11], (HEADS,), ((0, 64),), -0.2, 0.2), 0.0, 2.7),
        "d_skip": jnp.clip(0.5 + 1.0 * jax.random.uniform(key_list[12], (HEADS,), jnp.float32) ** levels(key_list[12], (HEADS,), ((0, 64),), -0.2, 0.2), 0.5, 1.5),
        "gate_norm_gain": jnp.clip(1.0 + 0.18 * jax.random.normal(key_list[13], (HEADS, HEAD_DIM), jnp.float32), 0.1, 1.9),
        "w_out": gaussian(key_list[14], (HEADS, HEAD_DIM, D), (HEADS * HEAD_DIM) ** -0.5, 0.0625, ((0, 64),)),
        "state_parts": gaussian_with(key_list[15], (PREFILL_SEGMENTS, PROMPTS, HEADS, HEAD_DIM, STATE), 1.0, 6.0, ((0, 16), (1, 8), (2, 4)), (0, 2, 16, 2.0)),
        "seg_rate": draw_seg_rate(jax.random.fold_in(key_list[19], 71), 0),
        "x_tail": gaussian(key_list[17], (PROMPTS, CONV - 1, HEADS, HEAD_DIM), 1.0, 6.0, ((0, 8), (2, 64))),
        "bc_tail": gaussian(key_list[18], (PROMPTS, CONV - 1, 2 * STATE), 1.0, 6.0, ((0, 8),)),
    }


epsilon = 1e-05

def rms_scale(values, gain):
    return values * lax.rsqrt(lax.optimization_barrier(jnp.mean(values * values, axis=-1, keepdims=True)) + epsilon) * gain

def reference(token_ids, decode_prompt, embedding, norm_gain, w_zx, w_bcdt, conv_x_weight, conv_x_bias, conv_bc_weight, conv_bc_bias, dt_bias, a_log, d_skip, gate_norm_gain, w_out, state_parts, seg_rate, x_tail, bc_tail):
    suffix = jnp.cumsum(seg_rate[::-1], axis=0)[::-1] - seg_rate
    seg_weight = jnp.exp(-suffix)

    def add_segment(running, seg_index):
        segment_part = lax.dynamic_index_in_dim(state_parts, seg_index, 0, keepdims=False).astype(jnp.float32)
        factor = lax.dynamic_index_in_dim(seg_weight, seg_index, 0, keepdims=False)
        scaled = (factor[:, :, None, None] * segment_part).astype(jnp.bfloat16)
        scaled = lax.optimization_barrier(scaled)
        return (running + scaled.astype(jnp.float32), None)
    combined, _ = lax.scan(add_segment, jnp.zeros(state_parts.shape[1:], jnp.float32), jnp.arange(PREFILL_SEGMENTS, dtype=jnp.int32))
    ssm_state = combined[decode_prompt]
    x_window = x_tail[decode_prompt].astype(jnp.float32)
    bc_window = bc_tail[decode_prompt].astype(jnp.float32)
    slot_tokens = token_ids[:, decode_prompt]
    embedded = embedding[slot_tokens]
    normed = rms_scale(embedded.astype(jnp.float32), norm_gain).astype(jnp.bfloat16)
    projected = jnp.einsum('tpd,khed->ktphe', normed.astype(jnp.float32), w_zx.astype(jnp.float32))
    columns = jnp.einsum('tpd,dc->tpc', normed.astype(jnp.float32), w_bcdt.astype(jnp.float32))
    decay_rate = -jnp.exp(a_log)
    gated_steps = []
    for moment in range(STEPS):
        x_window = jnp.concatenate([x_window, projected[1, moment][:, None]], axis=1)
        bc_window = jnp.concatenate([bc_window, columns[moment, :, None, :2 * STATE]], axis=1)
        x_conv = jax.nn.silu(jnp.einsum('pkhe,khe->phe', x_window, conv_x_weight) + conv_x_bias)
        bc_conv = jax.nn.silu(jnp.einsum('pkn,kn->pn', bc_window, conv_bc_weight) + conv_bc_bias)
        step_size = jax.nn.softplus(columns[moment, :, 2 * STATE:] + dt_bias)
        retain = jnp.exp(step_size * decay_rate)
        ssm_state = retain[:, :, None, None] * ssm_state + (step_size[:, :, None] * x_conv)[:, :, :, None] * bc_conv[:, None, None, :STATE]
        output = jnp.einsum('phen,pn->phe', ssm_state, bc_conv[:, STATE:]) + d_skip[None, :, None] * x_conv
        gated_steps.append(output * jax.nn.silu(projected[0, moment]))
        x_window = x_window[:, 1:]
        bc_window = bc_window[:, 1:]
    gated_all = jnp.stack(gated_steps).reshape(STEPS, -1, HEADS * HEAD_DIM)
    normed_out = rms_scale(gated_all, gate_norm_gain.reshape(-1)).astype(jnp.bfloat16)
    mixed = jnp.dot(normed_out.reshape(-1, HEADS * HEAD_DIM), w_out.reshape(HEADS * HEAD_DIM, D), preferred_element_type=jnp.float32)
    return (mixed.reshape(STEPS, -1, D).astype(jnp.bfloat16), ssm_state)
```

```python
import jax
import jax.numpy as jnp
from jax import lax
from jax.sharding import PartitionSpec as P

HEADS = 128
HEAD_DIM = 64
EPS = 1e-05
BOTH = ("ctx", "tp")
BF = jnp.bfloat16
F32 = jnp.float32


def exchange(pieces, axis):
    return lax.all_to_all(pieces, axis, 0, 0, tiled=True)


def in_three(values):
    first = values.astype(BF)
    rest = values - first.astype(F32)
    second = rest.astype(BF)
    third = (rest - second.astype(F32)).astype(BF)
    return first, second, third


def per_device(
    token_ids,
    decode_prompt,
    embedding,
    norm_gain,
    w_zx,
    w_bcdt,
    conv_x_weight,
    conv_x_bias,
    conv_bc_weight,
    conv_bc_bias,
    dt_bias,
    a_log,
    d_skip,
    gate_norm_gain,
    w_out,
    state_parts,
    seg_rate,
    x_tail,
    bc_tail,
):
    ctx, group, tp = (lax.axis_index(a) for a in ("ctx", "dp", "tp"))
    n_ctx, n_dp, n_tp = (lax.axis_size(a) for a in ("ctx", "dp", "tp"))
    slots = state_parts.shape[1]
    heads = w_zx.shape[1]
    state_width = state_parts.shape[-1]
    steps = token_ids.shape[0]
    vocab_rows, features = embedding.shape
    model = norm_gain.shape[0]
    rows = steps * slots
    channels = heads * HEAD_DIM
    block = features * n_tp

    states = state_parts[0].reshape(slots, n_ctx, heads, HEAD_DIM, state_width)
    states = jnp.swapaxes(states, 0, 1).reshape(n_ctx, -1, state_width)
    own_columns = w_bcdt.shape[1]
    w_pieces = w_bcdt.T.reshape(own_columns, n_ctx, block)
    w_pieces = jnp.swapaxes(w_pieces, 0, 1).reshape(n_ctx, -1, state_width)
    rates = jnp.swapaxes(seg_rate[0].reshape(slots, n_ctx, heads), 0, 1)
    rates = jnp.stack(in_three(rates), axis=1).reshape(n_ctx, -1, 1)
    rates = jnp.broadcast_to(rates, (*rates.shape[:2], state_width))
    state_rows, w_rows, rate_rows = states.shape[1], w_pieces.shape[1], rates.shape[1]
    sent = jnp.concatenate([states, w_pieces, rates], axis=1)
    filler = -sent.shape[1] % 16
    sent = jnp.pad(sent, ((0, 0), (0, filler), (0, 0)))
    got = exchange(sent, "ctx")

    prompts = decode_prompt.shape[0]
    chosen = (decode_prompt[:, None] == jnp.arange(prompts)[None, :]).astype(jnp.int32)
    tokens = jnp.sum(token_ids[:, None, :] * chosen[None], axis=2)
    tokens = jnp.swapaxes(tokens.reshape(steps, n_dp, slots), 0, 1).reshape(-1)
    hot = (tokens[:, None] - group * vocab_rows == jnp.arange(vocab_rows)[None, :]).astype(BF)
    found = jnp.dot(hot, embedding, preferred_element_type=F32).astype(BF)
    found = lax.psum(found, "dp")
    own = lax.dynamic_slice_in_dim(found, group * rows, rows)
    beside = lax.all_gather(own, "tp")

    near = jnp.swapaxes(beside, 0, 1).reshape(rows, block).astype(F32)
    near_gain = lax.dynamic_slice_in_dim(norm_gain, ctx * block, block)
    w_block = got[:, state_rows : state_rows + w_rows].reshape(-1, block)
    partial = lax.dot_general(
        (near * near_gain).astype(BF), w_block, (((1,), (1,)), ((), ())), preferred_element_type=F32
    ).astype(BF)
    piece = jnp.concatenate([own.reshape(-1, 128), partial.reshape(-1, 128)], axis=0)
    own_rows = own.size // 128
    everyone = exchange(jnp.broadcast_to(piece[None], (n_ctx * n_tp, *piece.shape)), BOTH)

    parts = got[:, state_rows + w_rows : state_rows + w_rows + rate_rows, 0].astype(F32)
    parts = parts.reshape(n_ctx, 3, slots, heads)
    rate = parts[:, 0] + parts[:, 1] + parts[:, 2]
    later = jnp.cumsum(rate[::-1], axis=0)[::-1] - rate
    weight = jnp.exp(-later)[..., None, None]
    scaled = weight * got[:, :state_rows].reshape(n_ctx, slots, heads, HEAD_DIM, state_width).astype(F32)
    combined = jnp.sum(scaled.astype(BF).astype(F32), axis=0).astype(BF)
    bundle = jnp.concatenate(
        [
            combined.reshape(slots, -1, 128),
            jnp.swapaxes(x_tail, 1, 1).reshape(slots, -1, 128),
            bc_tail.reshape(slots, -1, 128),
        ],
        axis=1,
    )
    bundle = jnp.pad(bundle, ((0, 0), (0, -bundle.shape[1] % 16), (0, 0)))
    wanted = decode_prompt.reshape(n_dp, slots) - group * slots
    second = jnp.any(wanted == 1, axis=1)
    routed = jnp.where(second[:, None, None], bundle[1][None], bundle[0][None])
    arrived = exchange(routed, "dp")

    taken = everyone[:, :own_rows].reshape(n_ctx * n_tp, rows, features)
    flat = jnp.swapaxes(taken, 0, 1).reshape(rows, model).astype(F32)
    inverse = lax.rsqrt(jnp.mean(flat * flat, axis=-1, keepdims=True) + EPS)
    normed = (flat * inverse * norm_gain).astype(BF)
    projected = jnp.einsum("rd,khed->krhe", normed, w_zx, preferred_element_type=F32)
    projected = projected.reshape(2, steps, slots, heads, HEAD_DIM)
    sums = everyone[:, own_rows:].reshape(n_ctx, n_tp, rows, n_ctx, own_columns).astype(F32)
    sums = jnp.sum(sums, axis=0).transpose(1, 2, 0, 3).reshape(rows, -1)
    columns = (sums * inverse).reshape(steps, slots, -1)

    own_slots = lax.dynamic_slice_in_dim(decode_prompt, group * slots, slots)
    taken = jnp.stack(
        [lax.dynamic_index_in_dim(arrived, own_slots[s] // slots, 0, keepdims=False) for s in range(slots)]
    ).astype(F32)
    at = combined.size // slots // 128
    ssm_state = taken[:, :at].reshape(slots, heads, HEAD_DIM, state_width)
    tail_rows = x_tail.size // slots // 128
    x_window = taken[:, at : at + tail_rows].reshape(slots, 3, heads, HEAD_DIM)
    bc_rows = bc_tail.size // slots // 128
    bc_window = taken[:, at + tail_rows : at + tail_rows + bc_rows].reshape(slots, 3, -1)

    head_start = 2 * state_width + (tp * n_ctx + ctx) * heads
    dt_raw = lax.dynamic_slice_in_dim(columns, head_start, heads, 2)
    decay_rate = -jnp.exp(a_log)
    gated_steps = []
    for moment in range(steps):
        x_window = jnp.concatenate([x_window, projected[1, moment][:, None]], axis=1)
        bc_window = jnp.concatenate([bc_window, columns[moment, :, None, : 2 * state_width]], axis=1)
        x_conv = jax.nn.silu(jnp.einsum("pkhe,khe->phe", x_window, conv_x_weight) + conv_x_bias)
        bc_conv = jax.nn.silu(jnp.einsum("pkn,kn->pn", bc_window, conv_bc_weight) + conv_bc_bias)
        step_size = jax.nn.softplus(dt_raw[moment] + dt_bias)
        retain = jnp.exp(step_size * decay_rate)
        ssm_state = (
            retain[:, :, None, None] * ssm_state
            + (step_size[:, :, None] * x_conv)[:, :, :, None] * bc_conv[:, None, None, :state_width]
        )
        output = (
            jnp.einsum("phen,pn->phe", ssm_state, bc_conv[:, state_width:])
            + d_skip[None, :, None] * x_conv
        )
        gated_steps.append(output * jax.nn.silu(projected[0, moment]))
        x_window = x_window[:, 1:]
        bc_window = bc_window[:, 1:]
    gated = jnp.stack(gated_steps).reshape(rows, channels)
    squares = jnp.sum(gated * gated, axis=1)
    weighted = (gated * gate_norm_gain.reshape(-1)).astype(BF)
    partial_out = jnp.dot(weighted, w_out.reshape(channels, model), preferred_element_type=F32)
    partial_out = jnp.swapaxes(partial_out.reshape(rows, n_ctx * n_tp, -1), 0, 1)
    partial_out = partial_out.reshape(n_ctx * n_tp, -1, 128).astype(BF)
    square_parts = jnp.concatenate(in_three(squares))
    square_parts = jnp.pad(square_parts, (0, 128 * 4 - square_parts.shape[0])).reshape(1, 4, 128)
    outgoing = jnp.concatenate(
        [partial_out, jnp.broadcast_to(square_parts, (n_ctx * n_tp, 4, 128))], axis=1
    )
    incoming = jnp.sum(exchange(outgoing, BOTH).astype(F32), axis=0)
    out_rows = partial_out.shape[1]
    total = jnp.sum(incoming[out_rows, : 3 * rows].reshape(3, rows), axis=0)
    scale = lax.rsqrt(total / (HEADS * HEAD_DIM) + EPS)
    mixed = incoming[:out_rows].reshape(rows, -1) * scale[:, None]
    return (mixed.reshape(steps, slots, -1).astype(BF), ssm_state)


def solution(mesh):
    return jax.shard_map(
        per_device,
        mesh=mesh,
        in_specs=(
            P(),
            P(),
            P("dp", ("ctx", "tp")),
            P(),
            P(None, ("tp", "ctx"), None, None),
            P(None, ("ctx", "tp")),
            P(None, ("tp", "ctx"), None),
            P(("tp", "ctx"), None),
            P(),
            P(),
            P(("tp", "ctx")),
            P(("tp", "ctx")),
            P(("tp", "ctx")),
            P(("tp", "ctx"), None),
            P(("tp", "ctx"), None, None),
            P("ctx", "dp", "tp", None, None),
            P("ctx", "dp", "tp"),
            P("dp", None, ("tp", "ctx"), None),
            P("dp", None, None),
        ),
        out_specs=(P(None, "dp", ("ctx", "tp")), P("dp", ("tp", "ctx"), None, None)),
        check_vma=False,
    )
```

```python
import functools

import jax
import jax.numpy as jnp
from jax import lax
from jax.experimental import pallas as pl
from jax.experimental.pallas import tpu as pltpu
from jax.sharding import PartitionSpec as P

HEADS = 128
HEAD_DIM = 64
EPS = 1e-05
BOTH = ("ctx", "tp")
BF = jnp.bfloat16
F32 = jnp.float32
LANES = 128
HALF = 64
VMEM_LIMIT = 48 * 1024 * 1024

STATE_ROWS = 256
RATE_ROWS = 16
TOKEN_ROWS = 32
ONE_STATE = 128
TAIL_ROWS = 16
NEAR_ROWS = 64


def exchange(pieces, axis):
    return lax.all_to_all(pieces, axis, 0, 0, tiled=True)


def in_three(values):
    first = values.astype(BF)
    rest = values - first.astype(F32)
    second = rest.astype(BF)
    third = (rest - second.astype(F32)).astype(BF)
    return first, second, third


def silu(v):
    return v / (1.0 + jnp.exp(-v))


def low_half(shape=(8, LANES)):
    return lax.broadcasted_iota(jnp.int32, shape, 1) < HALF


def combine_kernel(chosen_ref, got_ref, tails_ref, out_ref, combined_ref):
    count = got_ref.shape[0]
    groups = out_ref.shape[0]
    rates = []
    for k in range(count):
        parts = got_ref[k, STATE_ROWS : STATE_ROWS + RATE_ROWS, :].astype(F32)
        rates.append(parts[0:4] + parts[4:8] + parts[8:12])
    weights = [None] * count
    later = jnp.zeros_like(rates[0])
    for k in reversed(range(count)):
        weights[k] = jnp.exp(-later)
        later = later + rates[k]
    for part in range(4):
        total = jnp.zeros((HEAD_DIM, LANES), F32)
        for k in range(count):
            own = got_ref[k, part * HEAD_DIM : (part + 1) * HEAD_DIM, :].astype(F32)
            total = total + (own * weights[k][part : part + 1]).astype(BF).astype(F32)
        at = (part % 2) * HEAD_DIM
        combined_ref[part // 2, at : at + HEAD_DIM, :] = total.astype(BF)
    for g in range(groups):
        prompt = chosen_ref[g]
        out_ref[g, 0:ONE_STATE, :] = combined_ref[prompt]
        out_ref[g, ONE_STATE : ONE_STATE + TAIL_ROWS, :] = tails_ref[prompt]
    low = low_half((TOKEN_ROWS, LANES))
    at = STATE_ROWS + RATE_ROWS
    for pair in range(0, count // 2, 2):
        early, late = [], []
        for k in (pair, pair + 1):
            one = got_ref[k, at : at + TOKEN_ROWS, :].astype(F32)
            two = got_ref[count // 2 + k, at : at + TOKEN_ROWS, :].astype(F32)
            early.append(jnp.where(low, one, pltpu.roll(two, HALF, 1)))
            late.append(jnp.where(low, pltpu.roll(one, HALF, 1), two))
        for g in range(groups):
            source = early if g < groups // 2 else late
            r = (g % (groups // 2)) * 8
            both = jnp.concatenate([s[r : r + 8] for s in source], axis=0)
            start = ONE_STATE + TAIL_ROWS + pair * 8
            out_ref[g, start : start + 16, :] = both.astype(BF)


def columns_kernel(place_ref, arrived_ref, gain_ref, weight_ref, out_ref, near_ref):
    groups = arrived_ref.shape[0]
    at = ONE_STATE + TAIL_ROWS
    total = arrived_ref[0, at : at + NEAR_ROWS, :].astype(F32)
    for g in range(1, groups):
        total = total + arrived_ref[g, at : at + NEAR_ROWS, :].astype(F32)
    pieces = []
    for k in range(NEAR_ROWS // 8):
        rows = total[k * 8 : (k + 1) * 8]
        near_ref[k] = rows
        pieces.append((rows * gain_ref[k : k + 1, :]).astype(BF))
    weighted = jnp.concatenate(pieces, axis=1)
    partial = lax.dot_general(
        weighted, weight_ref[...], (((1,), (1,)), ((), ())), preferred_element_type=F32
    )
    own = pltpu.roll(near_ref[place_ref[0]], place_ref[1], 1)
    lane = lax.broadcasted_iota(jnp.int32, (8, LANES), 1)
    first = partial.astype(BF).astype(F32)
    tile = jnp.where(lane < HALF, own, jnp.where(lane < HALF + 24, first, partial - first))
    out_ref[...] = jnp.broadcast_to(tile.astype(BF)[None], out_ref.shape)


def decode_kernel(
    place_ref,
    everyone_ref,
    arrived_ref,
    gain_ref,
    small_ref,
    w_zx_ref,
    w_out_ref,
    out_ref,
    start_ref,
    extra_ref,
    zx_ref,
    wo_ref,
    x_ref,
    b_ref,
    c_ref,
    sems,
):
    load_zx = pltpu.make_async_copy(w_zx_ref, zx_ref, sems.at[0])
    load_zx.start()
    load_out = pltpu.make_async_copy(w_out_ref, wo_ref, sems.at[1])
    load_out.start()
    peers = everyone_ref.shape[0]
    model = peers * HALF
    lane = lax.broadcasted_iota(jnp.int32, (8, LANES), 1)
    row = lax.broadcasted_iota(jnp.int32, (8, LANES), 0)
    low = lane < HALF

    tiles = [everyone_ref[p].astype(F32) for p in range(peers)]
    rows = [
        jnp.where(low, tiles[2 * n], pltpu.roll(tiles[2 * n + 1], HALF, 1)) for n in range(peers // 2)
    ]
    squares = rows[0] * rows[0]
    for r in rows[1:]:
        squares = squares + r * r
    inverse = lax.rsqrt(jnp.sum(squares, axis=1, keepdims=True) * (1.0 / model) + EPS)
    normed = jnp.concatenate(
        [(r * inverse * gain_ref[n : n + 1, :]).astype(BF) for n, r in enumerate(rows)], axis=1
    )

    columns = [jnp.zeros((8, LANES), F32) for _ in range(3)]
    for c in range(16):
        part = tiles[4 * c] + tiles[4 * c + 1] + tiles[4 * c + 2] + tiles[4 * c + 3]
        part = part + pltpu.roll(part, LANES - 24, 1)
        part = jnp.where((lane >= HALF) & (lane < HALF + 24), part, 0.0)
        first, offset = divmod(c * 24, LANES)
        part = pltpu.roll(part, (offset - HALF) % LANES, 1)
        if offset + 24 <= LANES:
            columns[first] = columns[first] + part
        else:
            columns[first] = columns[first] + jnp.where(lane >= offset, part, 0.0)
            columns[first + 1] = columns[first + 1] + jnp.where(lane < offset, part, 0.0)
    columns = [v * inverse for v in columns]

    for slot in range(2):
        tail = arrived_ref[place_ref[slot], ONE_STATE : ONE_STATE + TAIL_ROWS, :].astype(F32)
        for k in range(3):
            at = 2 * k + slot
            x_ref[at : at + 1, :] = tail[k : k + 1]
            b_ref[at : at + 1, :] = tail[3 + 2 * k : 4 + 2 * k]
            c_ref[at : at + 1, :] = tail[4 + 2 * k : 5 + 2 * k]
    b_ref[6:14, :] = columns[0]
    c_ref[6:14, :] = columns[1]

    def convolved(ref, weight_at, bias_at):
        total = ref[0:8, :] * small_ref[weight_at : weight_at + 1, :]
        for k in range(1, 4):
            total = total + ref[2 * k : 2 * k + 8, :] * small_ref[weight_at + k : weight_at + k + 1, :]
        return silu(total + small_ref[bias_at : bias_at + 1, :])

    b_conv = convolved(b_ref, 4, 13)
    c_conv = convolved(c_ref, 8, 14)

    raw = pltpu.roll(columns[2], place_ref[2], 1)
    raw = jnp.where(low, raw[:, 0:1], raw[:, 1:2]) + small_ref[15:16, :]
    step = jnp.maximum(raw, 0.0) + jnp.log1p(jnp.exp(-jnp.abs(raw)))
    log_retain = -step * jnp.exp(small_ref[16:17, :])

    def earlier(v, lag):
        return jnp.where(row >= 2 * lag, pltpu.roll(v, 2 * lag, 0), 0.0)

    log_total = log_retain
    for lag in range(1, 4):
        log_total = log_total + earlier(log_retain, lag)

    c_parts = jnp.concatenate([p.astype(F32) for p in in_three(c_conv)], axis=0).astype(BF)
    from_start = []
    for slot in range(2):
        state = arrived_ref[place_ref[slot], 0:ONE_STATE, :]
        start_ref[slot] = state
        product = lax.dot_general(
            c_parts, state, (((1,), (1,)), ((), ())), preferred_element_type=F32
        )
        from_start.append(product[0:8] + product[8:16] + product[16:24])
    y = jnp.exp(log_total) * jnp.where(row % 2 == 0, from_start[0], from_start[1])

    load_zx.wait()
    projected = lax.dot_general(
        normed, zx_ref[...], (((1,), (1,)), ((), ())), preferred_element_type=F32
    )
    gate = projected[:, 0:LANES]
    x_ref[6:14, :] = projected[:, LANES : 2 * LANES]
    x_conv = convolved(x_ref, 0, 12)
    drive = step * x_conv
    y = y + small_ref[17:18, :] * x_conv
    for lag in range(4):
        match = jnp.sum(c_conv * earlier(b_conv, lag), axis=1, keepdims=True)
        if lag == 0:
            y = y + drive * match
        else:
            decay = jnp.exp(log_total - earlier(log_total, lag))
            y = y + decay * earlier(drive, lag) * match
    gated = y * silu(gate)
    total = jnp.sum(gated * gated, axis=1, keepdims=True)
    parts = [p.astype(F32) for p in in_three(total)]
    aside = jnp.where(
        lane == HALF,
        parts[0],
        jnp.where(lane == HALF + 1, parts[1], jnp.where(lane == HALF + 2, parts[2], 0.0)),
    )
    weighted = (gated * small_ref[18:19, :]).astype(BF)

    last = jnp.where(row % 2 == 0, log_total[6:7], log_total[7:8])
    extra_ref[0:8, :] = jnp.exp(last - log_total) * drive
    extra_ref[8:16, :] = b_conv
    extra_ref[16:24, :] = jnp.exp(last)

    load_out.wait()
    for n in range(peers // 8):
        wide = jnp.dot(
            weighted, wo_ref[:, n * 512 : (n + 1) * 512], preferred_element_type=F32
        )
        for m in range(4):
            piece = wide[:, m * LANES : (m + 1) * LANES]
            out_ref[8 * n + 2 * m] = jnp.where(low, piece, aside).astype(BF)
            out_ref[8 * n + 2 * m + 1] = jnp.where(low, pltpu.roll(piece, HALF, 1), aside).astype(BF)


def finish_kernel(incoming_ref, out_ref):
    total = incoming_ref[0].astype(F32)
    for p in range(1, incoming_ref.shape[0]):
        total = total + incoming_ref[p].astype(F32)
    squares = total[:, HALF : HALF + 1] + total[:, HALF + 1 : HALF + 2] + total[:, HALF + 2 : HALF + 3]
    scale = lax.rsqrt(squares * (1.0 / (HEADS * HEAD_DIM)) + EPS)
    out_ref[...] = (total[:, 0:HALF] * scale).astype(BF)


VM = pl.BlockSpec(memory_space=pltpu.VMEM)
SM = pl.BlockSpec(memory_space=pltpu.SMEM)
HB = pl.BlockSpec(memory_space=pl.ANY)
PARAMS = pltpu.CompilerParams(vmem_limit_bytes=VMEM_LIMIT)


def per_device(
    token_ids,
    decode_prompt,
    embedding,
    norm_gain,
    w_zx,
    w_bcdt,
    conv_x_weight,
    conv_x_bias,
    conv_bc_weight,
    conv_bc_bias,
    dt_bias,
    a_log,
    d_skip,
    gate_norm_gain,
    w_out,
    state_parts,
    seg_rate,
    x_tail,
    bc_tail,
):
    ctx, group, tp = (lax.axis_index(a) for a in ("ctx", "dp", "tp"))
    n_ctx, n_dp, n_tp = (lax.axis_size(a) for a in ("ctx", "dp", "tp"))
    peers = n_ctx * n_tp
    slots = state_parts.shape[1]
    heads = w_zx.shape[1]
    width = state_parts.shape[-1]
    steps = token_ids.shape[0]
    vocab_rows, features = embedding.shape
    model = norm_gain.shape[0]
    rows = steps * slots
    channels = heads * HEAD_DIM

    prompts = decode_prompt.shape[0]
    chosen = (decode_prompt[:, None] == jnp.arange(prompts)[None, :]).astype(jnp.int32)
    tokens = jnp.sum(token_ids[:, None, :] * chosen[None], axis=2)
    tokens = jnp.swapaxes(tokens.reshape(steps, n_dp, slots), 0, 1).reshape(-1)
    hot = (tokens[:, None] - group * vocab_rows == jnp.arange(vocab_rows)[None, :]).astype(BF)
    found = jnp.dot(hot, embedding, preferred_element_type=F32).astype(BF)
    found = jnp.concatenate([found[:TOKEN_ROWS], found[TOKEN_ROWS:]], axis=1)

    states = state_parts[0].reshape(slots, n_ctx, heads, HEAD_DIM, width)
    states = jnp.swapaxes(states, 0, 1).reshape(n_ctx, STATE_ROWS, width)
    rates = jnp.swapaxes(seg_rate[0].reshape(slots, n_ctx, heads), 0, 1)
    rates = jnp.stack(in_three(rates), axis=1).reshape(n_ctx, -1)
    rates = jnp.pad(rates, ((0, 0), (0, RATE_ROWS - rates.shape[1])))
    rates = jnp.broadcast_to(rates[..., None], (n_ctx, RATE_ROWS, width))
    sent = jnp.concatenate(
        [states, rates, jnp.broadcast_to(found[None], (n_ctx, *found.shape))], axis=1
    )
    got = exchange(sent, "ctx")

    w_near = lax.all_gather(w_bcdt.T, "tp")
    own_columns = n_tp * w_bcdt.shape[1]
    w_near = w_near.reshape(own_columns, 2, n_ctx // 2, n_tp, features)
    w_near = lax.dynamic_index_in_dim(w_near, tp, 3, keepdims=False)
    w_near = jnp.swapaxes(w_near, 1, 2).reshape(own_columns, -1)
    w_near = jnp.concatenate([w_near, w_near], axis=0)
    w_near = jnp.pad(w_near, ((HALF, LANES - HALF - 2 * own_columns), (0, 0)))
    near_gain = norm_gain.reshape(2, n_ctx // 2, n_tp, features)
    near_gain = lax.dynamic_index_in_dim(near_gain, tp, 2, keepdims=False)
    near_gain = jnp.swapaxes(near_gain, 0, 1).reshape(n_ctx // 2, -1)
    tails = jnp.concatenate([x_tail.reshape(slots, 3, LANES), bc_tail.reshape(slots, 6, LANES)], axis=1)
    tails = jnp.pad(tails, ((0, 0), (0, TAIL_ROWS - tails.shape[1]), (0, 0)))
    wanted = decode_prompt.reshape(n_dp, slots) - group * slots
    prompt_for = jnp.any(wanted == 1, axis=1).astype(jnp.int32)
    own_slots = lax.dynamic_slice_in_dim(decode_prompt, group * slots, slots)
    spread = functools.partial(jnp.repeat, repeats=HEAD_DIM, total_repeat_length=channels)
    small = jnp.concatenate(
        [
            conv_x_weight.reshape(4, channels),
            conv_bc_weight[:, :width],
            conv_bc_weight[:, width:],
            conv_x_bias.reshape(1, channels),
            conv_bc_bias.reshape(2, width),
            spread(dt_bias)[None],
            spread(a_log)[None],
            spread(d_skip)[None],
            gate_norm_gain.reshape(1, channels),
        ],
        axis=0,
    )
    small = jnp.pad(small, ((0, -small.shape[0] % 8), (0, 0)))

    routed = pl.pallas_call(
        combine_kernel,
        out_shape=jax.ShapeDtypeStruct((n_dp, ONE_STATE + TAIL_ROWS + NEAR_ROWS, width), BF),
        in_specs=[SM, VM, VM],
        out_specs=VM,
        scratch_shapes=[pltpu.VMEM((slots, ONE_STATE, width), BF)],
        compiler_params=PARAMS,
        name="combine",
    )(prompt_for, got, tails)
    arrived = exchange(routed, "dp")

    place = jnp.stack([ctx % (n_ctx // 2), (ctx // (n_ctx // 2)) * HALF]).astype(jnp.int32)
    piece = pl.pallas_call(
        columns_kernel,
        out_shape=jax.ShapeDtypeStruct((peers, rows, LANES), BF),
        in_specs=[SM, VM, VM, VM],
        out_specs=VM,
        scratch_shapes=[pltpu.VMEM((NEAR_ROWS // 8, 8, LANES), F32)],
        compiler_params=PARAMS,
        name="columns",
    )(place, arrived, near_gain, w_near)
    everyone = exchange(piece, BOTH)

    head_at = (tp * n_ctx + ctx) * heads
    place = jnp.concatenate(
        [own_slots // slots, ((LANES - head_at) % LANES)[None]]
    ).astype(jnp.int32)
    outgoing, start, extra = pl.pallas_call(
        decode_kernel,
        out_shape=(
            jax.ShapeDtypeStruct((peers, rows, LANES), BF),
            jax.ShapeDtypeStruct((slots, ONE_STATE, width), BF),
            jax.ShapeDtypeStruct((24, LANES), F32),
        ),
        in_specs=[SM, VM, VM, VM, VM, HB, HB],
        out_specs=(VM, VM, VM),
        scratch_shapes=[
            pltpu.VMEM((2 * channels, model), BF),
            pltpu.VMEM((channels, model), BF),
            pltpu.VMEM((16, LANES), F32),
            pltpu.VMEM((16, LANES), F32),
            pltpu.VMEM((16, LANES), F32),
            pltpu.SemaphoreType.DMA((2,)),
        ],
        compiler_params=PARAMS,
        name="decode",
    )(
        place,
        everyone,
        arrived,
        norm_gain.reshape(model // LANES, LANES),
        small,
        w_zx.reshape(2 * channels, model),
        w_out.reshape(channels, model),
    )
    incoming = exchange(outgoing, BOTH)

    push = extra[0:8].reshape(steps, slots, channels)
    b_conv = extra[8:16].reshape(steps, slots, width)
    kept = extra[16:18]
    final = kept[:, :, None] * start.astype(F32) + jnp.einsum(
        "tpc,tpn->pcn", push, b_conv, precision=lax.Precision.HIGHEST
    )

    mixed = pl.pallas_call(
        finish_kernel,
        out_shape=jax.ShapeDtypeStruct((rows, features), BF),
        in_specs=[VM],
        out_specs=VM,
        compiler_params=PARAMS,
        name="finish",
    )(incoming)
    return (
        mixed.reshape(steps, slots, features),
        final.reshape(slots, heads, HEAD_DIM, width),
    )


def solution(mesh):
    return jax.shard_map(
        per_device,
        mesh=mesh,
        in_specs=(
            P(),
            P(),
            P("dp", ("ctx", "tp")),
            P(),
            P(None, ("tp", "ctx"), None, None),
            P(None, ("ctx", "tp")),
            P(None, ("tp", "ctx"), None),
            P(("tp", "ctx"), None),
            P(),
            P(),
            P(("tp", "ctx")),
            P(("tp", "ctx")),
            P(("tp", "ctx")),
            P(("tp", "ctx"), None),
            P(("tp", "ctx"), None, None),
            P("ctx", "dp", "tp", None, None),
            P("ctx", "dp", "tp"),
            P("dp", None, ("tp", "ctx"), None),
            P("dp", None, None),
        ),
        out_specs=(P(None, "dp", ("ctx", "tp")), P("dp", ("tp", "ctx"), None, None)),
        check_vma=False,
    )
```

```python
import jax
import jax.numpy as jnp
from jax import lax
from jax.experimental import pallas as pl
from jax.experimental.pallas import tpu as pltpu
from jax.sharding import PartitionSpec as P

HEADS = 128
HEAD_DIM = 64
EPS = 1e-05
BOTH = ("ctx", "tp")
BF = jnp.bfloat16
F32 = jnp.float32
LANES = 128
HALF = 64
VMEM_LIMIT = 24 * 1024 * 1024

STATE_ROWS = 256
SIDE_ROWS = 16
ROWS_AT = 12
ONE_STATE = 128


def exchange(pieces, axis):
    return lax.all_to_all(pieces, axis, 0, 0, tiled=True)


def in_three(values):
    first = values.astype(BF)
    rest = values - first.astype(F32)
    second = rest.astype(BF)
    third = (rest - second.astype(F32)).astype(BF)
    return first, second, third


def silu(v):
    return v / (1.0 + jnp.exp(-v))


def low_half(shape=(8, LANES)):
    return lax.broadcasted_iota(jnp.int32, shape, 1) < HALF


def lookup_kernel(
    tokens_hbm, prompt_hbm, table_hbm, x_tail_hbm, bc_tail_hbm, out_ref,
    tokens_ref, prompt_ref, table_ref, x_tail_ref, bc_tail_ref, token_ref, block_ref, sems,
):
    pairs = [
        (tokens_hbm, tokens_ref),
        (prompt_hbm, prompt_ref),
        (table_hbm, table_ref),
        (x_tail_hbm, x_tail_ref),
        (bc_tail_hbm, bc_tail_ref),
    ]
    loads = [pltpu.make_async_copy(a, b, sems.at[n]) for n, (a, b) in enumerate(pairs)]
    for load in loads:
        load.start()
    group = lax.axis_index("dp")
    groups = out_ref.shape[0]
    slots = prompt_ref.shape[0] // groups
    steps = tokens_ref.shape[0]
    rows = steps * slots
    features, vocab_rows = table_ref.shape
    first = group * vocab_rows
    loads[0].wait()
    loads[1].wait()
    for g in range(groups):
        for step in range(steps):
            for slot in range(slots):
                token = tokens_ref[step, prompt_ref[g * slots + slot]] - first
                at = g * rows + step * slots + slot
                token_ref[at : at + 1, :] = jnp.full((1, LANES), token, jnp.int32)
    loads[2].wait()
    tokens = token_ref[:, 0:1]
    found = jnp.zeros((groups * rows, LANES), F32)
    whole = vocab_rows // LANES * LANES
    bounds = [*range(0, whole, 1024), whole, vocab_rows]
    for low_at, high_at in zip(bounds[:-1], bounds[1:]):
        ids = lax.broadcasted_iota(jnp.int32, (groups * rows, high_at - low_at), 1) + low_at
        hot = jnp.where(tokens == ids, 1.0, 0.0).astype(BF)
        table = table_ref[:, low_at:high_at]
        found = found + lax.dot_general(
            hot,
            jnp.concatenate([table, table], axis=0),
            (((1,), (1,)), ((), ())),
            preferred_element_type=F32,
        )
    low = low_half((4, LANES))
    loads[3].wait()
    loads[4].wait()
    for p in range(slots):
        block_ref[groups + p] = jnp.zeros((SIDE_ROWS, LANES), F32)
        for k in range(3):
            pair = x_tail_ref[p, k].astype(F32)
            block_ref[groups + p, k : k + 1, :] = jnp.concatenate([pair[0:1], pair[1:2]], axis=1)
            both = bc_tail_ref[k, p : p + 1, :].astype(F32)
            block_ref[groups + p, 3 + 2 * k : 4 + 2 * k, :] = both[:, 0:LANES]
            block_ref[groups + p, 4 + 2 * k : 5 + 2 * k, :] = both[:, LANES : 2 * LANES]
    for g in range(groups):
        wanted = group * slots + 1
        second = (prompt_ref[g * slots] == wanted) | (prompt_ref[g * slots + 1] == wanted)
        block_ref[g] = block_ref[jnp.where(second, groups + 1, groups)]
        block_ref[g, ROWS_AT : ROWS_AT + 4, :] = jnp.where(
            low, found[g * rows : g * rows + 4], found[g * rows + 4 : g * rows + 8]
        )
        out_ref[g] = block_ref[g].astype(BF)


def pack_kernel(near_ref, rates_ref, states_ref, out_ref, side_ref, sems):
    moves = []
    for p in range(states_ref.shape[0]):
        moves.append(
            pltpu.make_async_copy(
                states_ref.at[p], out_ref.at[:, p * ONE_STATE : (p + 1) * ONE_STATE, :], sems.at[p]
            )
        )
        moves[-1].start()
    total = near_ref[0].astype(F32)
    for g in range(1, near_ref.shape[0]):
        total = total + near_ref[g].astype(F32)
    row = lax.broadcasted_iota(jnp.int32, (SIDE_ROWS, LANES), 0)
    total = jnp.where(row >= ROWS_AT, total, 0.0)
    for c in range(out_ref.shape[0]):
        side_ref[c] = (rates_ref[c].astype(F32) + total).astype(BF)
    side = pltpu.make_async_copy(
        side_ref, out_ref.at[:, STATE_ROWS : STATE_ROWS + SIDE_ROWS, :], sems.at[2]
    )
    side.start()
    for move in moves:
        move.wait()
    side.wait()


def combine_kernel(chosen_ref, got_ref, out_ref, combined_ref, sems):
    count = got_ref.shape[0]
    groups = out_ref.shape[0]
    rates = []
    for k in range(count):
        parts = got_ref[k, STATE_ROWS : STATE_ROWS + SIDE_ROWS, :].astype(F32)
        rates.append(parts[0:4] + parts[4:8] + parts[8:12])
    weights = [None] * count
    later = jnp.zeros_like(rates[0])
    for k in reversed(range(count)):
        weights[k] = jnp.exp(-later)
        later = later + rates[k]
    for part in range(4):
        total = jnp.zeros((HEAD_DIM, LANES), F32)
        for k in range(count):
            own = got_ref[k, part * HEAD_DIM : (part + 1) * HEAD_DIM, :].astype(F32)
            total = total + (own * weights[k][part : part + 1]).astype(BF).astype(F32)
        at = (part % 2) * HEAD_DIM
        combined_ref[part // 2, at : at + HEAD_DIM, :] = total.astype(BF)
    moves = [
        pltpu.make_async_copy(combined_ref.at[chosen_ref[g]], out_ref.at[g], sems.at[g])
        for g in range(groups)
    ]
    for move in moves:
        move.start()
    for move in moves:
        move.wait()


def columns_kernel(place_ref, got_ref, gain_ref, weight_ref, out_ref, near_ref, tile_ref, sem):
    count = got_ref.shape[0]
    low = low_half()
    for c in range(count):
        side = got_ref[c, STATE_ROWS : STATE_ROWS + SIDE_ROWS, :].astype(F32)
        four = side[ROWS_AT : ROWS_AT + 4]
        near_ref[c, 0:4, :] = four
        near_ref[c, 4:8, :] = pltpu.roll(four, HALF, 1)
    pieces = []
    for k in range(count // 2):
        rows = jnp.where(low, near_ref[k], pltpu.roll(near_ref[count // 2 + k], HALF, 1))
        pieces.append((rows * gain_ref[k : k + 1, :]).astype(BF))
    weighted = jnp.concatenate(pieces, axis=1)
    partial = lax.dot_general(
        weighted, weight_ref[...], (((1,), (1,)), ((), ())), preferred_element_type=F32
    )
    own = near_ref[place_ref[0]]
    lane = lax.broadcasted_iota(jnp.int32, (8, LANES), 1)
    first = partial.astype(BF).astype(F32)
    tile = jnp.where(lane < HALF, own, jnp.where(lane < HALF + 24, first, partial - first))
    tile_ref[...] = jnp.broadcast_to(tile.astype(BF)[None], tile_ref.shape)
    move = pltpu.make_async_copy(tile_ref, out_ref, sem)
    move.start()
    move.wait()


def project_kernel(
    place_ref,
    everyone_ref,
    near_ref,
    gain_ref,
    small_ref,
    w_zx_ref,
    ready_ref,
    c_parts_ref,
    extra_ref,
    x_ref,
    b_ref,
    c_ref,
):
    peers = everyone_ref.shape[0]
    model = peers * HALF
    lane = lax.broadcasted_iota(jnp.int32, (8, LANES), 1)
    row = lax.broadcasted_iota(jnp.int32, (8, LANES), 0)
    low = lane < HALF

    tiles = [everyone_ref[p].astype(F32) for p in range(peers)]
    rows = [
        jnp.where(low, tiles[2 * n], pltpu.roll(tiles[2 * n + 1], HALF, 1)) for n in range(peers // 2)
    ]
    squares = rows[0] * rows[0]
    for r in rows[1:]:
        squares = squares + r * r
    inverse = lax.rsqrt(jnp.sum(squares, axis=1, keepdims=True) * (1.0 / model) + EPS)
    normed = jnp.concatenate(
        [(r * inverse * gain_ref[n : n + 1, :]).astype(BF) for n, r in enumerate(rows)], axis=1
    )

    columns = [jnp.zeros((8, LANES), F32) for _ in range(3)]
    for c in range(16):
        part = tiles[4 * c] + tiles[4 * c + 1] + tiles[4 * c + 2] + tiles[4 * c + 3]
        part = part + pltpu.roll(part, LANES - 24, 1)
        part = jnp.where((lane >= HALF) & (lane < HALF + 24), part, 0.0)
        first, offset = divmod(c * 24, LANES)
        part = pltpu.roll(part, (offset - HALF) % LANES, 1)
        if offset + 24 <= LANES:
            columns[first] = columns[first] + part
        else:
            columns[first] = columns[first] + jnp.where(lane >= offset, part, 0.0)
            columns[first + 1] = columns[first + 1] + jnp.where(lane < offset, part, 0.0)
    columns = [v * inverse for v in columns]

    for slot in range(2):
        tail = near_ref[place_ref[slot]].astype(F32)
        for k in range(3):
            at = 2 * k + slot
            x_ref[at : at + 1, :] = tail[k : k + 1]
            b_ref[at : at + 1, :] = tail[3 + 2 * k : 4 + 2 * k]
            c_ref[at : at + 1, :] = tail[4 + 2 * k : 5 + 2 * k]
    b_ref[6:14, :] = columns[0]
    c_ref[6:14, :] = columns[1]

    def convolved(ref, weight_at, bias_at):
        total = ref[0:8, :] * small_ref[weight_at : weight_at + 1, :]
        for k in range(1, 4):
            total = total + ref[2 * k : 2 * k + 8, :] * small_ref[weight_at + k : weight_at + k + 1, :]
        return silu(total + small_ref[bias_at : bias_at + 1, :])

    b_conv = convolved(b_ref, 4, 13)
    c_conv = convolved(c_ref, 8, 14)

    raw = pltpu.roll(columns[2], place_ref[2], 1)
    raw = jnp.where(low, raw[:, 0:1], raw[:, 1:2]) + small_ref[15:16, :]
    step = jnp.maximum(raw, 0.0) + jnp.log1p(jnp.exp(-jnp.abs(raw)))
    log_retain = -step * jnp.exp(small_ref[16:17, :])

    def earlier(v, lag):
        return jnp.where(row >= 2 * lag, pltpu.roll(v, 2 * lag, 0), 0.0)

    log_total = log_retain
    for lag in range(1, 4):
        log_total = log_total + earlier(log_retain, lag)

    parts = [p.astype(F32) for p in in_three(c_conv)]
    c_parts_ref[...] = jnp.concatenate([*parts, jnp.zeros_like(c_conv)], axis=0).astype(BF)

    projected = lax.dot_general(
        normed, w_zx_ref[...], (((1,), (1,)), ((), ())), preferred_element_type=F32
    )
    x_ref[6:14, :] = projected[:, LANES : 2 * LANES]
    x_conv = convolved(x_ref, 0, 12)
    drive = step * x_conv
    y = small_ref[17:18, :] * x_conv
    for lag in range(4):
        match = jnp.sum(c_conv * earlier(b_conv, lag), axis=1, keepdims=True)
        if lag == 0:
            y = y + drive * match
        else:
            decay = jnp.exp(log_total - earlier(log_total, lag))
            y = y + decay * earlier(drive, lag) * match
    ready_ref[0:8, :] = jnp.exp(log_total)
    ready_ref[8:16, :] = y
    ready_ref[16:24, :] = silu(projected[:, 0:LANES])
    ready_ref[24:32, :] = jnp.broadcast_to(small_ref[18:19, :], (8, LANES))

    last = jnp.where(row % 2 == 0, log_total[6:7], log_total[7:8])
    extra_ref[0:8, :] = jnp.exp(last - log_total) * drive
    extra_ref[8:16, :] = b_conv
    extra_ref[16:24, :] = jnp.exp(last)


def decode_kernel(
    place_ref, arrived_ref, ready_ref, c_parts_ref, w_out_hbm, out_ref, w_out_ref, tile_ref, load_sems, sems
):
    loads = []
    for n in range(out_ref.shape[0] // 16):
        part = pl.ds(n * 1024, 1024)
        loads.append(
            pltpu.make_async_copy(w_out_hbm.at[:, part], w_out_ref.at[:, part], load_sems.at[n])
        )
        loads[-1].start()
    lane = lax.broadcasted_iota(jnp.int32, (8, LANES), 1)
    row = lax.broadcasted_iota(jnp.int32, (8, LANES), 0)
    low = lane < HALF
    from_start = []
    for slot in range(2):
        product = lax.dot_general(
            c_parts_ref[...],
            arrived_ref[place_ref[slot]],
            (((1,), (1,)), ((), ())),
            preferred_element_type=F32,
        )
        from_start.append(product[0:8] + product[8:16] + product[16:24])
    y = ready_ref[0:8, :] * jnp.where(row % 2 == 0, from_start[0], from_start[1]) + ready_ref[8:16, :]
    gated = y * ready_ref[16:24, :]
    weighted = (gated * ready_ref[24:32, :]).astype(BF)
    total = jnp.sum(gated * gated, axis=1, keepdims=True)
    parts = [p.astype(F32) for p in in_three(total)]
    aside = jnp.where(
        lane == HALF,
        parts[0],
        jnp.where(lane == HALF + 1, parts[1], jnp.where(lane == HALF + 2, parts[2], 0.0)),
    )
    moves = []
    for n in range(out_ref.shape[0] // 16):
        loads[n].wait()
        wide = jnp.dot(
            weighted, w_out_ref[:, n * 1024 : (n + 1) * 1024], preferred_element_type=F32
        )
        for m in range(8):
            piece = wide[:, m * LANES : (m + 1) * LANES]
            tile_ref[16 * n + 2 * m] = jnp.where(low, piece, aside).astype(BF)
            tile_ref[16 * n + 2 * m + 1] = jnp.where(low, pltpu.roll(piece, HALF, 1), aside).astype(BF)
        part = pl.ds(16 * n, 16)
        moves.append(pltpu.make_async_copy(tile_ref.at[part], out_ref.at[part], sems.at[n]))
        moves[-1].start()
    for move in moves:
        move.wait()


def finish_kernel(incoming_ref, out_ref):
    total = incoming_ref[0].astype(F32)
    for p in range(1, incoming_ref.shape[0]):
        total = total + incoming_ref[p].astype(F32)
    squares = total[:, HALF : HALF + 1] + total[:, HALF + 1 : HALF + 2] + total[:, HALF + 2 : HALF + 3]
    scale = lax.rsqrt(squares * (1.0 / (HEADS * HEAD_DIM)) + EPS)
    out_ref[...] = (total[:, 0:HALF] * scale).astype(BF)


VM = pl.BlockSpec(memory_space=pltpu.VMEM)
SM = pl.BlockSpec(memory_space=pltpu.SMEM)
HB = pl.BlockSpec(memory_space=pltpu.HBM)


def in_hbm(array):
    return pltpu.with_memory_space_constraint(array, pltpu.HBM)


PARAMS = pltpu.CompilerParams(vmem_limit_bytes=VMEM_LIMIT)


def per_device(
    token_ids,
    decode_prompt,
    embedding,
    norm_gain,
    w_zx,
    w_bcdt,
    conv_x_weight,
    conv_x_bias,
    conv_bc_weight,
    conv_bc_bias,
    dt_bias,
    a_log,
    d_skip,
    gate_norm_gain,
    w_out,
    state_parts,
    seg_rate,
    x_tail,
    bc_tail,
):
    ctx, group, tp = (lax.axis_index(a) for a in ("ctx", "dp", "tp"))
    n_ctx, n_dp, n_tp = (lax.axis_size(a) for a in ("ctx", "dp", "tp"))
    peers = n_ctx * n_tp
    slots = state_parts.shape[1]
    heads = w_zx.shape[1]
    width = state_parts.shape[-1]
    steps = token_ids.shape[0]
    vocab_rows, features = embedding.shape
    model = norm_gain.shape[0]
    rows = steps * slots
    channels = heads * HEAD_DIM

    near = pl.pallas_call(
        lookup_kernel,
        out_shape=jax.ShapeDtypeStruct((n_dp, SIDE_ROWS, LANES), BF),
        in_specs=[HB] * 5,
        out_specs=VM,
        scratch_shapes=[
            pltpu.SMEM(token_ids.shape, jnp.int32),
            pltpu.SMEM(decode_prompt.shape, jnp.int32),
            pltpu.VMEM((features, vocab_rows), BF),
            pltpu.VMEM(x_tail.shape, BF),
            pltpu.VMEM((bc_tail.shape[1], slots, bc_tail.shape[2]), BF),
            pltpu.VMEM((n_dp * rows, LANES), jnp.int32),
            pltpu.VMEM((n_dp + slots, SIDE_ROWS, LANES), F32),
            pltpu.SemaphoreType.DMA((5,)),
        ],
        compiler_params=PARAMS,
        name="lookup",
    )(
        in_hbm(token_ids),
        in_hbm(decode_prompt),
        in_hbm(embedding.T),
        in_hbm(x_tail),
        in_hbm(jnp.swapaxes(bc_tail, 0, 1)),
    )
    near = exchange(near, "dp")

    rates = jnp.swapaxes(seg_rate[0].reshape(slots, n_ctx, heads), 0, 1)
    rates = jnp.stack(in_three(rates), axis=1).reshape(n_ctx, -1)
    rates = jnp.pad(rates, ((0, 0), (0, SIDE_ROWS - rates.shape[1])))
    rates = jnp.broadcast_to(rates[..., None], (n_ctx, SIDE_ROWS, width))
    sent = pl.pallas_call(
        pack_kernel,
        out_shape=jax.ShapeDtypeStruct((n_ctx, STATE_ROWS + SIDE_ROWS, width), BF),
        in_specs=[VM, VM, HB],
        out_specs=HB,
        scratch_shapes=[
            pltpu.VMEM((n_ctx, SIDE_ROWS, width), BF),
            pltpu.SemaphoreType.DMA((3,)),
        ],
        compiler_params=PARAMS,
        name="pack",
    )(near, rates, state_parts.reshape(slots, n_ctx, ONE_STATE, width))
    got = exchange(sent, "ctx")

    w_near = lax.all_gather(w_bcdt.T, "tp")
    own_columns = n_tp * w_bcdt.shape[1]
    w_near = w_near.reshape(own_columns, 2, n_ctx // 2, n_tp, features)
    w_near = lax.dynamic_index_in_dim(w_near, tp, 3, keepdims=False)
    w_near = jnp.swapaxes(w_near, 1, 2).reshape(own_columns, -1)
    w_near = jnp.concatenate([w_near, w_near], axis=0)
    w_near = jnp.pad(w_near, ((HALF, LANES - HALF - 2 * own_columns), (0, 0)))
    near_gain = norm_gain.reshape(2, n_ctx // 2, n_tp, features)
    near_gain = lax.dynamic_index_in_dim(near_gain, tp, 2, keepdims=False)
    near_gain = jnp.swapaxes(near_gain, 0, 1).reshape(n_ctx // 2, -1)
    wanted = decode_prompt.reshape(n_dp, slots) - group * slots
    prompt_for = jnp.any(wanted == 1, axis=1).astype(jnp.int32)
    own_slots = lax.dynamic_slice_in_dim(decode_prompt, group * slots, slots)

    def spread(values):
        return jnp.broadcast_to(values[:, None], (heads, HEAD_DIM)).reshape(1, channels)

    small = jnp.concatenate(
        [
            conv_x_weight.reshape(4, channels),
            conv_bc_weight[:, :width],
            conv_bc_weight[:, width:],
            conv_x_bias.reshape(1, channels),
            conv_bc_bias.reshape(2, width),
            spread(dt_bias),
            spread(a_log),
            spread(d_skip),
            gate_norm_gain.reshape(1, channels),
        ],
        axis=0,
    )
    small = jnp.pad(small, ((0, -small.shape[0] % 8), (0, 0)))

    piece = pl.pallas_call(
        columns_kernel,
        out_shape=jax.ShapeDtypeStruct((peers, rows, LANES), BF),
        in_specs=[SM, VM, VM, VM],
        out_specs=HB,
        scratch_shapes=[
            pltpu.VMEM((n_ctx, 8, LANES), F32),
            pltpu.VMEM((peers, rows, LANES), BF),
            pltpu.SemaphoreType.DMA(()),
        ],
        compiler_params=PARAMS,
        name="columns",
    )(ctx.astype(jnp.int32)[None], got, near_gain, w_near)
    piece, got = lax.optimization_barrier((piece, got))
    everyone = exchange(piece, BOTH)

    routed = pl.pallas_call(
        combine_kernel,
        out_shape=jax.ShapeDtypeStruct((n_dp, ONE_STATE, width), BF),
        in_specs=[SM, VM],
        out_specs=HB,
        scratch_shapes=[
            pltpu.VMEM((slots, ONE_STATE, width), BF),
            pltpu.SemaphoreType.DMA((n_dp,)),
        ],
        compiler_params=PARAMS,
        name="combine",
    )(prompt_for, got)
    arrived = exchange(routed, "dp")

    head_at = (tp * n_ctx + ctx) * heads
    place = jnp.concatenate(
        [own_slots // slots, ((LANES - head_at) % LANES)[None]]
    ).astype(jnp.int32)
    ready, c_parts, extra = pl.pallas_call(
        project_kernel,
        out_shape=(
            jax.ShapeDtypeStruct((32, LANES), F32),
            jax.ShapeDtypeStruct((32, LANES), BF),
            jax.ShapeDtypeStruct((24, LANES), F32),
        ),
        in_specs=[SM, VM, VM, VM, VM, VM],
        out_specs=(VM, VM, VM),
        scratch_shapes=[pltpu.VMEM((16, LANES), F32) for _ in range(3)],
        compiler_params=PARAMS,
        name="project",
    )(
        place,
        everyone,
        near,
        norm_gain.reshape(model // LANES, LANES),
        small,
        w_zx.reshape(2 * channels, model),
    )
    outgoing = pl.pallas_call(
        decode_kernel,
        out_shape=jax.ShapeDtypeStruct((peers, rows, LANES), BF),
        in_specs=[SM, VM, VM, VM, HB],
        out_specs=HB,
        scratch_shapes=[
            pltpu.VMEM((channels, model), BF),
            pltpu.VMEM((peers, rows, LANES), BF),
            pltpu.SemaphoreType.DMA((peers // 16,)),
            pltpu.SemaphoreType.DMA((peers // 16,)),
        ],
        compiler_params=PARAMS,
        name="decode",
    )(place, arrived, ready, c_parts, in_hbm(w_out.reshape(channels, model)))
    incoming = exchange(outgoing, BOTH)

    start = jnp.stack(
        [lax.dynamic_index_in_dim(arrived, place[s], 0, keepdims=False) for s in range(slots)]
    )
    push = extra[0:8].reshape(steps, slots, channels)
    b_conv = extra[8:16].reshape(steps, slots, width)
    kept = extra[16:18]
    final = kept[:, :, None] * start.astype(F32) + jnp.einsum(
        "tpc,tpn->pcn", push, b_conv, precision=lax.Precision.HIGHEST
    )

    mixed = pl.pallas_call(
        finish_kernel,
        out_shape=jax.ShapeDtypeStruct((rows, features), BF),
        in_specs=[VM],
        out_specs=VM,
        compiler_params=PARAMS,
        name="finish",
    )(incoming)
    return (
        mixed.reshape(steps, slots, features),
        final.reshape(slots, heads, HEAD_DIM, width),
    )


def solution(mesh):
    return jax.shard_map(
        per_device,
        mesh=mesh,
        in_specs=(
            P(),
            P(),
            P("dp", ("ctx", "tp")),
            P(),
            P(None, ("tp", "ctx"), None, None),
            P(None, ("ctx", "tp")),
            P(None, ("tp", "ctx"), None),
            P(("tp", "ctx"), None),
            P(),
            P(),
            P(("tp", "ctx")),
            P(("tp", "ctx")),
            P(("tp", "ctx")),
            P(("tp", "ctx"), None),
            P(("tp", "ctx"), None, None),
            P("ctx", "dp", "tp", None, None),
            P("ctx", "dp", "tp"),
            P("dp", None, ("tp", "ctx"), None),
            P("dp", None, None),
        ),
        out_specs=(P(None, "dp", ("ctx", "tp")), P("dp", ("tp", "ctx"), None, None)),
        check_vma=False,
    )
```

```python
import jax
import jax.numpy as jnp
from jax import lax
from jax.experimental import pallas as pl
from jax.experimental.pallas import tpu as pltpu
from jax.sharding import PartitionSpec as P

HEADS = 128
HEAD_DIM = 64
EPS = 1e-05
BOTH = ("ctx", "tp")
BF = jnp.bfloat16
F32 = jnp.float32
LANES = 128
HALF = 64
VMEM_LIMIT = 24 * 1024 * 1024

STATE_ROWS = 256
SIDE_ROWS = 16
ROWS_AT = 12
ONE_STATE = 128


def exchange(pieces, axis):
    return lax.all_to_all(pieces, axis, 0, 0, tiled=True)


def in_three(values):
    first = values.astype(BF)
    rest = values - first.astype(F32)
    second = rest.astype(BF)
    third = (rest - second.astype(F32)).astype(BF)
    return first, second, third


def silu(v):
    return v / (1.0 + jnp.exp(-v))


def low_half(shape=(8, LANES)):
    return lax.broadcasted_iota(jnp.int32, shape, 1) < HALF


def lookup_kernel(
    tokens_hbm, prompt_hbm, table_hbm, x_tail_hbm, bc_tail_hbm, out_ref,
    tokens_ref, prompt_ref, table_ref, x_tail_ref, bc_tail_ref, token_ref, block_ref, sems,
):
    pairs = [
        (tokens_hbm, tokens_ref),
        (prompt_hbm, prompt_ref),
        (table_hbm, table_ref),
        (x_tail_hbm, x_tail_ref),
        (bc_tail_hbm, bc_tail_ref),
    ]
    loads = [pltpu.make_async_copy(a, b, sems.at[n]) for n, (a, b) in enumerate(pairs)]
    for load in loads:
        load.start()
    group = lax.axis_index("dp")
    groups = out_ref.shape[0]
    slots = prompt_ref.shape[0] // groups
    steps = tokens_ref.shape[0]
    rows = steps * slots
    features, vocab_rows = table_ref.shape
    first = group * vocab_rows
    loads[0].wait()
    loads[1].wait()
    for g in range(groups):
        for step in range(steps):
            for slot in range(slots):
                token = tokens_ref[step, prompt_ref[g * slots + slot]] - first
                at = g * rows + step * slots + slot
                token_ref[at : at + 1, :] = jnp.full((1, LANES), token, jnp.int32)
    loads[2].wait()
    tokens = token_ref[:, 0:1]
    found = jnp.zeros((groups * rows, LANES), F32)
    whole = vocab_rows // LANES * LANES
    bounds = [*range(0, whole, 1024), whole, vocab_rows]
    for low_at, high_at in zip(bounds[:-1], bounds[1:]):
        ids = lax.broadcasted_iota(jnp.int32, (groups * rows, high_at - low_at), 1) + low_at
        hot = jnp.where(tokens == ids, 1.0, 0.0).astype(BF)
        table = table_ref[:, low_at:high_at]
        found = found + lax.dot_general(
            hot,
            jnp.concatenate([table, table], axis=0),
            (((1,), (1,)), ((), ())),
            preferred_element_type=F32,
        )
    low = low_half((4, LANES))
    loads[3].wait()
    loads[4].wait()
    for p in range(slots):
        block_ref[groups + p] = jnp.zeros((SIDE_ROWS, LANES), F32)
        for k in range(3):
            pair = x_tail_ref[p, k].astype(F32)
            block_ref[groups + p, k : k + 1, :] = jnp.concatenate([pair[0:1], pair[1:2]], axis=1)
            both = bc_tail_ref[k, p : p + 1, :].astype(F32)
            block_ref[groups + p, 3 + 2 * k : 4 + 2 * k, :] = both[:, 0:LANES]
            block_ref[groups + p, 4 + 2 * k : 5 + 2 * k, :] = both[:, LANES : 2 * LANES]
    for g in range(groups):
        wanted = group * slots + 1
        second = (prompt_ref[g * slots] == wanted) | (prompt_ref[g * slots + 1] == wanted)
        block_ref[g] = block_ref[jnp.where(second, groups + 1, groups)]
        block_ref[g, ROWS_AT : ROWS_AT + 4, :] = jnp.where(
            low, found[g * rows : g * rows + 4], found[g * rows + 4 : g * rows + 8]
        )
        out_ref[g] = block_ref[g].astype(BF)


def pack_kernel(states_ref, out_ref, sems):
    moves = []
    for p in range(states_ref.shape[0]):
        moves.append(
            pltpu.make_async_copy(
                states_ref.at[p], out_ref.at[:, p * ONE_STATE : (p + 1) * ONE_STATE, :], sems.at[p]
            )
        )
        moves[-1].start()
    for move in moves:
        move.wait()


def side_kernel(near_ref, rates_ref, packed_ref, out_ref, side_ref, sem):
    total = near_ref[0].astype(F32)
    for g in range(1, near_ref.shape[0]):
        total = total + near_ref[g].astype(F32)
    row = lax.broadcasted_iota(jnp.int32, (SIDE_ROWS, LANES), 0)
    total = jnp.where(row >= ROWS_AT, total, 0.0)
    for c in range(out_ref.shape[0]):
        side_ref[c] = (rates_ref[c].astype(F32) + total).astype(BF)
    side = pltpu.make_async_copy(
        side_ref, out_ref.at[:, STATE_ROWS : STATE_ROWS + SIDE_ROWS, :], sem
    )
    side.start()
    side.wait()


def combine_kernel(chosen_ref, got_ref, out_ref, combined_ref, sems):
    count = got_ref.shape[0]
    groups = out_ref.shape[0]
    rates = []
    for k in range(count):
        parts = got_ref[k, STATE_ROWS : STATE_ROWS + SIDE_ROWS, :].astype(F32)
        rates.append(parts[0:4] + parts[4:8] + parts[8:12])
    weights = [None] * count
    later = jnp.zeros_like(rates[0])
    for k in reversed(range(count)):
        weights[k] = jnp.exp(-later)
        later = later + rates[k]
    for part in range(4):
        total = jnp.zeros((HEAD_DIM, LANES), F32)
        for k in range(count):
            own = got_ref[k, part * HEAD_DIM : (part + 1) * HEAD_DIM, :].astype(F32)
            total = total + (own * weights[k][part : part + 1]).astype(BF).astype(F32)
        at = (part % 2) * HEAD_DIM
        combined_ref[part // 2, at : at + HEAD_DIM, :] = total.astype(BF)
    moves = [
        pltpu.make_async_copy(combined_ref.at[chosen_ref[g]], out_ref.at[g], sems.at[g])
        for g in range(groups)
    ]
    for move in moves:
        move.start()
    for move in moves:
        move.wait()


def columns_kernel(place_ref, got_ref, gain_ref, weight_ref, out_ref, near_ref, tile_ref, sem):
    count = got_ref.shape[0]
    low = low_half()
    for c in range(count):
        side = got_ref[c, STATE_ROWS : STATE_ROWS + SIDE_ROWS, :].astype(F32)
        four = side[ROWS_AT : ROWS_AT + 4]
        near_ref[c, 0:4, :] = four
        near_ref[c, 4:8, :] = pltpu.roll(four, HALF, 1)
    pieces = []
    for k in range(count // 2):
        rows = jnp.where(low, near_ref[k], pltpu.roll(near_ref[count // 2 + k], HALF, 1))
        pieces.append((rows * gain_ref[k : k + 1, :]).astype(BF))
    weighted = jnp.concatenate(pieces, axis=1)
    partial = lax.dot_general(
        weighted, weight_ref[...], (((1,), (1,)), ((), ())), preferred_element_type=F32
    )
    own = near_ref[place_ref[0]]
    lane = lax.broadcasted_iota(jnp.int32, (8, LANES), 1)
    first = partial.astype(BF).astype(F32)
    tile = jnp.where(lane < HALF, own, jnp.where(lane < HALF + 24, first, partial - first))
    tile_ref[...] = jnp.broadcast_to(tile.astype(BF)[None], tile_ref.shape)
    move = pltpu.make_async_copy(tile_ref, out_ref, sem)
    move.start()
    move.wait()


def project_kernel(
    place_ref,
    everyone_ref,
    near_ref,
    gain_ref,
    small_ref,
    w_zx_ref,
    ready_ref,
    c_parts_ref,
    extra_ref,
    x_ref,
    b_ref,
    c_ref,
):
    peers = everyone_ref.shape[0]
    model = peers * HALF
    lane = lax.broadcasted_iota(jnp.int32, (8, LANES), 1)
    row = lax.broadcasted_iota(jnp.int32, (8, LANES), 0)
    low = lane < HALF

    tiles = [everyone_ref[p].astype(F32) for p in range(peers)]
    rows = [
        jnp.where(low, tiles[2 * n], pltpu.roll(tiles[2 * n + 1], HALF, 1)) for n in range(peers // 2)
    ]
    squares = rows[0] * rows[0]
    for r in rows[1:]:
        squares = squares + r * r
    inverse = lax.rsqrt(jnp.sum(squares, axis=1, keepdims=True) * (1.0 / model) + EPS)
    normed = jnp.concatenate(
        [(r * inverse * gain_ref[n : n + 1, :]).astype(BF) for n, r in enumerate(rows)], axis=1
    )

    columns = [jnp.zeros((8, LANES), F32) for _ in range(3)]
    for c in range(16):
        part = tiles[4 * c] + tiles[4 * c + 1] + tiles[4 * c + 2] + tiles[4 * c + 3]
        part = part + pltpu.roll(part, LANES - 24, 1)
        part = jnp.where((lane >= HALF) & (lane < HALF + 24), part, 0.0)
        first, offset = divmod(c * 24, LANES)
        part = pltpu.roll(part, (offset - HALF) % LANES, 1)
        if offset + 24 <= LANES:
            columns[first] = columns[first] + part
        else:
            columns[first] = columns[first] + jnp.where(lane >= offset, part, 0.0)
            columns[first + 1] = columns[first + 1] + jnp.where(lane < offset, part, 0.0)
    columns = [v * inverse for v in columns]

    for slot in range(2):
        tail = near_ref[place_ref[slot]].astype(F32)
        for k in range(3):
            at = 2 * k + slot
            x_ref[at : at + 1, :] = tail[k : k + 1]
            b_ref[at : at + 1, :] = tail[3 + 2 * k : 4 + 2 * k]
            c_ref[at : at + 1, :] = tail[4 + 2 * k : 5 + 2 * k]
    b_ref[6:14, :] = columns[0]
    c_ref[6:14, :] = columns[1]

    def convolved(ref, weight_at, bias_at):
        total = ref[0:8, :] * small_ref[weight_at : weight_at + 1, :]
        for k in range(1, 4):
            total = total + ref[2 * k : 2 * k + 8, :] * small_ref[weight_at + k : weight_at + k + 1, :]
        return silu(total + small_ref[bias_at : bias_at + 1, :])

    b_conv = convolved(b_ref, 4, 13)
    c_conv = convolved(c_ref, 8, 14)

    raw = pltpu.roll(columns[2], place_ref[2], 1)
    raw = jnp.where(low, raw[:, 0:1], raw[:, 1:2]) + small_ref[15:16, :]
    step = jnp.maximum(raw, 0.0) + jnp.log1p(jnp.exp(-jnp.abs(raw)))
    log_retain = -step * jnp.exp(small_ref[16:17, :])

    def earlier(v, lag):
        return jnp.where(row >= 2 * lag, pltpu.roll(v, 2 * lag, 0), 0.0)

    log_total = log_retain
    for lag in range(1, 4):
        log_total = log_total + earlier(log_retain, lag)

    parts = [p.astype(F32) for p in in_three(c_conv)]
    c_parts_ref[...] = jnp.concatenate([*parts, jnp.zeros_like(c_conv)], axis=0).astype(BF)

    projected = lax.dot_general(
        normed, w_zx_ref[...], (((1,), (1,)), ((), ())), preferred_element_type=F32
    )
    x_ref[6:14, :] = projected[:, LANES : 2 * LANES]
    x_conv = convolved(x_ref, 0, 12)
    drive = step * x_conv
    y = small_ref[17:18, :] * x_conv
    for lag in range(4):
        match = jnp.sum(c_conv * earlier(b_conv, lag), axis=1, keepdims=True)
        if lag == 0:
            y = y + drive * match
        else:
            decay = jnp.exp(log_total - earlier(log_total, lag))
            y = y + decay * earlier(drive, lag) * match
    ready_ref[0:8, :] = jnp.exp(log_total)
    ready_ref[8:16, :] = y
    ready_ref[16:24, :] = silu(projected[:, 0:LANES])
    ready_ref[24:32, :] = jnp.broadcast_to(small_ref[18:19, :], (8, LANES))

    last = jnp.where(row % 2 == 0, log_total[6:7], log_total[7:8])
    extra_ref[0:8, :] = jnp.exp(last - log_total) * drive
    extra_ref[8:16, :] = b_conv
    extra_ref[16:24, :] = jnp.exp(last)


def decode_kernel(
    place_ref, arrived_ref, ready_ref, c_parts_ref, w_out_hbm, out_ref, w_out_ref, tile_ref, load_sem, sems
):
    load = pltpu.make_async_copy(w_out_hbm, w_out_ref, load_sem)
    load.start()
    lane = lax.broadcasted_iota(jnp.int32, (8, LANES), 1)
    row = lax.broadcasted_iota(jnp.int32, (8, LANES), 0)
    low = lane < HALF
    from_start = []
    for slot in range(2):
        product = lax.dot_general(
            c_parts_ref[...],
            arrived_ref[place_ref[slot]],
            (((1,), (1,)), ((), ())),
            preferred_element_type=F32,
        )
        from_start.append(product[0:8] + product[8:16] + product[16:24])
    y = ready_ref[0:8, :] * jnp.where(row % 2 == 0, from_start[0], from_start[1]) + ready_ref[8:16, :]
    gated = y * ready_ref[16:24, :]
    weighted = (gated * ready_ref[24:32, :]).astype(BF)
    total = jnp.sum(gated * gated, axis=1, keepdims=True)
    parts = [p.astype(F32) for p in in_three(total)]
    aside = jnp.where(
        lane == HALF,
        parts[0],
        jnp.where(lane == HALF + 1, parts[1], jnp.where(lane == HALF + 2, parts[2], 0.0)),
    )
    moves = []
    load.wait()
    for n in range(out_ref.shape[0] // 16):
        wide = jnp.dot(
            weighted, w_out_ref[:, n * 1024 : (n + 1) * 1024], preferred_element_type=F32
        )
        for m in range(8):
            piece = wide[:, m * LANES : (m + 1) * LANES]
            tile_ref[16 * n + 2 * m] = jnp.where(low, piece, aside).astype(BF)
            tile_ref[16 * n + 2 * m + 1] = jnp.where(low, pltpu.roll(piece, HALF, 1), aside).astype(BF)
        part = pl.ds(16 * n, 16)
        moves.append(pltpu.make_async_copy(tile_ref.at[part], out_ref.at[part], sems.at[n]))
        moves[-1].start()
    for move in moves:
        move.wait()


def finish_kernel(incoming_ref, out_ref):
    total = incoming_ref[0].astype(F32)
    for p in range(1, incoming_ref.shape[0]):
        total = total + incoming_ref[p].astype(F32)
    squares = total[:, HALF : HALF + 1] + total[:, HALF + 1 : HALF + 2] + total[:, HALF + 2 : HALF + 3]
    scale = lax.rsqrt(squares * (1.0 / (HEADS * HEAD_DIM)) + EPS)
    out_ref[...] = (total[:, 0:HALF] * scale).astype(BF)


VM = pl.BlockSpec(memory_space=pltpu.VMEM)
SM = pl.BlockSpec(memory_space=pltpu.SMEM)
HB = pl.BlockSpec(memory_space=pltpu.HBM)


def in_hbm(array):
    return pltpu.with_memory_space_constraint(array, pltpu.HBM)


PARAMS = pltpu.CompilerParams(vmem_limit_bytes=VMEM_LIMIT)


def per_device(
    token_ids,
    decode_prompt,
    embedding,
    norm_gain,
    w_zx,
    w_bcdt,
    conv_x_weight,
    conv_x_bias,
    conv_bc_weight,
    conv_bc_bias,
    dt_bias,
    a_log,
    d_skip,
    gate_norm_gain,
    w_out,
    state_parts,
    seg_rate,
    x_tail,
    bc_tail,
):
    ctx, group, tp = (lax.axis_index(a) for a in ("ctx", "dp", "tp"))
    n_ctx, n_dp, n_tp = (lax.axis_size(a) for a in ("ctx", "dp", "tp"))
    peers = n_ctx * n_tp
    slots = state_parts.shape[1]
    heads = w_zx.shape[1]
    width = state_parts.shape[-1]
    steps = token_ids.shape[0]
    vocab_rows, features = embedding.shape
    model = norm_gain.shape[0]
    rows = steps * slots
    channels = heads * HEAD_DIM

    near = pl.pallas_call(
        lookup_kernel,
        out_shape=jax.ShapeDtypeStruct((n_dp, SIDE_ROWS, LANES), BF),
        in_specs=[HB] * 5,
        out_specs=VM,
        scratch_shapes=[
            pltpu.SMEM(token_ids.shape, jnp.int32),
            pltpu.SMEM(decode_prompt.shape, jnp.int32),
            pltpu.VMEM((features, vocab_rows), BF),
            pltpu.VMEM(x_tail.shape, BF),
            pltpu.VMEM((bc_tail.shape[1], slots, bc_tail.shape[2]), BF),
            pltpu.VMEM((n_dp * rows, LANES), jnp.int32),
            pltpu.VMEM((n_dp + slots, SIDE_ROWS, LANES), F32),
            pltpu.SemaphoreType.DMA((5,)),
        ],
        compiler_params=PARAMS,
        name="lookup",
    )(
        in_hbm(token_ids),
        in_hbm(decode_prompt),
        in_hbm(embedding.T),
        in_hbm(x_tail),
        in_hbm(jnp.swapaxes(bc_tail, 0, 1)),
    )
    near = exchange(near, "dp")

    w_near = lax.all_gather(w_bcdt.T, "tp")

    rates = jnp.swapaxes(seg_rate[0].reshape(slots, n_ctx, heads), 0, 1)
    rates = jnp.stack(in_three(rates), axis=1).reshape(n_ctx, -1)
    rates = jnp.pad(rates, ((0, 0), (0, SIDE_ROWS - rates.shape[1])))
    rates = jnp.broadcast_to(rates[..., None], (n_ctx, SIDE_ROWS, width))
    packed = pl.pallas_call(
        pack_kernel,
        out_shape=pltpu.HBM((n_ctx, STATE_ROWS + SIDE_ROWS, width), BF),
        in_specs=[HB],
        out_specs=HB,
        scratch_shapes=[pltpu.SemaphoreType.DMA((slots,))],
        compiler_params=PARAMS,
        name="pack",
    )(in_hbm(state_parts.reshape(slots, n_ctx, ONE_STATE, width)))
    w_near, packed, rates = lax.optimization_barrier((w_near, packed, rates))
    sent = pl.pallas_call(
        side_kernel,
        out_shape=pltpu.HBM((n_ctx, STATE_ROWS + SIDE_ROWS, width), BF),
        in_specs=[VM, VM, HB],
        out_specs=HB,
        scratch_shapes=[
            pltpu.VMEM((n_ctx, SIDE_ROWS, width), BF),
            pltpu.SemaphoreType.DMA(()),
        ],
        input_output_aliases={2: 0},
        compiler_params=PARAMS,
        name="side",
    )(near, rates, in_hbm(packed))
    got = exchange(sent, "ctx")

    own_columns = n_tp * w_bcdt.shape[1]
    w_near = w_near.reshape(own_columns, 2, n_ctx // 2, n_tp, features)
    w_near = lax.dynamic_index_in_dim(w_near, tp, 3, keepdims=False)
    w_near = jnp.swapaxes(w_near, 1, 2).reshape(own_columns, -1)
    w_near = jnp.concatenate([w_near, w_near], axis=0)
    w_near = jnp.pad(w_near, ((HALF, LANES - HALF - 2 * own_columns), (0, 0)))
    near_gain = norm_gain.reshape(2, n_ctx // 2, n_tp, features)
    near_gain = lax.dynamic_index_in_dim(near_gain, tp, 2, keepdims=False)
    near_gain = jnp.swapaxes(near_gain, 0, 1).reshape(n_ctx // 2, -1)
    wanted = decode_prompt.reshape(n_dp, slots) - group * slots
    prompt_for = jnp.any(wanted == 1, axis=1).astype(jnp.int32)
    own_slots = lax.dynamic_slice_in_dim(decode_prompt, group * slots, slots)

    def spread(values):
        return jnp.broadcast_to(values[:, None], (heads, HEAD_DIM)).reshape(1, channels)

    small = jnp.concatenate(
        [
            conv_x_weight.reshape(4, channels),
            conv_bc_weight[:, :width],
            conv_bc_weight[:, width:],
            conv_x_bias.reshape(1, channels),
            conv_bc_bias.reshape(2, width),
            spread(dt_bias),
            spread(a_log),
            spread(d_skip),
            gate_norm_gain.reshape(1, channels),
        ],
        axis=0,
    )
    small = jnp.pad(small, ((0, -small.shape[0] % 8), (0, 0)))

    piece = pl.pallas_call(
        columns_kernel,
        out_shape=jax.ShapeDtypeStruct((peers, rows, LANES), BF),
        in_specs=[SM, VM, VM, VM],
        out_specs=HB,
        scratch_shapes=[
            pltpu.VMEM((n_ctx, 8, LANES), F32),
            pltpu.VMEM((peers, rows, LANES), BF),
            pltpu.SemaphoreType.DMA(()),
        ],
        compiler_params=PARAMS,
        name="columns",
    )(ctx.astype(jnp.int32)[None], got, near_gain, w_near)
    piece, got = lax.optimization_barrier((piece, got))
    everyone = exchange(piece, BOTH)

    routed = pl.pallas_call(
        combine_kernel,
        out_shape=jax.ShapeDtypeStruct((n_dp, ONE_STATE, width), BF),
        in_specs=[SM, VM],
        out_specs=HB,
        scratch_shapes=[
            pltpu.VMEM((slots, ONE_STATE, width), BF),
            pltpu.SemaphoreType.DMA((n_dp,)),
        ],
        compiler_params=PARAMS,
        name="combine",
    )(prompt_for, got)
    arrived = exchange(routed, "dp")

    head_at = (tp * n_ctx + ctx) * heads
    place = jnp.concatenate(
        [own_slots // slots, ((LANES - head_at) % LANES)[None]]
    ).astype(jnp.int32)
    ready, c_parts, extra = pl.pallas_call(
        project_kernel,
        out_shape=(
            jax.ShapeDtypeStruct((32, LANES), F32),
            jax.ShapeDtypeStruct((32, LANES), BF),
            jax.ShapeDtypeStruct((24, LANES), F32),
        ),
        in_specs=[SM, VM, VM, VM, VM, VM],
        out_specs=(VM, VM, VM),
        scratch_shapes=[pltpu.VMEM((16, LANES), F32) for _ in range(3)],
        compiler_params=PARAMS,
        name="project",
    )(
        place,
        everyone,
        near,
        norm_gain.reshape(model // LANES, LANES),
        small,
        w_zx.reshape(2 * channels, model),
    )
    outgoing = pl.pallas_call(
        decode_kernel,
        out_shape=jax.ShapeDtypeStruct((peers, rows, LANES), BF),
        in_specs=[SM, VM, VM, VM, HB],
        out_specs=HB,
        scratch_shapes=[
            pltpu.VMEM((channels, model), BF),
            pltpu.VMEM((peers, rows, LANES), BF),
            pltpu.SemaphoreType.DMA(()),
            pltpu.SemaphoreType.DMA((peers // 16,)),
        ],
        compiler_params=PARAMS,
        name="decode",
    )(place, arrived, ready, c_parts, in_hbm(w_out.reshape(channels, model)))
    incoming = exchange(outgoing, BOTH)

    start = jnp.stack(
        [lax.dynamic_index_in_dim(arrived, place[s], 0, keepdims=False) for s in range(slots)]
    )
    push = extra[0:8].reshape(steps, slots, channels)
    b_conv = extra[8:16].reshape(steps, slots, width)
    kept = extra[16:18]
    final = kept[:, :, None] * start.astype(F32) + jnp.einsum(
        "tpc,tpn->pcn", push, b_conv, precision=lax.Precision.HIGHEST
    )

    mixed = pl.pallas_call(
        finish_kernel,
        out_shape=jax.ShapeDtypeStruct((rows, features), BF),
        in_specs=[VM],
        out_specs=VM,
        compiler_params=PARAMS,
        name="finish",
    )(incoming)
    return (
        mixed.reshape(steps, slots, features),
        final.reshape(slots, heads, HEAD_DIM, width),
    )


def solution(mesh):
    return jax.shard_map(
        per_device,
        mesh=mesh,
        in_specs=(
            P(),
            P(),
            P("dp", ("ctx", "tp")),
            P(),
            P(None, ("tp", "ctx"), None, None),
            P(None, ("ctx", "tp")),
            P(None, ("tp", "ctx"), None),
            P(("tp", "ctx"), None),
            P(),
            P(),
            P(("tp", "ctx")),
            P(("tp", "ctx")),
            P(("tp", "ctx")),
            P(("tp", "ctx"), None),
            P(("tp", "ctx"), None, None),
            P("ctx", "dp", "tp", None, None),
            P("ctx", "dp", "tp"),
            P("dp", None, ("tp", "ctx"), None),
            P("dp", None, None),
        ),
        out_specs=(P(None, "dp", ("ctx", "tp")), P("dp", ("tp", "ctx"), None, None)),
        check_vma=False,
    )
```

```python
import jax
import jax.numpy as jnp
from jax import lax
from jax.experimental import pallas as pl
from jax.experimental.pallas import tpu as pltpu
from jax.sharding import PartitionSpec as P

HEADS = 128
HEAD_DIM = 64
EPS = 1e-05
BOTH = ("ctx", "tp")
BF = jnp.bfloat16
F32 = jnp.float32
LANES = 128
HALF = 64
VMEM_LIMIT = 24 * 1024 * 1024

STATE_ROWS = 256
RATE_ROWS = 16
TOKEN_ROWS = 32
SIDE_ROWS = RATE_ROWS + TOKEN_ROWS
ONE_STATE = 128
TAIL_ROWS = 16
NEAR_ROWS = 64


def exchange(pieces, axis):
    return lax.all_to_all(pieces, axis, 0, 0, tiled=True)


def in_three(values):
    first = values.astype(BF)
    rest = values - first.astype(F32)
    second = rest.astype(BF)
    third = (rest - second.astype(F32)).astype(BF)
    return first, second, third


def silu(v):
    return v / (1.0 + jnp.exp(-v))


def low_half(shape=(8, LANES)):
    return lax.broadcasted_iota(jnp.int32, shape, 1) < HALF


def send_kernel(
    tokens_hbm, prompt_hbm, rate_hbm, table_hbm, states_hbm, out_ref,
    tokens_ref, prompt_ref, rate_ref, table_ref, states_ref, token_ref, rows_ref, block_ref, side_ref, sems,
):
    pairs = [
        (tokens_hbm, tokens_ref),
        (prompt_hbm, prompt_ref),
        (rate_hbm, rate_ref),
        (table_hbm, table_ref),
        (states_hbm, states_ref),
    ]
    loads = [pltpu.make_async_copy(a, b, sems.at[n]) for n, (a, b) in enumerate(pairs)]
    for load in loads:
        load.start()
    group = lax.axis_index("dp")
    count = out_ref.shape[0]
    slots = states_ref.shape[0]
    heads = rate_ref.shape[1] // count
    steps = tokens_ref.shape[0]
    rows = steps * slots
    groups = prompt_ref.shape[0] // slots
    vocab_rows = table_ref.shape[1]
    first = group * vocab_rows
    loads[0].wait()
    loads[1].wait()
    for g in range(groups):
        for step in range(steps):
            for slot in range(slots):
                token = tokens_ref[step, prompt_ref[g * slots + slot]] - first
                at = g * rows + step * slots + slot
                token_ref[at : at + 1, :] = jnp.full((1, LANES), token, jnp.int32)
    loads[2].wait()
    for c in range(count):
        for p in range(slots):
            for h in range(heads):
                at = (c * slots + p) * heads + h
                rows_ref[at : at + 1, :] = jnp.full((1, LANES), rate_ref[p, c * heads + h], F32)
    each = slots * heads
    parts = [p.astype(F32) for p in in_three(rows_ref[...])]
    for c in range(count):
        for n, part in enumerate(parts):
            block_ref[c, n * each : (n + 1) * each, :] = part[c * each : (c + 1) * each]
        block_ref[c, 3 * each : RATE_ROWS, :] = jnp.zeros((RATE_ROWS - 3 * each, LANES), F32)
        side_ref[c, 0:RATE_ROWS, :] = block_ref[c].astype(BF)
    loads[4].wait()
    stores = []
    for p in range(slots):
        stores.append(
            pltpu.make_async_copy(
                states_ref.at[p], out_ref.at[:, p * ONE_STATE : (p + 1) * ONE_STATE, :], sems.at[5 + p]
            )
        )
        stores[-1].start()
    loads[3].wait()
    tokens = token_ref[:, 0:1]
    found = jnp.zeros((groups * rows, LANES), F32)
    whole = vocab_rows // LANES * LANES
    bounds = [*range(0, whole, 1024), whole, vocab_rows]
    for low_at, high_at in zip(bounds[:-1], bounds[1:]):
        ids = lax.broadcasted_iota(jnp.int32, (groups * rows, high_at - low_at), 1) + low_at
        hot = jnp.where(tokens == ids, 1.0, 0.0).astype(BF)
        table = table_ref[:, low_at:high_at]
        found = found + lax.dot_general(
            hot,
            jnp.concatenate([table, table], axis=0),
            (((1,), (1,)), ((), ())),
            preferred_element_type=F32,
        )
    low = low_half((TOKEN_ROWS, LANES))
    tile = jnp.where(low, found[0:TOKEN_ROWS], found[TOKEN_ROWS : 2 * TOKEN_ROWS]).astype(BF)
    for c in range(count):
        side_ref[c, RATE_ROWS:SIDE_ROWS, :] = tile
    stores.append(
        pltpu.make_async_copy(
            side_ref, out_ref.at[:, STATE_ROWS : STATE_ROWS + SIDE_ROWS, :], sems.at[5 + slots]
        )
    )
    stores[-1].start()
    for store in stores:
        store.wait()


def combine_kernel(chosen_ref, got_ref, tails_ref, out_ref, bundle_ref, near_ref, sems):
    count = got_ref.shape[0]
    groups = out_ref.shape[0]
    own_rows = ONE_STATE + TAIL_ROWS
    rates = []
    for k in range(count):
        parts = got_ref[k, STATE_ROWS : STATE_ROWS + RATE_ROWS, :].astype(F32)
        rates.append(parts[0:4] + parts[4:8] + parts[8:12])
    weights = [None] * count
    later = jnp.zeros_like(rates[0])
    for k in reversed(range(count)):
        weights[k] = jnp.exp(-later)
        later = later + rates[k]
    for part in range(4):
        total = jnp.zeros((HEAD_DIM, LANES), F32)
        for k in range(count):
            own = got_ref[k, part * HEAD_DIM : (part + 1) * HEAD_DIM, :].astype(F32)
            total = total + (own * weights[k][part : part + 1]).astype(BF).astype(F32)
        at = (part % 2) * HEAD_DIM
        bundle_ref[part // 2, at : at + HEAD_DIM, :] = total.astype(BF)
    for p in range(bundle_ref.shape[0]):
        bundle_ref[p, ONE_STATE:own_rows, :] = tails_ref[p]
    moves = [
        pltpu.make_async_copy(
            bundle_ref.at[chosen_ref[g]], out_ref.at[g, 0:own_rows, :], sems.at[g]
        )
        for g in range(groups)
    ]
    for move in moves:
        move.start()
    low = low_half((TOKEN_ROWS, LANES))
    at = STATE_ROWS + RATE_ROWS
    for pair in range(0, count // 2, 2):
        early, late = [], []
        for k in (pair, pair + 1):
            one = got_ref[k, at : at + TOKEN_ROWS, :].astype(F32)
            two = got_ref[count // 2 + k, at : at + TOKEN_ROWS, :].astype(F32)
            early.append(jnp.where(low, one, pltpu.roll(two, HALF, 1)))
            late.append(jnp.where(low, pltpu.roll(one, HALF, 1), two))
        for g in range(groups):
            source = early if g < groups // 2 else late
            r = (g % (groups // 2)) * 8
            both = jnp.concatenate([s[r : r + 8] for s in source], axis=0)
            near_ref[g, pair * 8 : pair * 8 + 16, :] = both.astype(BF)
    moves.append(
        pltpu.make_async_copy(
            near_ref, out_ref.at[:, own_rows : own_rows + NEAR_ROWS, :], sems.at[groups]
        )
    )
    moves[-1].start()
    for move in moves:
        move.wait()


def columns_kernel(place_ref, arrived_ref, gain_ref, weight_ref, out_ref, near_ref, tile_ref, sem):
    groups = arrived_ref.shape[0]
    at = ONE_STATE + TAIL_ROWS
    total = arrived_ref[0, at : at + NEAR_ROWS, :].astype(F32)
    for g in range(1, groups):
        total = total + arrived_ref[g, at : at + NEAR_ROWS, :].astype(F32)
    pieces = []
    for k in range(NEAR_ROWS // 8):
        rows = total[k * 8 : (k + 1) * 8]
        near_ref[k] = rows
        pieces.append((rows * gain_ref[k : k + 1, :]).astype(BF))
    weighted = jnp.concatenate(pieces, axis=1)
    partial = lax.dot_general(
        weighted, weight_ref[...], (((1,), (1,)), ((), ())), preferred_element_type=F32
    )
    own = pltpu.roll(near_ref[place_ref[0]], place_ref[1], 1)
    lane = lax.broadcasted_iota(jnp.int32, (8, LANES), 1)
    first = partial.astype(BF).astype(F32)
    tile = jnp.where(lane < HALF, own, jnp.where(lane < HALF + 24, first, partial - first))
    tile_ref[...] = jnp.broadcast_to(tile.astype(BF)[None], tile_ref.shape)
    move = pltpu.make_async_copy(tile_ref, out_ref, sem)
    move.start()
    move.wait()


def decode_kernel(
    place_ref, everyone_ref, arrived_ref, gain_ref, small_ref, zx_ref, w_out_hbm, out_ref, extra_ref,
    wo_ref, x_ref, b_ref, c_ref, tile_ref, load_sem, sems,
):
    load_out = pltpu.make_async_copy(w_out_hbm, wo_ref, load_sem)
    load_out.start()
    peers = everyone_ref.shape[0]
    model = peers * HALF
    lane = lax.broadcasted_iota(jnp.int32, (8, LANES), 1)
    row = lax.broadcasted_iota(jnp.int32, (8, LANES), 0)
    low = lane < HALF

    tiles = [everyone_ref[p].astype(F32) for p in range(peers)]
    rows = [
        jnp.where(low, tiles[2 * n], pltpu.roll(tiles[2 * n + 1], HALF, 1)) for n in range(peers // 2)
    ]
    squares = rows[0] * rows[0]
    for r in rows[1:]:
        squares = squares + r * r
    inverse = lax.rsqrt(jnp.sum(squares, axis=1, keepdims=True) * (1.0 / model) + EPS)
    normed = jnp.concatenate(
        [(r * inverse * gain_ref[n : n + 1, :]).astype(BF) for n, r in enumerate(rows)], axis=1
    )

    columns = [jnp.zeros((8, LANES), F32) for _ in range(3)]
    for c in range(16):
        part = tiles[4 * c] + tiles[4 * c + 1] + tiles[4 * c + 2] + tiles[4 * c + 3]
        part = part + pltpu.roll(part, LANES - 24, 1)
        part = jnp.where((lane >= HALF) & (lane < HALF + 24), part, 0.0)
        first, offset = divmod(c * 24, LANES)
        part = pltpu.roll(part, (offset - HALF) % LANES, 1)
        if offset + 24 <= LANES:
            columns[first] = columns[first] + part
        else:
            columns[first] = columns[first] + jnp.where(lane >= offset, part, 0.0)
            columns[first + 1] = columns[first + 1] + jnp.where(lane < offset, part, 0.0)
    columns = [v * inverse for v in columns]

    for slot in range(2):
        tail = arrived_ref[place_ref[slot], ONE_STATE : ONE_STATE + TAIL_ROWS, :].astype(F32)
        for k in range(3):
            at = 2 * k + slot
            x_ref[at : at + 1, :] = tail[k : k + 1]
            b_ref[at : at + 1, :] = tail[3 + 2 * k : 4 + 2 * k]
            c_ref[at : at + 1, :] = tail[4 + 2 * k : 5 + 2 * k]
    b_ref[6:14, :] = columns[0]
    c_ref[6:14, :] = columns[1]

    def convolved(ref, weight_at, bias_at):
        total = ref[0:8, :] * small_ref[weight_at : weight_at + 1, :]
        for k in range(1, 4):
            total = total + ref[2 * k : 2 * k + 8, :] * small_ref[weight_at + k : weight_at + k + 1, :]
        return silu(total + small_ref[bias_at : bias_at + 1, :])

    b_conv = convolved(b_ref, 4, 13)
    c_conv = convolved(c_ref, 8, 14)

    raw = pltpu.roll(columns[2], place_ref[2], 1)
    raw = jnp.where(low, raw[:, 0:1], raw[:, 1:2]) + small_ref[15:16, :]
    step = jnp.maximum(raw, 0.0) + jnp.log1p(jnp.exp(-jnp.abs(raw)))
    log_retain = -step * jnp.exp(small_ref[16:17, :])

    def earlier(v, lag):
        return jnp.where(row >= 2 * lag, pltpu.roll(v, 2 * lag, 0), 0.0)

    log_total = log_retain
    for lag in range(1, 4):
        log_total = log_total + earlier(log_retain, lag)

    c_parts = jnp.concatenate([p.astype(F32) for p in in_three(c_conv)], axis=0).astype(BF)
    from_start = []
    for slot in range(2):
        state = arrived_ref[place_ref[slot], 0:ONE_STATE, :]
        product = lax.dot_general(
            c_parts, state, (((1,), (1,)), ((), ())), preferred_element_type=F32
        )
        from_start.append(product[0:8] + product[8:16] + product[16:24])
    y = jnp.exp(log_total) * jnp.where(row % 2 == 0, from_start[0], from_start[1])

    projected = lax.dot_general(
        normed, zx_ref[...], (((1,), (1,)), ((), ())), preferred_element_type=F32
    )
    gate = projected[:, 0:LANES]
    x_ref[6:14, :] = projected[:, LANES : 2 * LANES]
    x_conv = convolved(x_ref, 0, 12)
    drive = step * x_conv
    y = y + small_ref[17:18, :] * x_conv
    for lag in range(4):
        match = jnp.sum(c_conv * earlier(b_conv, lag), axis=1, keepdims=True)
        if lag == 0:
            y = y + drive * match
        else:
            decay = jnp.exp(log_total - earlier(log_total, lag))
            y = y + decay * earlier(drive, lag) * match
    gated = y * silu(gate)
    total = jnp.sum(gated * gated, axis=1, keepdims=True)
    parts = [p.astype(F32) for p in in_three(total)]
    aside = jnp.where(
        lane == HALF,
        parts[0],
        jnp.where(lane == HALF + 1, parts[1], jnp.where(lane == HALF + 2, parts[2], 0.0)),
    )
    weighted = (gated * small_ref[18:19, :]).astype(BF)

    last = jnp.where(row % 2 == 0, log_total[6:7], log_total[7:8])
    extra_ref[0:8, :] = jnp.exp(last - log_total) * drive
    extra_ref[8:16, :] = b_conv
    extra_ref[16:24, :] = jnp.exp(last)

    load_out.wait()
    moves = []
    for n in range(peers // 16):
        wide = jnp.dot(
            weighted, wo_ref[:, n * 1024 : (n + 1) * 1024], preferred_element_type=F32
        )
        for m in range(8):
            piece = wide[:, m * LANES : (m + 1) * LANES]
            tile_ref[16 * n + 2 * m] = jnp.where(low, piece, aside).astype(BF)
            tile_ref[16 * n + 2 * m + 1] = jnp.where(low, pltpu.roll(piece, HALF, 1), aside).astype(BF)
        part = pl.ds(16 * n, 16)
        moves.append(pltpu.make_async_copy(tile_ref.at[part], out_ref.at[part], sems.at[n]))
        moves[-1].start()
    for move in moves:
        move.wait()


def finish_kernel(incoming_ref, out_ref):
    total = incoming_ref[0].astype(F32)
    for p in range(1, incoming_ref.shape[0]):
        total = total + incoming_ref[p].astype(F32)
    squares = total[:, HALF : HALF + 1] + total[:, HALF + 1 : HALF + 2] + total[:, HALF + 2 : HALF + 3]
    scale = lax.rsqrt(squares * (1.0 / (HEADS * HEAD_DIM)) + EPS)
    out_ref[...] = (total[:, 0:HALF] * scale).astype(BF)


VM = pl.BlockSpec(memory_space=pltpu.VMEM)
SM = pl.BlockSpec(memory_space=pltpu.SMEM)
HB = pl.BlockSpec(memory_space=pltpu.HBM)


def in_hbm(array):
    return pltpu.with_memory_space_constraint(array, pltpu.HBM)


PARAMS = pltpu.CompilerParams(vmem_limit_bytes=VMEM_LIMIT)


def per_device(
    token_ids,
    decode_prompt,
    embedding,
    norm_gain,
    w_zx,
    w_bcdt,
    conv_x_weight,
    conv_x_bias,
    conv_bc_weight,
    conv_bc_bias,
    dt_bias,
    a_log,
    d_skip,
    gate_norm_gain,
    w_out,
    state_parts,
    seg_rate,
    x_tail,
    bc_tail,
):
    ctx, group, tp = (lax.axis_index(a) for a in ("ctx", "dp", "tp"))
    n_ctx, n_dp, n_tp = (lax.axis_size(a) for a in ("ctx", "dp", "tp"))
    peers = n_ctx * n_tp
    slots = state_parts.shape[1]
    heads = w_zx.shape[1]
    width = state_parts.shape[-1]
    steps = token_ids.shape[0]
    vocab_rows, features = embedding.shape
    model = norm_gain.shape[0]
    rows = steps * slots
    channels = heads * HEAD_DIM

    sent = pl.pallas_call(
        send_kernel,
        out_shape=jax.ShapeDtypeStruct((n_ctx, STATE_ROWS + SIDE_ROWS, width), BF),
        in_specs=[HB] * 5,
        out_specs=HB,
        scratch_shapes=[
            pltpu.SMEM(token_ids.shape, jnp.int32),
            pltpu.SMEM(decode_prompt.shape, jnp.int32),
            pltpu.SMEM(seg_rate.shape[1:], F32),
            pltpu.VMEM((features, vocab_rows), BF),
            pltpu.VMEM((slots, n_ctx, ONE_STATE, width), BF),
            pltpu.VMEM((n_dp * rows, LANES), jnp.int32),
            pltpu.VMEM((n_ctx * slots * heads, LANES), F32),
            pltpu.VMEM((n_ctx, RATE_ROWS, LANES), F32),
            pltpu.VMEM((n_ctx, SIDE_ROWS, LANES), BF),
            pltpu.SemaphoreType.DMA((6 + slots,)),
        ],
        compiler_params=PARAMS,
        name="send",
    )(
        in_hbm(token_ids),
        in_hbm(decode_prompt),
        in_hbm(seg_rate[0]),
        in_hbm(embedding.T),
        in_hbm(state_parts.reshape(slots, n_ctx, ONE_STATE, width)),
    )
    got = exchange(sent, "ctx")

    w_near = lax.all_gather(w_bcdt.T, "tp")
    own_columns = n_tp * w_bcdt.shape[1]
    w_near = w_near.reshape(own_columns, 2, n_ctx // 2, n_tp, features)
    w_near = lax.dynamic_index_in_dim(w_near, tp, 3, keepdims=False)
    w_near = jnp.swapaxes(w_near, 1, 2).reshape(own_columns, -1)
    w_near = jnp.concatenate([w_near, w_near], axis=0)
    w_near = jnp.pad(w_near, ((HALF, LANES - HALF - 2 * own_columns), (0, 0)))
    near_gain = norm_gain.reshape(2, n_ctx // 2, n_tp, features)
    near_gain = lax.dynamic_index_in_dim(near_gain, tp, 2, keepdims=False)
    near_gain = jnp.swapaxes(near_gain, 0, 1).reshape(n_ctx // 2, -1)
    tails = jnp.concatenate([x_tail.reshape(slots, 3, LANES), bc_tail.reshape(slots, 6, LANES)], axis=1)
    tails = jnp.pad(tails, ((0, 0), (0, TAIL_ROWS - tails.shape[1]), (0, 0)))
    wanted = decode_prompt.reshape(n_dp, slots) - group * slots
    prompt_for = jnp.any(wanted == 1, axis=1).astype(jnp.int32)
    own_slots = lax.dynamic_slice_in_dim(decode_prompt, group * slots, slots)

    def spread(values):
        return jnp.broadcast_to(values[:, None], (heads, HEAD_DIM)).reshape(1, channels)

    small = jnp.concatenate(
        [
            conv_x_weight.reshape(4, channels),
            conv_bc_weight[:, :width],
            conv_bc_weight[:, width:],
            conv_x_bias.reshape(1, channels),
            conv_bc_bias.reshape(2, width),
            spread(dt_bias),
            spread(a_log),
            spread(d_skip),
            gate_norm_gain.reshape(1, channels),
        ],
        axis=0,
    )
    small = jnp.pad(small, ((0, -small.shape[0] % 8), (0, 0)))

    got, w_near, near_gain = lax.optimization_barrier((got, w_near, near_gain))
    routed = pl.pallas_call(
        combine_kernel,
        out_shape=jax.ShapeDtypeStruct((n_dp, ONE_STATE + TAIL_ROWS + NEAR_ROWS, width), BF),
        in_specs=[SM, VM, VM],
        out_specs=HB,
        scratch_shapes=[
            pltpu.VMEM((slots, ONE_STATE + TAIL_ROWS, width), BF),
            pltpu.VMEM((n_dp, NEAR_ROWS, width), BF),
            pltpu.SemaphoreType.DMA((n_dp + 1,)),
        ],
        compiler_params=PARAMS,
        name="combine",
    )(prompt_for, got, tails)
    arrived = exchange(routed, "dp")

    place = jnp.stack([ctx % (n_ctx // 2), (ctx // (n_ctx // 2)) * HALF]).astype(jnp.int32)
    piece = pl.pallas_call(
        columns_kernel,
        out_shape=jax.ShapeDtypeStruct((peers, rows, LANES), BF),
        in_specs=[SM, VM, VM, VM],
        out_specs=HB,
        scratch_shapes=[
            pltpu.VMEM((NEAR_ROWS // 8, 8, LANES), F32),
            pltpu.VMEM((peers, rows, LANES), BF),
            pltpu.SemaphoreType.DMA(()),
        ],
        compiler_params=PARAMS,
        name="columns",
    )(place, arrived, near_gain, w_near)
    everyone = exchange(piece, BOTH)

    head_at = (tp * n_ctx + ctx) * heads
    place = jnp.concatenate(
        [own_slots // slots, ((LANES - head_at) % LANES)[None]]
    ).astype(jnp.int32)
    outgoing, extra = pl.pallas_call(
        decode_kernel,
        out_shape=(
            jax.ShapeDtypeStruct((peers, rows, LANES), BF),
            jax.ShapeDtypeStruct((24, LANES), F32),
        ),
        in_specs=[SM, VM, VM, VM, VM, VM, HB],
        out_specs=(HB, VM),
        scratch_shapes=[
            pltpu.VMEM((channels, model), BF),
            pltpu.VMEM((16, LANES), F32),
            pltpu.VMEM((16, LANES), F32),
            pltpu.VMEM((16, LANES), F32),
            pltpu.VMEM((peers, rows, LANES), BF),
            pltpu.SemaphoreType.DMA(()),
            pltpu.SemaphoreType.DMA((peers // 16,)),
        ],
        compiler_params=PARAMS,
        name="decode",
    )(
        place,
        everyone,
        arrived,
        norm_gain.reshape(model // LANES, LANES),
        small,
        w_zx.reshape(2 * channels, model),
        in_hbm(w_out.reshape(channels, model)),
    )
    incoming = exchange(outgoing, BOTH)

    start = jnp.stack(
        [
            lax.dynamic_index_in_dim(arrived[:, :ONE_STATE], place[s], 0, keepdims=False)
            for s in range(slots)
        ]
    )
    push = extra[0:8].reshape(steps, slots, channels)
    b_conv = extra[8:16].reshape(steps, slots, width)
    kept = extra[16:18]
    final = kept[:, :, None] * start.astype(F32) + jnp.einsum(
        "tpc,tpn->pcn", push, b_conv, precision=lax.Precision.HIGHEST
    )

    mixed = pl.pallas_call(
        finish_kernel,
        out_shape=jax.ShapeDtypeStruct((rows, features), BF),
        in_specs=[VM],
        out_specs=VM,
        compiler_params=PARAMS,
        name="finish",
    )(incoming)
    return (
        mixed.reshape(steps, slots, features),
        final.reshape(slots, heads, HEAD_DIM, width),
    )


def solution(mesh):
    return jax.shard_map(
        per_device,
        mesh=mesh,
        in_specs=(
            P(),
            P(),
            P("dp", ("ctx", "tp")),
            P(),
            P(None, ("tp", "ctx"), None, None),
            P(None, ("ctx", "tp")),
            P(None, ("tp", "ctx"), None),
            P(("tp", "ctx"), None),
            P(),
            P(),
            P(("tp", "ctx")),
            P(("tp", "ctx")),
            P(("tp", "ctx")),
            P(("tp", "ctx"), None),
            P(("tp", "ctx"), None, None),
            P("ctx", "dp", "tp", None, None),
            P("ctx", "dp", "tp"),
            P("dp", None, ("tp", "ctx"), None),
            P("dp", None, None),
        ),
        out_specs=(P(None, "dp", ("ctx", "tp")), P("dp", ("tp", "ctx"), None, None)),
        check_vma=False,
    )
```

```python
import jax
import jax.numpy as jnp
from jax import lax
from jax.experimental import pallas as pl
from jax.experimental.pallas import tpu as pltpu
from jax.sharding import PartitionSpec as P

HEADS = 128
HEAD_DIM = 64
EPS = 1e-05
BOTH = ("ctx", "tp")
BF = jnp.bfloat16
F32 = jnp.float32
LANES = 128
HALF = 64
VMEM_LIMIT = 12 * 1024 * 1024

STATE_ROWS = 256
RATE_ROWS = 16
TOKEN_ROWS = 32
SIDE_ROWS = RATE_ROWS + TOKEN_ROWS
ONE_STATE = 128
TAIL_ROWS = 16
NEAR_ROWS = 64


def exchange(pieces, axis):
    return lax.all_to_all(pieces, axis, 0, 0, tiled=True)


def in_three(values):
    first = values.astype(BF)
    rest = values - first.astype(F32)
    second = rest.astype(BF)
    third = (rest - second.astype(F32)).astype(BF)
    return first, second, third


def silu(v):
    return v / (1.0 + jnp.exp(-v))


def low_half(shape=(8, LANES)):
    return lax.broadcasted_iota(jnp.int32, shape, 1) < HALF


def send_kernel(
    tokens_hbm, prompt_hbm, rate_hbm, table_hbm, states_hbm, out_ref,
    tokens_ref, prompt_ref, rate_ref, table_ref, states_ref, token_ref, rows_ref, block_ref, side_ref, sems,
):
    pairs = [
        (tokens_hbm, tokens_ref),
        (prompt_hbm, prompt_ref),
        (rate_hbm, rate_ref),
        (table_hbm, table_ref),
        (states_hbm, states_ref),
    ]
    loads = [pltpu.make_async_copy(a, b, sems.at[n]) for n, (a, b) in enumerate(pairs)]
    for load in loads:
        load.start()
    group = lax.axis_index("dp")
    count = out_ref.shape[0]
    slots = states_ref.shape[0]
    heads = rate_ref.shape[1] // count
    steps = tokens_ref.shape[0]
    rows = steps * slots
    groups = prompt_ref.shape[0] // slots
    vocab_rows = table_ref.shape[1]
    first = group * vocab_rows
    loads[0].wait()
    loads[1].wait()
    for g in range(groups):
        for step in range(steps):
            for slot in range(slots):
                token = tokens_ref[step, prompt_ref[g * slots + slot]] - first
                at = g * rows + step * slots + slot
                token_ref[at : at + 1, :] = jnp.full((1, LANES), token, jnp.int32)
    loads[2].wait()
    for c in range(count):
        for p in range(slots):
            for h in range(heads):
                at = (c * slots + p) * heads + h
                rows_ref[at : at + 1, :] = jnp.full((1, LANES), rate_ref[p, c * heads + h], F32)
    each = slots * heads
    parts = [p.astype(F32) for p in in_three(rows_ref[...])]
    for c in range(count):
        for n, part in enumerate(parts):
            block_ref[c, n * each : (n + 1) * each, :] = part[c * each : (c + 1) * each]
        block_ref[c, 3 * each : RATE_ROWS, :] = jnp.zeros((RATE_ROWS - 3 * each, LANES), F32)
        side_ref[c, 0:RATE_ROWS, :] = block_ref[c].astype(BF)
    loads[4].wait()
    stores = []
    for p in range(slots):
        stores.append(
            pltpu.make_async_copy(
                states_ref.at[p], out_ref.at[:, p * ONE_STATE : (p + 1) * ONE_STATE, :], sems.at[5 + p]
            )
        )
        stores[-1].start()
    loads[3].wait()
    tokens = token_ref[:, 0:1]
    found = jnp.zeros((groups * rows, LANES), F32)
    whole = vocab_rows // LANES * LANES
    bounds = [*range(0, whole, 1024), whole, vocab_rows]
    for low_at, high_at in zip(bounds[:-1], bounds[1:]):
        ids = lax.broadcasted_iota(jnp.int32, (groups * rows, high_at - low_at), 1) + low_at
        hot = jnp.where(tokens == ids, 1.0, 0.0).astype(BF)
        table = table_ref[:, low_at:high_at]
        found = found + lax.dot_general(
            hot,
            jnp.concatenate([table, table], axis=0),
            (((1,), (1,)), ((), ())),
            preferred_element_type=F32,
        )
    low = low_half((TOKEN_ROWS, LANES))
    tile = jnp.where(low, found[0:TOKEN_ROWS], found[TOKEN_ROWS : 2 * TOKEN_ROWS]).astype(BF)
    for c in range(count):
        side_ref[c, RATE_ROWS:SIDE_ROWS, :] = tile
    stores.append(
        pltpu.make_async_copy(
            side_ref, out_ref.at[:, STATE_ROWS : STATE_ROWS + SIDE_ROWS, :], sems.at[5 + slots]
        )
    )
    stores[-1].start()
    for store in stores:
        store.wait()


def combine_kernel(chosen_ref, got_ref, tails_ref, out_ref, bundle_ref, near_ref, sems):
    count = got_ref.shape[0]
    groups = out_ref.shape[0]
    own_rows = ONE_STATE + TAIL_ROWS
    low = low_half((TOKEN_ROWS, LANES))
    at = STATE_ROWS + RATE_ROWS
    for pair in range(0, count // 2, 2):
        early, late = [], []
        for k in (pair, pair + 1):
            one = got_ref[k, at : at + TOKEN_ROWS, :].astype(F32)
            two = got_ref[count // 2 + k, at : at + TOKEN_ROWS, :].astype(F32)
            early.append(jnp.where(low, one, pltpu.roll(two, HALF, 1)))
            late.append(jnp.where(low, pltpu.roll(one, HALF, 1), two))
        for g in range(groups):
            source = early if g < groups // 2 else late
            r = (g % (groups // 2)) * 8
            both = jnp.concatenate([s[r : r + 8] for s in source], axis=0)
            near_ref[g, pair * 8 : pair * 8 + 16, :] = both.astype(BF)
    move_near = pltpu.make_async_copy(
        near_ref, out_ref.at[:, own_rows : own_rows + NEAR_ROWS, :], sems.at[groups]
    )
    move_near.start()
    rates = []
    for k in range(count):
        parts = got_ref[k, STATE_ROWS : STATE_ROWS + RATE_ROWS, :].astype(F32)
        rates.append(parts[0:4] + parts[4:8] + parts[8:12])
    weights = [None] * count
    later = jnp.zeros_like(rates[0])
    for k in reversed(range(count)):
        weights[k] = jnp.exp(-later)
        later = later + rates[k]
    for part in range(4):
        total = jnp.zeros((HEAD_DIM, LANES), F32)
        for k in range(count):
            own = got_ref[k, part * HEAD_DIM : (part + 1) * HEAD_DIM, :].astype(F32)
            total = total + (own * weights[k][part : part + 1]).astype(BF).astype(F32)
        at = (part % 2) * HEAD_DIM
        bundle_ref[part // 2, at : at + HEAD_DIM, :] = total.astype(BF)
    for p in range(bundle_ref.shape[0]):
        bundle_ref[p, ONE_STATE:own_rows, :] = tails_ref[p]
    moves = [
        pltpu.make_async_copy(
            bundle_ref.at[chosen_ref[g]], out_ref.at[g, 0:own_rows, :], sems.at[g]
        )
        for g in range(groups)
    ]
    for move in moves:
        move.start()
    for move in [*moves, move_near]:
        move.wait()


def columns_kernel(place_ref, arrived_ref, gain_ref, weight_ref, out_ref, near_ref, tile_ref, sem):
    groups = arrived_ref.shape[0]
    at = ONE_STATE + TAIL_ROWS
    total = arrived_ref[0, at : at + NEAR_ROWS, :].astype(F32)
    for g in range(1, groups):
        total = total + arrived_ref[g, at : at + NEAR_ROWS, :].astype(F32)
    pieces = []
    for k in range(NEAR_ROWS // 8):
        rows = total[k * 8 : (k + 1) * 8]
        near_ref[k] = rows
        pieces.append((rows * gain_ref[k : k + 1, :]).astype(BF))
    weighted = jnp.concatenate(pieces, axis=1)
    partial = lax.dot_general(
        weighted, weight_ref[...], (((1,), (1,)), ((), ())), preferred_element_type=F32
    )
    own = pltpu.roll(near_ref[place_ref[0]], place_ref[1], 1)
    lane = lax.broadcasted_iota(jnp.int32, (8, LANES), 1)
    first = partial.astype(BF).astype(F32)
    tile = jnp.where(lane < HALF, own, jnp.where(lane < HALF + 24, first, partial - first))
    tile_ref[...] = jnp.broadcast_to(tile.astype(BF)[None], tile_ref.shape)
    move = pltpu.make_async_copy(tile_ref, out_ref, sem)
    move.start()
    move.wait()


def decode_kernel(
    place_ref, everyone_ref, arrived_ref, gain_ref, small_ref, weights_ref, out_ref, extra_ref,
    x_ref, b_ref, c_ref, tile_ref, sems,
):
    peers = everyone_ref.shape[0]
    model = peers * HALF
    lane = lax.broadcasted_iota(jnp.int32, (8, LANES), 1)
    row = lax.broadcasted_iota(jnp.int32, (8, LANES), 0)
    low = lane < HALF

    tiles = [everyone_ref[p].astype(F32) for p in range(peers)]
    rows = [
        jnp.where(low, tiles[2 * n], pltpu.roll(tiles[2 * n + 1], HALF, 1)) for n in range(peers // 2)
    ]
    squares = rows[0] * rows[0]
    for r in rows[1:]:
        squares = squares + r * r
    inverse = lax.rsqrt(jnp.sum(squares, axis=1, keepdims=True) * (1.0 / model) + EPS)
    normed = jnp.concatenate(
        [(r * inverse * gain_ref[n : n + 1, :]).astype(BF) for n, r in enumerate(rows)], axis=1
    )

    columns = [jnp.zeros((8, LANES), F32) for _ in range(3)]
    for c in range(16):
        part = tiles[4 * c] + tiles[4 * c + 1] + tiles[4 * c + 2] + tiles[4 * c + 3]
        part = part + pltpu.roll(part, LANES - 24, 1)
        part = jnp.where((lane >= HALF) & (lane < HALF + 24), part, 0.0)
        first, offset = divmod(c * 24, LANES)
        part = pltpu.roll(part, (offset - HALF) % LANES, 1)
        if offset + 24 <= LANES:
            columns[first] = columns[first] + part
        else:
            columns[first] = columns[first] + jnp.where(lane >= offset, part, 0.0)
            columns[first + 1] = columns[first + 1] + jnp.where(lane < offset, part, 0.0)
    columns = [v * inverse for v in columns]

    for slot in range(2):
        tail = arrived_ref[place_ref[slot], ONE_STATE : ONE_STATE + TAIL_ROWS, :].astype(F32)
        for k in range(3):
            at = 2 * k + slot
            x_ref[at : at + 1, :] = tail[k : k + 1]
            b_ref[at : at + 1, :] = tail[3 + 2 * k : 4 + 2 * k]
            c_ref[at : at + 1, :] = tail[4 + 2 * k : 5 + 2 * k]
    b_ref[6:14, :] = columns[0]
    c_ref[6:14, :] = columns[1]

    def convolved(ref, weight_at, bias_at):
        total = ref[0:8, :] * small_ref[weight_at : weight_at + 1, :]
        for k in range(1, 4):
            total = total + ref[2 * k : 2 * k + 8, :] * small_ref[weight_at + k : weight_at + k + 1, :]
        return silu(total + small_ref[bias_at : bias_at + 1, :])

    b_conv = convolved(b_ref, 4, 13)
    c_conv = convolved(c_ref, 8, 14)

    raw = pltpu.roll(columns[2], place_ref[2], 1)
    raw = jnp.where(low, raw[:, 0:1], raw[:, 1:2]) + small_ref[15:16, :]
    step = jnp.maximum(raw, 0.0) + jnp.log1p(jnp.exp(-jnp.abs(raw)))
    log_retain = -step * jnp.exp(small_ref[16:17, :])

    def earlier(v, lag):
        return jnp.where(row >= 2 * lag, pltpu.roll(v, 2 * lag, 0), 0.0)

    log_total = log_retain
    for lag in range(1, 4):
        log_total = log_total + earlier(log_retain, lag)

    c_parts = jnp.concatenate([p.astype(F32) for p in in_three(c_conv)], axis=0).astype(BF)
    from_start = []
    for slot in range(2):
        state = arrived_ref[place_ref[slot], 0:ONE_STATE, :]
        product = lax.dot_general(
            c_parts, state, (((1,), (1,)), ((), ())), preferred_element_type=F32
        )
        from_start.append(product[0:8] + product[8:16] + product[16:24])
    y = jnp.exp(log_total) * jnp.where(row % 2 == 0, from_start[0], from_start[1])

    projected = lax.dot_general(
        normed, weights_ref[0 : 2 * LANES, :], (((1,), (1,)), ((), ())), preferred_element_type=F32
    )
    gate = projected[:, 0:LANES]
    x_ref[6:14, :] = projected[:, LANES : 2 * LANES]
    x_conv = convolved(x_ref, 0, 12)
    drive = step * x_conv
    y = y + small_ref[17:18, :] * x_conv
    for lag in range(4):
        match = jnp.sum(c_conv * earlier(b_conv, lag), axis=1, keepdims=True)
        if lag == 0:
            y = y + drive * match
        else:
            decay = jnp.exp(log_total - earlier(log_total, lag))
            y = y + decay * earlier(drive, lag) * match
    gated = y * silu(gate)
    total = jnp.sum(gated * gated, axis=1, keepdims=True)
    parts = [p.astype(F32) for p in in_three(total)]
    aside = jnp.where(
        lane == HALF,
        parts[0],
        jnp.where(lane == HALF + 1, parts[1], jnp.where(lane == HALF + 2, parts[2], 0.0)),
    )
    weighted = (gated * small_ref[18:19, :]).astype(BF)

    last = jnp.where(row % 2 == 0, log_total[6:7], log_total[7:8])
    extra_ref[0:8, :] = jnp.exp(last - log_total) * drive
    extra_ref[8:16, :] = b_conv
    extra_ref[16:24, :] = jnp.exp(last)

    moves = []
    for n in range(peers // 16):
        wide = jnp.dot(
            weighted, weights_ref[2 * LANES :, n * 1024 : (n + 1) * 1024], preferred_element_type=F32
        )
        for m in range(8):
            piece = wide[:, m * LANES : (m + 1) * LANES]
            tile_ref[16 * n + 2 * m] = jnp.where(low, piece, aside).astype(BF)
            tile_ref[16 * n + 2 * m + 1] = jnp.where(low, pltpu.roll(piece, HALF, 1), aside).astype(BF)
        part = pl.ds(16 * n, 16)
        moves.append(pltpu.make_async_copy(tile_ref.at[part], out_ref.at[part], sems.at[n]))
        moves[-1].start()
    for move in moves:
        move.wait()


def finish_kernel(incoming_ref, out_ref):
    total = incoming_ref[0].astype(F32)
    for p in range(1, incoming_ref.shape[0]):
        total = total + incoming_ref[p].astype(F32)
    squares = total[:, HALF : HALF + 1] + total[:, HALF + 1 : HALF + 2] + total[:, HALF + 2 : HALF + 3]
    scale = lax.rsqrt(squares * (1.0 / (HEADS * HEAD_DIM)) + EPS)
    out_ref[...] = (total[:, 0:HALF] * scale).astype(BF)


VM = pl.BlockSpec(memory_space=pltpu.VMEM)
SM = pl.BlockSpec(memory_space=pltpu.SMEM)
HB = pl.BlockSpec(memory_space=pltpu.HBM)


def in_hbm(array):
    return pltpu.with_memory_space_constraint(array, pltpu.HBM)


PARAMS = pltpu.CompilerParams(vmem_limit_bytes=VMEM_LIMIT)


def per_device(
    token_ids,
    decode_prompt,
    embedding,
    norm_gain,
    w_zx,
    w_bcdt,
    conv_x_weight,
    conv_x_bias,
    conv_bc_weight,
    conv_bc_bias,
    dt_bias,
    a_log,
    d_skip,
    gate_norm_gain,
    w_out,
    state_parts,
    seg_rate,
    x_tail,
    bc_tail,
):
    ctx, group, tp = (lax.axis_index(a) for a in ("ctx", "dp", "tp"))
    n_ctx, n_dp, n_tp = (lax.axis_size(a) for a in ("ctx", "dp", "tp"))
    peers = n_ctx * n_tp
    slots = state_parts.shape[1]
    heads = w_zx.shape[1]
    width = state_parts.shape[-1]
    steps = token_ids.shape[0]
    vocab_rows, features = embedding.shape
    model = norm_gain.shape[0]
    rows = steps * slots
    channels = heads * HEAD_DIM

    sent = pl.pallas_call(
        send_kernel,
        out_shape=jax.ShapeDtypeStruct((n_ctx, STATE_ROWS + SIDE_ROWS, width), BF),
        in_specs=[HB] * 5,
        out_specs=HB,
        scratch_shapes=[
            pltpu.SMEM(token_ids.shape, jnp.int32),
            pltpu.SMEM(decode_prompt.shape, jnp.int32),
            pltpu.SMEM(seg_rate.shape[1:], F32),
            pltpu.VMEM((features, vocab_rows), BF),
            pltpu.VMEM((slots, n_ctx, ONE_STATE, width), BF),
            pltpu.VMEM((n_dp * rows, LANES), jnp.int32),
            pltpu.VMEM((n_ctx * slots * heads, LANES), F32),
            pltpu.VMEM((n_ctx, RATE_ROWS, LANES), F32),
            pltpu.VMEM((n_ctx, SIDE_ROWS, LANES), BF),
            pltpu.SemaphoreType.DMA((6 + slots,)),
        ],
        compiler_params=PARAMS,
        name="send",
    )(
        in_hbm(token_ids),
        in_hbm(decode_prompt),
        in_hbm(seg_rate[0]),
        in_hbm(embedding.T),
        in_hbm(state_parts.reshape(slots, n_ctx, ONE_STATE, width)),
    )
    got = exchange(sent, "ctx")

    w_near = lax.all_gather(w_bcdt.T, "tp")
    own_columns = n_tp * w_bcdt.shape[1]
    w_near = w_near.reshape(own_columns, 2, n_ctx // 2, n_tp, features)
    w_near = lax.dynamic_index_in_dim(w_near, tp, 3, keepdims=False)
    w_near = jnp.swapaxes(w_near, 1, 2).reshape(own_columns, -1)
    w_near = jnp.concatenate([w_near, w_near], axis=0)
    w_near = jnp.pad(w_near, ((HALF, LANES - HALF - 2 * own_columns), (0, 0)))
    near_gain = norm_gain.reshape(2, n_ctx // 2, n_tp, features)
    near_gain = lax.dynamic_index_in_dim(near_gain, tp, 2, keepdims=False)
    near_gain = jnp.swapaxes(near_gain, 0, 1).reshape(n_ctx // 2, -1)
    tails = jnp.concatenate([x_tail.reshape(slots, 3, LANES), bc_tail.reshape(slots, 6, LANES)], axis=1)
    tails = jnp.pad(tails, ((0, 0), (0, TAIL_ROWS - tails.shape[1]), (0, 0)))
    wanted = decode_prompt.reshape(n_dp, slots) - group * slots
    prompt_for = jnp.any(wanted == 1, axis=1).astype(jnp.int32)
    own_slots = lax.dynamic_slice_in_dim(decode_prompt, group * slots, slots)

    def spread(values):
        return jnp.broadcast_to(values[:, None], (heads, HEAD_DIM)).reshape(1, channels)

    small = jnp.concatenate(
        [
            conv_x_weight.reshape(4, channels),
            conv_bc_weight[:, :width],
            conv_bc_weight[:, width:],
            conv_x_bias.reshape(1, channels),
            conv_bc_bias.reshape(2, width),
            spread(dt_bias),
            spread(a_log),
            spread(d_skip),
            gate_norm_gain.reshape(1, channels),
        ],
        axis=0,
    )
    small = jnp.pad(small, ((0, -small.shape[0] % 8), (0, 0)))

    got, w_near, near_gain = lax.optimization_barrier((got, w_near, near_gain))
    routed = pl.pallas_call(
        combine_kernel,
        out_shape=jax.ShapeDtypeStruct((n_dp, ONE_STATE + TAIL_ROWS + NEAR_ROWS, width), BF),
        in_specs=[SM, VM, VM],
        out_specs=HB,
        scratch_shapes=[
            pltpu.VMEM((slots, ONE_STATE + TAIL_ROWS, width), BF),
            pltpu.VMEM((n_dp, NEAR_ROWS, width), BF),
            pltpu.SemaphoreType.DMA((n_dp + 1,)),
        ],
        compiler_params=PARAMS,
        name="combine",
    )(prompt_for, got, tails)
    arrived = exchange(routed, "dp")

    place = jnp.stack([ctx % (n_ctx // 2), (ctx // (n_ctx // 2)) * HALF]).astype(jnp.int32)
    piece = pl.pallas_call(
        columns_kernel,
        out_shape=jax.ShapeDtypeStruct((peers, rows, LANES), BF),
        in_specs=[SM, VM, VM, VM],
        out_specs=HB,
        scratch_shapes=[
            pltpu.VMEM((NEAR_ROWS // 8, 8, LANES), F32),
            pltpu.VMEM((peers, rows, LANES), BF),
            pltpu.SemaphoreType.DMA(()),
        ],
        compiler_params=PARAMS,
        name="columns",
    )(place, arrived, near_gain, w_near)
    piece, w_zx, w_out = lax.optimization_barrier((piece, w_zx, w_out))
    everyone = exchange(piece, BOTH)
    weights = jnp.concatenate(
        [w_zx.reshape(2 * channels, model), w_out.reshape(channels, model)], axis=0
    )

    head_at = (tp * n_ctx + ctx) * heads
    place = jnp.concatenate(
        [own_slots // slots, ((LANES - head_at) % LANES)[None]]
    ).astype(jnp.int32)
    outgoing, extra = pl.pallas_call(
        decode_kernel,
        out_shape=(
            jax.ShapeDtypeStruct((peers, rows, LANES), BF),
            jax.ShapeDtypeStruct((24, LANES), F32),
        ),
        in_specs=[SM, VM, VM, VM, VM, VM],
        out_specs=(HB, VM),
        scratch_shapes=[
            pltpu.VMEM((16, LANES), F32),
            pltpu.VMEM((16, LANES), F32),
            pltpu.VMEM((16, LANES), F32),
            pltpu.VMEM((peers, rows, LANES), BF),
            pltpu.SemaphoreType.DMA((peers // 16,)),
        ],
        compiler_params=PARAMS,
        name="decode",
    )(
        place,
        everyone,
        arrived,
        norm_gain.reshape(model // LANES, LANES),
        small,
        weights,
    )
    incoming = exchange(outgoing, BOTH)

    start = jnp.stack(
        [
            lax.dynamic_index_in_dim(arrived[:, :ONE_STATE], place[s], 0, keepdims=False)
            for s in range(slots)
        ]
    )
    push = extra[0:8].reshape(steps, slots, channels)
    b_conv = extra[8:16].reshape(steps, slots, width)
    kept = extra[16:18]
    final = kept[:, :, None] * start.astype(F32) + jnp.einsum(
        "tpc,tpn->pcn", push, b_conv, precision=lax.Precision.HIGHEST
    )

    mixed = pl.pallas_call(
        finish_kernel,
        out_shape=jax.ShapeDtypeStruct((rows, features), BF),
        in_specs=[VM],
        out_specs=VM,
        compiler_params=PARAMS,
        name="finish",
    )(incoming)
    return (
        mixed.reshape(steps, slots, features),
        final.reshape(slots, heads, HEAD_DIM, width),
    )


def solution(mesh):
    return jax.shard_map(
        per_device,
        mesh=mesh,
        in_specs=(
            P(),
            P(),
            P("dp", ("ctx", "tp")),
            P(),
            P(None, ("tp", "ctx"), None, None),
            P(None, ("ctx", "tp")),
            P(None, ("tp", "ctx"), None),
            P(("tp", "ctx"), None),
            P(),
            P(),
            P(("tp", "ctx")),
            P(("tp", "ctx")),
            P(("tp", "ctx")),
            P(("tp", "ctx"), None),
            P(("tp", "ctx"), None, None),
            P("ctx", "dp", "tp", None, None),
            P("ctx", "dp", "tp"),
            P("dp", None, ("tp", "ctx"), None),
            P("dp", None, None),
        ),
        out_specs=(P(None, "dp", ("ctx", "tp")), P("dp", ("tp", "ctx"), None, None)),
        check_vma=False,
    )
```

```python
import jax
import jax.numpy as jnp
from jax import lax
from jax.experimental import pallas as pl
from jax.experimental.pallas import tpu as pltpu
from jax.sharding import PartitionSpec as P

HEADS = 128
HEAD_DIM = 64
EPS = 1e-05
BOTH = ("ctx", "tp")
BF = jnp.bfloat16
F32 = jnp.float32
LANES = 128
HALF = 64
VMEM_LIMIT = 12 * 1024 * 1024

STATE_ROWS = 256
RATE_ROWS = 16
TOKEN_ROWS = 32
SIDE_ROWS = RATE_ROWS + TOKEN_ROWS
ONE_STATE = 128
TAIL_ROWS = 16
NEAR_ROWS = 64


def exchange(pieces, axis):
    return lax.all_to_all(pieces, axis, 0, 0, tiled=True)


def in_three(values):
    first = values.astype(BF)
    rest = values - first.astype(F32)
    second = rest.astype(BF)
    third = (rest - second.astype(F32)).astype(BF)
    return first, second, third


def silu(v):
    return v / (1.0 + jnp.exp(-v))


def low_half(shape=(8, LANES)):
    return lax.broadcasted_iota(jnp.int32, shape, 1) < HALF


def send_kernel(
    tokens_hbm, prompt_hbm, rate_hbm, table_hbm, states_hbm, out_ref,
    tokens_ref, prompt_ref, rate_ref, table_ref, states_ref, token_ref, rows_ref, block_ref, side_ref, sems,
):
    pairs = [
        (tokens_hbm, tokens_ref),
        (prompt_hbm, prompt_ref),
        (rate_hbm, rate_ref),
        (table_hbm, table_ref),
        (states_hbm, states_ref),
    ]
    loads = [pltpu.make_async_copy(a, b, sems.at[n]) for n, (a, b) in enumerate(pairs)]
    for load in loads:
        load.start()
    group = lax.axis_index("dp")
    count = out_ref.shape[0]
    slots = states_ref.shape[0]
    heads = rate_ref.shape[1] // count
    steps = tokens_ref.shape[0]
    rows = steps * slots
    groups = prompt_ref.shape[0] // slots
    vocab_rows = table_ref.shape[1]
    first = group * vocab_rows
    loads[0].wait()
    loads[1].wait()
    for g in range(groups):
        for step in range(steps):
            for slot in range(slots):
                token = tokens_ref[step, prompt_ref[g * slots + slot]] - first
                at = g * rows + step * slots + slot
                token_ref[at : at + 1, :] = jnp.full((1, LANES), token, jnp.int32)
    loads[2].wait()
    for c in range(count):
        for p in range(slots):
            for h in range(heads):
                at = (c * slots + p) * heads + h
                rows_ref[at : at + 1, :] = jnp.full((1, LANES), rate_ref[p, c * heads + h], F32)
    each = slots * heads
    parts = [p.astype(F32) for p in in_three(rows_ref[...])]
    for c in range(count):
        for n, part in enumerate(parts):
            block_ref[c, n * each : (n + 1) * each, :] = part[c * each : (c + 1) * each]
        block_ref[c, 3 * each : RATE_ROWS, :] = jnp.zeros((RATE_ROWS - 3 * each, LANES), F32)
        side_ref[c, 0:RATE_ROWS, :] = block_ref[c].astype(BF)
    loads[4].wait()
    stores = []
    for p in range(slots):
        stores.append(
            pltpu.make_async_copy(
                states_ref.at[p], out_ref.at[:, p * ONE_STATE : (p + 1) * ONE_STATE, :], sems.at[5 + p]
            )
        )
        stores[-1].start()
    loads[3].wait()
    tokens = token_ref[:, 0:1]
    found = jnp.zeros((groups * rows, LANES), F32)
    whole = vocab_rows // LANES * LANES
    bounds = [*range(0, whole, 1024), whole, vocab_rows]
    for low_at, high_at in zip(bounds[:-1], bounds[1:]):
        ids = lax.broadcasted_iota(jnp.int32, (groups * rows, high_at - low_at), 1) + low_at
        hot = jnp.where(tokens == ids, 1.0, 0.0).astype(BF)
        table = table_ref[:, low_at:high_at]
        found = found + lax.dot_general(
            hot,
            jnp.concatenate([table, table], axis=0),
            (((1,), (1,)), ((), ())),
            preferred_element_type=F32,
        )
    low = low_half((TOKEN_ROWS, LANES))
    tile = jnp.where(low, found[0:TOKEN_ROWS], found[TOKEN_ROWS : 2 * TOKEN_ROWS]).astype(BF)
    for c in range(count):
        side_ref[c, RATE_ROWS:SIDE_ROWS, :] = tile
    stores.append(
        pltpu.make_async_copy(
            side_ref, out_ref.at[:, STATE_ROWS : STATE_ROWS + SIDE_ROWS, :], sems.at[5 + slots]
        )
    )
    stores[-1].start()
    for store in stores:
        store.wait()


def combine_kernel(chosen_ref, got_ref, tails_ref, out_ref, bundle_ref, near_ref, sems):
    count = got_ref.shape[0]
    groups = out_ref.shape[0]
    own_rows = ONE_STATE + TAIL_ROWS
    low = low_half((TOKEN_ROWS, LANES))
    at = STATE_ROWS + RATE_ROWS
    for pair in range(0, count // 2, 2):
        early, late = [], []
        for k in (pair, pair + 1):
            one = got_ref[k, at : at + TOKEN_ROWS, :].astype(F32)
            two = got_ref[count // 2 + k, at : at + TOKEN_ROWS, :].astype(F32)
            early.append(jnp.where(low, one, pltpu.roll(two, HALF, 1)))
            late.append(jnp.where(low, pltpu.roll(one, HALF, 1), two))
        for g in range(groups):
            source = early if g < groups // 2 else late
            r = (g % (groups // 2)) * 8
            both = jnp.concatenate([s[r : r + 8] for s in source], axis=0)
            near_ref[g, pair * 8 : pair * 8 + 16, :] = both.astype(BF)
    move_near = pltpu.make_async_copy(
        near_ref, out_ref.at[:, own_rows : own_rows + NEAR_ROWS, :], sems.at[groups]
    )
    move_near.start()
    rates = []
    for k in range(count):
        parts = got_ref[k, STATE_ROWS : STATE_ROWS + RATE_ROWS, :].astype(F32)
        rates.append(parts[0:4] + parts[4:8] + parts[8:12])
    weights = [None] * count
    later = jnp.zeros_like(rates[0])
    for k in reversed(range(count)):
        weights[k] = jnp.exp(-later)
        later = later + rates[k]
    for part in range(4):
        total = jnp.zeros((HEAD_DIM, LANES), F32)
        for k in range(count):
            own = got_ref[k, part * HEAD_DIM : (part + 1) * HEAD_DIM, :].astype(F32)
            total = total + (own * weights[k][part : part + 1]).astype(BF).astype(F32)
        at = (part % 2) * HEAD_DIM
        bundle_ref[part // 2, at : at + HEAD_DIM, :] = total.astype(BF)
    for p in range(bundle_ref.shape[0]):
        bundle_ref[p, ONE_STATE:own_rows, :] = tails_ref[p]
    moves = [
        pltpu.make_async_copy(
            bundle_ref.at[chosen_ref[g]], out_ref.at[g, 0:own_rows, :], sems.at[g]
        )
        for g in range(groups)
    ]
    for move in moves:
        move.start()
    for move in [*moves, move_near]:
        move.wait()


def columns_kernel(arrived_ref, gain_ref, weight_ref, out_ref, near_ref, tile_ref, sem):
    groups = arrived_ref.shape[0]
    at = ONE_STATE + TAIL_ROWS
    total = arrived_ref[0, at : at + NEAR_ROWS, :].astype(F32)
    for g in range(1, groups):
        total = total + arrived_ref[g, at : at + NEAR_ROWS, :].astype(F32)
    pieces = []
    for k in range(NEAR_ROWS // 8):
        rows = total[k * 8 : (k + 1) * 8]
        near_ref[k] = rows
        pieces.append((rows * gain_ref[k : k + 1, :]).astype(BF))
    weighted = jnp.concatenate(pieces, axis=1)
    partial = lax.dot_general(
        weighted, weight_ref[...], (((1,), (1,)), ((), ())), preferred_element_type=F32
    )
    ctx = lax.axis_index("ctx")
    half = lax.axis_size("ctx") // 2
    own = pltpu.roll(near_ref[lax.rem(ctx, half)], ctx // half * HALF, 1)
    lane = lax.broadcasted_iota(jnp.int32, (8, LANES), 1)
    first = partial.astype(BF).astype(F32)
    tile = jnp.where(lane < HALF, own, jnp.where(lane < HALF + 24, first, partial - first))
    tile_ref[...] = jnp.broadcast_to(tile.astype(BF)[None], tile_ref.shape)
    move = pltpu.make_async_copy(tile_ref, out_ref, sem)
    move.start()
    move.wait()


def decode_kernel(
    everyone_ref, weights_ref, arrived_hbm, prompt_hbm, gain_hbm, small_hbm, out_ref, extra_ref,
    arrived_ref, prompt_ref, gain_ref, small_ref, x_ref, b_ref, c_ref, tile_ref, load_sems, sems,
):
    pairs = [(prompt_hbm, prompt_ref), (gain_hbm, gain_ref), (small_hbm, small_ref)]
    loads = [pltpu.make_async_copy(a, b, load_sems.at[n]) for n, (a, b) in enumerate(pairs)]
    for load in loads:
        load.start()
    ctx, group, tp = (lax.axis_index(a) for a in ("ctx", "dp", "tp"))
    head_at = (tp * lax.axis_size("ctx") + ctx) * 2
    peers = everyone_ref.shape[0]
    model = peers * HALF
    lane = lax.broadcasted_iota(jnp.int32, (8, LANES), 1)
    row = lax.broadcasted_iota(jnp.int32, (8, LANES), 0)
    low = lane < HALF

    tiles = [everyone_ref[p].astype(F32) for p in range(peers)]
    rows = [
        jnp.where(low, tiles[2 * n], pltpu.roll(tiles[2 * n + 1], HALF, 1)) for n in range(peers // 2)
    ]
    squares = rows[0] * rows[0]
    for r in rows[1:]:
        squares = squares + r * r
    own_rows = arrived_ref.shape[1]
    loads[0].wait()
    for slot in range(2):
        holder = prompt_ref[group * 2 + slot] // 2
        loads.append(
            pltpu.make_async_copy(
                arrived_hbm.at[holder, 0:own_rows, :], arrived_ref.at[slot], load_sems.at[3 + slot]
            )
        )
        loads[-1].start()
    loads[1].wait()
    inverse = lax.rsqrt(jnp.sum(squares, axis=1, keepdims=True) * (1.0 / model) + EPS)
    normed = jnp.concatenate(
        [(r * inverse * gain_ref[n : n + 1, :]).astype(BF) for n, r in enumerate(rows)], axis=1
    )

    projected = lax.dot_general(
        normed, weights_ref[0 : 2 * LANES, :], (((1,), (1,)), ((), ())), preferred_element_type=F32
    )

    columns = [jnp.zeros((8, LANES), F32) for _ in range(3)]
    for c in range(16):
        part = tiles[4 * c] + tiles[4 * c + 1] + tiles[4 * c + 2] + tiles[4 * c + 3]
        part = part + pltpu.roll(part, LANES - 24, 1)
        part = jnp.where((lane >= HALF) & (lane < HALF + 24), part, 0.0)
        first, offset = divmod(c * 24, LANES)
        part = pltpu.roll(part, (offset - HALF) % LANES, 1)
        if offset + 24 <= LANES:
            columns[first] = columns[first] + part
        else:
            columns[first] = columns[first] + jnp.where(lane >= offset, part, 0.0)
            columns[first + 1] = columns[first + 1] + jnp.where(lane < offset, part, 0.0)
    columns = [v * inverse for v in columns]

    for load in loads[2:]:
        load.wait()

    for slot in range(2):
        tail = arrived_ref[slot, ONE_STATE : ONE_STATE + TAIL_ROWS, :].astype(F32)
        for k in range(3):
            at = 2 * k + slot
            x_ref[at : at + 1, :] = tail[k : k + 1]
            b_ref[at : at + 1, :] = tail[3 + 2 * k : 4 + 2 * k]
            c_ref[at : at + 1, :] = tail[4 + 2 * k : 5 + 2 * k]
    b_ref[6:14, :] = columns[0]
    c_ref[6:14, :] = columns[1]

    def convolved(ref, weight_at, bias_at):
        total = ref[0:8, :] * small_ref[weight_at : weight_at + 1, :]
        for k in range(1, 4):
            total = total + ref[2 * k : 2 * k + 8, :] * small_ref[weight_at + k : weight_at + k + 1, :]
        return silu(total + small_ref[bias_at : bias_at + 1, :])

    b_conv = convolved(b_ref, 4, 13)
    c_conv = convolved(c_ref, 8, 14)

    raw = pltpu.roll(columns[2], lax.rem(LANES - head_at, LANES), 1)
    raw = jnp.where(low, raw[:, 0:1], raw[:, 1:2]) + small_ref[15:16, :]
    step = jnp.maximum(raw, 0.0) + jnp.log1p(jnp.exp(-jnp.abs(raw)))
    log_retain = -step * jnp.exp(small_ref[16:17, :])

    def earlier(v, lag):
        return jnp.where(row >= 2 * lag, pltpu.roll(v, 2 * lag, 0), 0.0)

    log_total = log_retain
    for lag in range(1, 4):
        log_total = log_total + earlier(log_retain, lag)

    c_parts = jnp.concatenate([p.astype(F32) for p in in_three(c_conv)], axis=0).astype(BF)
    from_start = []
    for slot in range(2):
        state = arrived_ref[slot, 0:ONE_STATE, :]
        product = lax.dot_general(
            c_parts, state, (((1,), (1,)), ((), ())), preferred_element_type=F32
        )
        from_start.append(product[0:8] + product[8:16] + product[16:24])
    y = jnp.exp(log_total) * jnp.where(row % 2 == 0, from_start[0], from_start[1])

    gate = projected[:, 0:LANES]
    x_ref[6:14, :] = projected[:, LANES : 2 * LANES]
    x_conv = convolved(x_ref, 0, 12)
    drive = step * x_conv
    y = y + small_ref[17:18, :] * x_conv
    for lag in range(4):
        match = jnp.sum(c_conv * earlier(b_conv, lag), axis=1, keepdims=True)
        if lag == 0:
            y = y + drive * match
        else:
            decay = jnp.exp(log_total - earlier(log_total, lag))
            y = y + decay * earlier(drive, lag) * match
    gated = y * silu(gate)
    total = jnp.sum(gated * gated, axis=1, keepdims=True)
    parts = [p.astype(F32) for p in in_three(total)]
    aside = jnp.where(
        lane == HALF,
        parts[0],
        jnp.where(lane == HALF + 1, parts[1], jnp.where(lane == HALF + 2, parts[2], 0.0)),
    )
    weighted = (gated * small_ref[18:19, :]).astype(BF)

    last = jnp.where(row % 2 == 0, log_total[6:7], log_total[7:8])
    extra_ref[0:8, :] = jnp.exp(last - log_total) * drive
    extra_ref[8:16, :] = b_conv
    extra_ref[16:24, :] = jnp.exp(last)

    moves = []
    for n in range(peers // 16):
        wide = jnp.dot(
            weighted, weights_ref[2 * LANES :, n * 1024 : (n + 1) * 1024], preferred_element_type=F32
        )
        for m in range(8):
            piece = wide[:, m * LANES : (m + 1) * LANES]
            tile_ref[16 * n + 2 * m] = jnp.where(low, piece, aside).astype(BF)
            tile_ref[16 * n + 2 * m + 1] = jnp.where(low, pltpu.roll(piece, HALF, 1), aside).astype(BF)
        part = pl.ds(16 * n, 16)
        moves.append(pltpu.make_async_copy(tile_ref.at[part], out_ref.at[part], sems.at[n]))
        moves[-1].start()
    for move in moves:
        move.wait()


def finish_kernel(incoming_ref, out_ref):
    total = incoming_ref[0].astype(F32)
    for p in range(1, incoming_ref.shape[0]):
        total = total + incoming_ref[p].astype(F32)
    squares = total[:, HALF : HALF + 1] + total[:, HALF + 1 : HALF + 2] + total[:, HALF + 2 : HALF + 3]
    scale = lax.rsqrt(squares * (1.0 / (HEADS * HEAD_DIM)) + EPS)
    out_ref[...] = (total[:, 0:HALF] * scale).astype(BF)


VM = pl.BlockSpec(memory_space=pltpu.VMEM)
SM = pl.BlockSpec(memory_space=pltpu.SMEM)
HB = pl.BlockSpec(memory_space=pltpu.HBM)


def in_hbm(array):
    return pltpu.with_memory_space_constraint(array, pltpu.HBM)


PARAMS = pltpu.CompilerParams(vmem_limit_bytes=VMEM_LIMIT)


def per_device(
    token_ids,
    decode_prompt,
    embedding,
    norm_gain,
    w_zx,
    w_bcdt,
    conv_x_weight,
    conv_x_bias,
    conv_bc_weight,
    conv_bc_bias,
    dt_bias,
    a_log,
    d_skip,
    gate_norm_gain,
    w_out,
    state_parts,
    seg_rate,
    x_tail,
    bc_tail,
):
    ctx, group, tp = (lax.axis_index(a) for a in ("ctx", "dp", "tp"))
    n_ctx, n_dp, n_tp = (lax.axis_size(a) for a in ("ctx", "dp", "tp"))
    peers = n_ctx * n_tp
    slots = state_parts.shape[1]
    heads = w_zx.shape[1]
    width = state_parts.shape[-1]
    steps = token_ids.shape[0]
    vocab_rows, features = embedding.shape
    model = norm_gain.shape[0]
    rows = steps * slots
    channels = heads * HEAD_DIM

    sent = pl.pallas_call(
        send_kernel,
        out_shape=jax.ShapeDtypeStruct((n_ctx, STATE_ROWS + SIDE_ROWS, width), BF),
        in_specs=[HB] * 5,
        out_specs=HB,
        scratch_shapes=[
            pltpu.SMEM(token_ids.shape, jnp.int32),
            pltpu.SMEM(decode_prompt.shape, jnp.int32),
            pltpu.SMEM(seg_rate.shape[1:], F32),
            pltpu.VMEM((features, vocab_rows), BF),
            pltpu.VMEM((slots, n_ctx, ONE_STATE, width), BF),
            pltpu.VMEM((n_dp * rows, LANES), jnp.int32),
            pltpu.VMEM((n_ctx * slots * heads, LANES), F32),
            pltpu.VMEM((n_ctx, RATE_ROWS, LANES), F32),
            pltpu.VMEM((n_ctx, SIDE_ROWS, LANES), BF),
            pltpu.SemaphoreType.DMA((6 + slots,)),
        ],
        compiler_params=PARAMS,
        name="send",
    )(
        in_hbm(token_ids),
        in_hbm(decode_prompt),
        in_hbm(seg_rate[0]),
        in_hbm(embedding.T),
        in_hbm(state_parts.reshape(slots, n_ctx, ONE_STATE, width)),
    )
    got = exchange(sent, "ctx")

    w_near = lax.all_gather(w_bcdt.T, "tp")
    own_columns = n_tp * w_bcdt.shape[1]
    w_near = w_near.reshape(own_columns, 2, n_ctx // 2, n_tp, features)
    w_near = lax.dynamic_index_in_dim(w_near, tp, 3, keepdims=False)
    w_near = jnp.swapaxes(w_near, 1, 2).reshape(own_columns, -1)
    w_near = jnp.concatenate([w_near, w_near], axis=0)
    w_near = jnp.pad(w_near, ((HALF, LANES - HALF - 2 * own_columns), (0, 0)))
    near_gain = norm_gain.reshape(2, n_ctx // 2, n_tp, features)
    near_gain = lax.dynamic_index_in_dim(near_gain, tp, 2, keepdims=False)
    near_gain = jnp.swapaxes(near_gain, 0, 1).reshape(n_ctx // 2, -1)
    tails = jnp.concatenate([x_tail.reshape(slots, 3, LANES), bc_tail.reshape(slots, 6, LANES)], axis=1)
    tails = jnp.pad(tails, ((0, 0), (0, TAIL_ROWS - tails.shape[1]), (0, 0)))
    wanted = decode_prompt.reshape(n_dp, slots) - group * slots
    prompt_for = jnp.any(wanted == 1, axis=1).astype(jnp.int32)
    own_slots = lax.dynamic_slice_in_dim(decode_prompt, group * slots, slots)

    def spread(values):
        return jnp.broadcast_to(values[:, None], (heads, HEAD_DIM)).reshape(1, channels)

    small = jnp.concatenate(
        [
            conv_x_weight.reshape(4, channels),
            conv_bc_weight[:, :width],
            conv_bc_weight[:, width:],
            conv_x_bias.reshape(1, channels),
            conv_bc_bias.reshape(2, width),
            spread(dt_bias),
            spread(a_log),
            spread(d_skip),
            gate_norm_gain.reshape(1, channels),
        ],
        axis=0,
    )
    small = jnp.pad(small, ((0, -small.shape[0] % 8), (0, 0)))

    got, w_near, near_gain = lax.optimization_barrier((got, w_near, near_gain))
    routed = pl.pallas_call(
        combine_kernel,
        out_shape=jax.ShapeDtypeStruct((n_dp, ONE_STATE + TAIL_ROWS + NEAR_ROWS, width), BF),
        in_specs=[SM, VM, VM],
        out_specs=HB,
        scratch_shapes=[
            pltpu.VMEM((slots, ONE_STATE + TAIL_ROWS, width), BF),
            pltpu.VMEM((n_dp, NEAR_ROWS, width), BF),
            pltpu.SemaphoreType.DMA((n_dp + 1,)),
        ],
        compiler_params=PARAMS,
        name="combine",
    )(prompt_for, got, tails)
    arrived = exchange(routed, "dp")

    piece = pl.pallas_call(
        columns_kernel,
        out_shape=jax.ShapeDtypeStruct((peers, rows, LANES), BF),
        in_specs=[VM, VM, VM],
        out_specs=HB,
        scratch_shapes=[
            pltpu.VMEM((NEAR_ROWS // 8, 8, LANES), F32),
            pltpu.VMEM((peers, rows, LANES), BF),
            pltpu.SemaphoreType.DMA(()),
        ],
        compiler_params=PARAMS,
        name="columns",
    )(arrived, near_gain, w_near)
    piece, w_zx, w_out = lax.optimization_barrier((piece, w_zx, w_out))
    everyone = exchange(piece, BOTH)
    weights = jnp.concatenate(
        [w_zx.reshape(2 * channels, model), w_out.reshape(channels, model)], axis=0
    )

    outgoing, extra = pl.pallas_call(
        decode_kernel,
        out_shape=(
            jax.ShapeDtypeStruct((peers, rows, LANES), BF),
            jax.ShapeDtypeStruct((24, LANES), F32),
        ),
        in_specs=[VM, VM, HB, HB, HB, HB],
        out_specs=(HB, VM),
        scratch_shapes=[
            pltpu.VMEM((slots, ONE_STATE + TAIL_ROWS, width), BF),
            pltpu.SMEM(decode_prompt.shape, jnp.int32),
            pltpu.VMEM((model // LANES, LANES), F32),
            pltpu.VMEM(small.shape, F32),
            pltpu.VMEM((16, LANES), F32),
            pltpu.VMEM((16, LANES), F32),
            pltpu.VMEM((16, LANES), F32),
            pltpu.VMEM((peers, rows, LANES), BF),
            pltpu.SemaphoreType.DMA((3 + slots,)),
            pltpu.SemaphoreType.DMA((peers // 16,)),
        ],
        compiler_params=PARAMS,
        name="decode",
    )(
        everyone,
        weights,
        in_hbm(arrived),
        in_hbm(decode_prompt),
        in_hbm(norm_gain.reshape(model // LANES, LANES)),
        in_hbm(small),
    )
    incoming = exchange(outgoing, BOTH)

    start = jnp.stack(
        [
            lax.dynamic_index_in_dim(arrived[:, :ONE_STATE], own_slots[s] // slots, 0, keepdims=False)
            for s in range(slots)
        ]
    )
    push = extra[0:8].reshape(steps, slots, channels)
    b_conv = extra[8:16].reshape(steps, slots, width)
    kept = extra[16:18]
    final = kept[:, :, None] * start.astype(F32) + jnp.einsum(
        "tpc,tpn->pcn", push, b_conv, precision=lax.Precision.HIGHEST
    )

    mixed = pl.pallas_call(
        finish_kernel,
        out_shape=jax.ShapeDtypeStruct((rows, features), BF),
        in_specs=[VM],
        out_specs=VM,
        compiler_params=PARAMS,
        name="finish",
    )(incoming)
    return (
        mixed.reshape(steps, slots, features),
        final.reshape(slots, heads, HEAD_DIM, width),
    )


def solution(mesh):
    return jax.shard_map(
        per_device,
        mesh=mesh,
        in_specs=(
            P(),
            P(),
            P("dp", ("ctx", "tp")),
            P(),
            P(None, ("tp", "ctx"), None, None),
            P(None, ("ctx", "tp")),
            P(None, ("tp", "ctx"), None),
            P(("tp", "ctx"), None),
            P(),
            P(),
            P(("tp", "ctx")),
            P(("tp", "ctx")),
            P(("tp", "ctx")),
            P(("tp", "ctx"), None),
            P(("tp", "ctx"), None, None),
            P("ctx", "dp", "tp", None, None),
            P("ctx", "dp", "tp"),
            P("dp", None, ("tp", "ctx"), None),
            P("dp", None, None),
        ),
        out_specs=(P(None, "dp", ("ctx", "tp")), P("dp", ("tp", "ctx"), None, None)),
        check_vma=False,
    )
```

```python
import jax
import jax.numpy as jnp
from jax import lax
from jax.experimental import pallas as pl
from jax.experimental.pallas import tpu as pltpu
from jax.sharding import PartitionSpec as P

HEADS = 128
HEAD_DIM = 64
EPS = 1e-05
BOTH = ("ctx", "tp")
BF = jnp.bfloat16
F32 = jnp.float32
LANES = 128
HALF = 64
VMEM_LIMIT = 12 * 1024 * 1024

STATE_ROWS = 256
RATE_ROWS = 16
TOKEN_ROWS = 32
SIDE_ROWS = RATE_ROWS + TOKEN_ROWS
ONE_STATE = 128
TAIL_ROWS = 16
NEAR_ROWS = 64


def exchange(pieces, axis):
    return lax.all_to_all(pieces, axis, 0, 0, tiled=True)


def in_three(values):
    first = values.astype(BF)
    rest = values - first.astype(F32)
    second = rest.astype(BF)
    third = (rest - second.astype(F32)).astype(BF)
    return first, second, third


def silu(v):
    return v / (1.0 + jnp.exp(-v))


def low_half(shape=(8, LANES)):
    return lax.broadcasted_iota(jnp.int32, shape, 1) < HALF


def send_kernel(
    tokens_hbm, prompt_hbm, rate_hbm, table_hbm, states_hbm, out_ref,
    tokens_ref, prompt_ref, rate_ref, table_ref, states_ref, token_ref, rows_ref, block_ref, side_ref, sems,
):
    pairs = [
        (tokens_hbm, tokens_ref),
        (prompt_hbm, prompt_ref),
        (rate_hbm, rate_ref),
        (table_hbm, table_ref),
        (states_hbm, states_ref),
    ]
    loads = [pltpu.make_async_copy(a, b, sems.at[n]) for n, (a, b) in enumerate(pairs)]
    for load in loads:
        load.start()
    group = lax.axis_index("dp")
    count = out_ref.shape[0]
    slots = states_ref.shape[0]
    heads = rate_ref.shape[1] // count
    steps = tokens_ref.shape[0]
    rows = steps * slots
    groups = prompt_ref.shape[0] // slots
    vocab_rows = table_ref.shape[1]
    first = group * vocab_rows
    loads[0].wait()
    loads[1].wait()
    for g in range(groups):
        for step in range(steps):
            for slot in range(slots):
                token = tokens_ref[step, prompt_ref[g * slots + slot]] - first
                at = g * rows + step * slots + slot
                token_ref[at : at + 1, :] = jnp.full((1, LANES), token, jnp.int32)
    loads[2].wait()
    for c in range(count):
        for p in range(slots):
            for h in range(heads):
                at = (c * slots + p) * heads + h
                rows_ref[at : at + 1, :] = jnp.full((1, LANES), rate_ref[p, c * heads + h], F32)
    each = slots * heads
    parts = [p.astype(F32) for p in in_three(rows_ref[...])]
    for c in range(count):
        for n, part in enumerate(parts):
            block_ref[c, n * each : (n + 1) * each, :] = part[c * each : (c + 1) * each]
        block_ref[c, 3 * each : RATE_ROWS, :] = jnp.zeros((RATE_ROWS - 3 * each, LANES), F32)
        side_ref[c, 0:RATE_ROWS, :] = block_ref[c].astype(BF)
    loads[4].wait()
    stores = []
    for p in range(slots):
        stores.append(
            pltpu.make_async_copy(
                states_ref.at[p], out_ref.at[:, p * ONE_STATE : (p + 1) * ONE_STATE, :], sems.at[5 + p]
            )
        )
        stores[-1].start()
    loads[3].wait()
    tokens = token_ref[:, 0:1]
    found = jnp.zeros((groups * rows, LANES), F32)
    whole = vocab_rows // LANES * LANES
    bounds = [*range(0, whole, 1024), whole, vocab_rows]
    for low_at, high_at in zip(bounds[:-1], bounds[1:]):
        ids = lax.broadcasted_iota(jnp.int32, (groups * rows, high_at - low_at), 1) + low_at
        hot = jnp.where(tokens == ids, 1.0, 0.0).astype(BF)
        table = table_ref[:, low_at:high_at]
        found = found + lax.dot_general(
            hot,
            jnp.concatenate([table, table], axis=0),
            (((1,), (1,)), ((), ())),
            preferred_element_type=F32,
        )
    low = low_half((TOKEN_ROWS, LANES))
    tile = jnp.where(low, found[0:TOKEN_ROWS], found[TOKEN_ROWS : 2 * TOKEN_ROWS]).astype(BF)
    for c in range(count):
        side_ref[c, RATE_ROWS:SIDE_ROWS, :] = tile
    stores.append(
        pltpu.make_async_copy(
            side_ref, out_ref.at[:, STATE_ROWS : STATE_ROWS + SIDE_ROWS, :], sems.at[5 + slots]
        )
    )
    stores[-1].start()
    for store in stores:
        store.wait()


def combine_kernel(chosen_ref, got_ref, tails_ref, out_ref, bundle_ref, near_ref, sems):
    count = got_ref.shape[0]
    groups = out_ref.shape[0]
    own_rows = ONE_STATE + TAIL_ROWS
    low = low_half((TOKEN_ROWS, LANES))
    at = STATE_ROWS + RATE_ROWS
    for pair in range(0, count // 2, 2):
        early, late = [], []
        for k in (pair, pair + 1):
            one = got_ref[k, at : at + TOKEN_ROWS, :].astype(F32)
            two = got_ref[count // 2 + k, at : at + TOKEN_ROWS, :].astype(F32)
            early.append(jnp.where(low, one, pltpu.roll(two, HALF, 1)))
            late.append(jnp.where(low, pltpu.roll(one, HALF, 1), two))
        for g in range(groups):
            source = early if g < groups // 2 else late
            r = (g % (groups // 2)) * 8
            both = jnp.concatenate([s[r : r + 8] for s in source], axis=0)
            near_ref[g, pair * 8 : pair * 8 + 16, :] = both.astype(BF)
    move_near = pltpu.make_async_copy(
        near_ref, out_ref.at[:, own_rows : own_rows + NEAR_ROWS, :], sems.at[groups]
    )
    move_near.start()
    rates = []
    for k in range(count):
        parts = got_ref[k, STATE_ROWS : STATE_ROWS + RATE_ROWS, :].astype(F32)
        rates.append(parts[0:4] + parts[4:8] + parts[8:12])
    weights = [None] * count
    later = jnp.zeros_like(rates[0])
    for k in reversed(range(count)):
        weights[k] = jnp.exp(-later)
        later = later + rates[k]
    for part in range(4):
        total = jnp.zeros((HEAD_DIM, LANES), F32)
        for k in range(count):
            own = got_ref[k, part * HEAD_DIM : (part + 1) * HEAD_DIM, :].astype(F32)
            total = total + (own * weights[k][part : part + 1]).astype(BF).astype(F32)
        at = (part % 2) * HEAD_DIM
        bundle_ref[part // 2, at : at + HEAD_DIM, :] = total.astype(BF)
    for p in range(bundle_ref.shape[0]):
        bundle_ref[p, ONE_STATE:own_rows, :] = tails_ref[p]
    moves = [
        pltpu.make_async_copy(
            bundle_ref.at[chosen_ref[g]], out_ref.at[g, 0:own_rows, :], sems.at[g]
        )
        for g in range(groups)
    ]
    for move in moves:
        move.start()
    for move in [*moves, move_near]:
        move.wait()


def columns_kernel(arrived_ref, gain_ref, weight_ref, out_ref, near_ref, tile_ref, sem):
    groups = arrived_ref.shape[0]
    at = ONE_STATE + TAIL_ROWS
    total = arrived_ref[0, at : at + NEAR_ROWS, :].astype(F32)
    for g in range(1, groups):
        total = total + arrived_ref[g, at : at + NEAR_ROWS, :].astype(F32)
    pieces = []
    for k in range(NEAR_ROWS // 8):
        rows = total[k * 8 : (k + 1) * 8]
        near_ref[k] = rows
        pieces.append((rows * gain_ref[k : k + 1, :]).astype(BF))
    weighted = jnp.concatenate(pieces, axis=1)
    partial = lax.dot_general(
        weighted, weight_ref[...], (((1,), (1,)), ((), ())), preferred_element_type=F32
    )
    ctx = lax.axis_index("ctx")
    half = lax.axis_size("ctx") // 2
    own = pltpu.roll(near_ref[lax.rem(ctx, half)], ctx // half * HALF, 1)
    lane = lax.broadcasted_iota(jnp.int32, (8, LANES), 1)
    first = partial.astype(BF).astype(F32)
    tile = jnp.where(lane < HALF, own, jnp.where(lane < HALF + 24, first, partial - first))
    tile_ref[...] = jnp.broadcast_to(tile.astype(BF)[None], tile_ref.shape)
    move = pltpu.make_async_copy(tile_ref, out_ref, sem)
    move.start()
    move.wait()


def decode_kernel(
    everyone_ref, weights_ref, arrived_hbm, prompt_hbm, gain_hbm, small_hbm, out_ref, extra_ref,
    arrived_ref, prompt_ref, gain_ref, small_ref, x_ref, b_ref, c_ref, tile_ref, load_sems, sems,
):
    pairs = [(prompt_hbm, prompt_ref), (gain_hbm, gain_ref), (small_hbm, small_ref)]
    loads = [pltpu.make_async_copy(a, b, load_sems.at[n]) for n, (a, b) in enumerate(pairs)]
    for load in loads:
        load.start()
    ctx, group, tp = (lax.axis_index(a) for a in ("ctx", "dp", "tp"))
    head_at = (tp * lax.axis_size("ctx") + ctx) * 2
    peers = everyone_ref.shape[0]
    model = peers * HALF
    lane = lax.broadcasted_iota(jnp.int32, (8, LANES), 1)
    row = lax.broadcasted_iota(jnp.int32, (8, LANES), 0)
    low = lane < HALF

    tiles = [everyone_ref[p].astype(F32) for p in range(peers)]
    rows = [
        jnp.where(low, tiles[2 * n], pltpu.roll(tiles[2 * n + 1], HALF, 1)) for n in range(peers // 2)
    ]
    squares = rows[0] * rows[0]
    for r in rows[1:]:
        squares = squares + r * r
    own_rows = arrived_ref.shape[1]
    loads[0].wait()
    for slot in range(2):
        holder = prompt_ref[group * 2 + slot] // 2
        loads.append(
            pltpu.make_async_copy(
                arrived_hbm.at[holder, 0:own_rows, :], arrived_ref.at[slot], load_sems.at[3 + slot]
            )
        )
        loads[-1].start()
    loads[1].wait()
    inverse = lax.rsqrt(jnp.sum(squares, axis=1, keepdims=True) * (1.0 / model) + EPS)
    normed = jnp.concatenate(
        [(r * inverse * gain_ref[n : n + 1, :]).astype(BF) for n, r in enumerate(rows)], axis=1
    )

    projected = lax.dot_general(
        normed, weights_ref[0 : 2 * LANES, :], (((1,), (1,)), ((), ())), preferred_element_type=F32
    )

    columns = [jnp.zeros((8, LANES), F32) for _ in range(3)]
    for c in range(16):
        part = tiles[4 * c] + tiles[4 * c + 1] + tiles[4 * c + 2] + tiles[4 * c + 3]
        part = part + pltpu.roll(part, LANES - 24, 1)
        part = jnp.where((lane >= HALF) & (lane < HALF + 24), part, 0.0)
        first, offset = divmod(c * 24, LANES)
        part = pltpu.roll(part, (offset - HALF) % LANES, 1)
        if offset + 24 <= LANES:
            columns[first] = columns[first] + part
        else:
            columns[first] = columns[first] + jnp.where(lane >= offset, part, 0.0)
            columns[first + 1] = columns[first + 1] + jnp.where(lane < offset, part, 0.0)
    columns = [v * inverse for v in columns]

    for load in loads[2:]:
        load.wait()

    for slot in range(2):
        tail = arrived_ref[slot, ONE_STATE : ONE_STATE + TAIL_ROWS, :].astype(F32)
        for k in range(3):
            at = 2 * k + slot
            x_ref[at : at + 1, :] = tail[k : k + 1]
            b_ref[at : at + 1, :] = tail[3 + 2 * k : 4 + 2 * k]
            c_ref[at : at + 1, :] = tail[4 + 2 * k : 5 + 2 * k]
    b_ref[6:14, :] = columns[0]
    c_ref[6:14, :] = columns[1]

    def convolved(ref, weight_at, bias_at):
        total = ref[0:8, :] * small_ref[weight_at : weight_at + 1, :]
        for k in range(1, 4):
            total = total + ref[2 * k : 2 * k + 8, :] * small_ref[weight_at + k : weight_at + k + 1, :]
        return silu(total + small_ref[bias_at : bias_at + 1, :])

    b_conv = convolved(b_ref, 4, 13)
    c_conv = convolved(c_ref, 8, 14)

    raw = pltpu.roll(columns[2], lax.rem(LANES - head_at, LANES), 1)
    raw = jnp.where(low, raw[:, 0:1], raw[:, 1:2]) + small_ref[15:16, :]
    step = jnp.maximum(raw, 0.0) + jnp.log1p(jnp.exp(-jnp.abs(raw)))
    log_retain = -step * jnp.exp(small_ref[16:17, :])

    def earlier(v, lag):
        return jnp.where(row >= 2 * lag, pltpu.roll(v, 2 * lag, 0), 0.0)

    log_total = log_retain
    for lag in range(1, 4):
        log_total = log_total + earlier(log_retain, lag)

    c_parts = jnp.concatenate([p.astype(F32) for p in in_three(c_conv)], axis=0).astype(BF)
    from_start = []
    for slot in range(2):
        state = arrived_ref[slot, 0:ONE_STATE, :]
        product = lax.dot_general(
            c_parts, state, (((1,), (1,)), ((), ())), preferred_element_type=F32
        )
        from_start.append(product[0:8] + product[8:16] + product[16:24])
    y = jnp.exp(log_total) * jnp.where(row % 2 == 0, from_start[0], from_start[1])

    gate = projected[:, 0:LANES]
    x_ref[6:14, :] = projected[:, LANES : 2 * LANES]
    x_conv = convolved(x_ref, 0, 12)
    drive = step * x_conv
    y = y + small_ref[17:18, :] * x_conv
    for lag in range(4):
        match = jnp.sum(c_conv * earlier(b_conv, lag), axis=1, keepdims=True)
        if lag == 0:
            y = y + drive * match
        else:
            decay = jnp.exp(log_total - earlier(log_total, lag))
            y = y + decay * earlier(drive, lag) * match
    gated = y * silu(gate)
    total = jnp.sum(gated * gated, axis=1, keepdims=True)
    parts = [p.astype(F32) for p in in_three(total)]
    aside = jnp.where(
        lane == HALF,
        parts[0],
        jnp.where(lane == HALF + 1, parts[1], jnp.where(lane == HALF + 2, parts[2], 0.0)),
    )
    weighted = (gated * small_ref[18:19, :]).astype(BF)

    last = jnp.where(row % 2 == 0, log_total[6:7], log_total[7:8])
    extra_ref[0:8, :] = jnp.exp(last - log_total) * drive
    extra_ref[8:16, :] = b_conv
    extra_ref[16:24, :] = jnp.exp(last)

    moves = []
    for n in range(peers // 16):
        wide = jnp.dot(
            weighted, weights_ref[2 * LANES :, n * 1024 : (n + 1) * 1024], preferred_element_type=F32
        )
        for m in range(8):
            piece = wide[:, m * LANES : (m + 1) * LANES]
            tile_ref[16 * n + 2 * m] = jnp.where(low, piece, aside).astype(BF)
            tile_ref[16 * n + 2 * m + 1] = jnp.where(low, pltpu.roll(piece, HALF, 1), aside).astype(BF)
        part = pl.ds(16 * n, 16)
        moves.append(pltpu.make_async_copy(tile_ref.at[part], out_ref.at[part], sems.at[n]))
        moves[-1].start()
    for move in moves:
        move.wait()


def finish_kernel(incoming_ref, out_ref):
    total = incoming_ref[0].astype(F32)
    for p in range(1, incoming_ref.shape[0]):
        total = total + incoming_ref[p].astype(F32)
    squares = total[:, HALF : HALF + 1] + total[:, HALF + 1 : HALF + 2] + total[:, HALF + 2 : HALF + 3]
    scale = lax.rsqrt(squares * (1.0 / (HEADS * HEAD_DIM)) + EPS)
    out_ref[...] = (total[:, 0:HALF] * scale).astype(BF)


VM = pl.BlockSpec(memory_space=pltpu.VMEM)
SM = pl.BlockSpec(memory_space=pltpu.SMEM)
HB = pl.BlockSpec(memory_space=pltpu.HBM)


def in_hbm(array):
    return pltpu.with_memory_space_constraint(array, pltpu.HBM)


PARAMS = pltpu.CompilerParams(vmem_limit_bytes=VMEM_LIMIT)


def per_device(
    token_ids,
    decode_prompt,
    embedding,
    norm_gain,
    w_zx,
    w_bcdt,
    conv_x_weight,
    conv_x_bias,
    conv_bc_weight,
    conv_bc_bias,
    dt_bias,
    a_log,
    d_skip,
    gate_norm_gain,
    w_out,
    state_parts,
    seg_rate,
    x_tail,
    bc_tail,
):
    ctx, group, tp = (lax.axis_index(a) for a in ("ctx", "dp", "tp"))
    n_ctx, n_dp, n_tp = (lax.axis_size(a) for a in ("ctx", "dp", "tp"))
    peers = n_ctx * n_tp
    slots = state_parts.shape[1]
    heads = w_zx.shape[1]
    width = state_parts.shape[-1]
    steps = token_ids.shape[0]
    vocab_rows, features = embedding.shape
    model = norm_gain.shape[0]
    rows = steps * slots
    channels = heads * HEAD_DIM

    sent = pl.pallas_call(
        send_kernel,
        out_shape=jax.ShapeDtypeStruct((n_ctx, STATE_ROWS + SIDE_ROWS, width), BF),
        in_specs=[HB] * 5,
        out_specs=HB,
        scratch_shapes=[
            pltpu.SMEM(token_ids.shape, jnp.int32),
            pltpu.SMEM(decode_prompt.shape, jnp.int32),
            pltpu.SMEM(seg_rate.shape[1:], F32),
            pltpu.VMEM((features, vocab_rows), BF),
            pltpu.VMEM((slots, n_ctx, ONE_STATE, width), BF),
            pltpu.VMEM((n_dp * rows, LANES), jnp.int32),
            pltpu.VMEM((n_ctx * slots * heads, LANES), F32),
            pltpu.VMEM((n_ctx, RATE_ROWS, LANES), F32),
            pltpu.VMEM((n_ctx, SIDE_ROWS, LANES), BF),
            pltpu.SemaphoreType.DMA((6 + slots,)),
        ],
        compiler_params=PARAMS,
        name="send",
    )(
        in_hbm(token_ids),
        in_hbm(decode_prompt),
        in_hbm(seg_rate[0]),
        in_hbm(embedding.T),
        in_hbm(state_parts.reshape(slots, n_ctx, ONE_STATE, width)),
    )
    got = exchange(sent, "ctx")

    near_gain = norm_gain.reshape(2, n_ctx // 2, n_tp, features)
    near_gain = lax.dynamic_index_in_dim(near_gain, tp, 2, keepdims=False)
    near_gain = jnp.swapaxes(near_gain, 0, 1).reshape(n_ctx // 2, -1)
    tails = jnp.concatenate([x_tail.reshape(slots, 3, LANES), bc_tail.reshape(slots, 6, LANES)], axis=1)
    tails = jnp.pad(tails, ((0, 0), (0, TAIL_ROWS - tails.shape[1]), (0, 0)))
    wanted = decode_prompt.reshape(n_dp, slots) - group * slots
    prompt_for = jnp.any(wanted == 1, axis=1).astype(jnp.int32)
    own_slots = lax.dynamic_slice_in_dim(decode_prompt, group * slots, slots)

    def spread(values):
        return jnp.broadcast_to(values[:, None], (heads, HEAD_DIM)).reshape(1, channels)

    small = jnp.concatenate(
        [
            conv_x_weight.reshape(4, channels),
            conv_bc_weight[:, :width],
            conv_bc_weight[:, width:],
            conv_x_bias.reshape(1, channels),
            conv_bc_bias.reshape(2, width),
            spread(dt_bias),
            spread(a_log),
            spread(d_skip),
            gate_norm_gain.reshape(1, channels),
        ],
        axis=0,
    )
    small = jnp.pad(small, ((0, -small.shape[0] % 8), (0, 0)))

    got, near_gain, small = lax.optimization_barrier((got, near_gain, small))
    routed = pl.pallas_call(
        combine_kernel,
        out_shape=jax.ShapeDtypeStruct((n_dp, ONE_STATE + TAIL_ROWS + NEAR_ROWS, width), BF),
        in_specs=[SM, VM, VM],
        out_specs=HB,
        scratch_shapes=[
            pltpu.VMEM((slots, ONE_STATE + TAIL_ROWS, width), BF),
            pltpu.VMEM((n_dp, NEAR_ROWS, width), BF),
            pltpu.SemaphoreType.DMA((n_dp + 1,)),
        ],
        compiler_params=PARAMS,
        name="combine",
    )(prompt_for, got, tails)
    routed, w_bcdt = lax.optimization_barrier((routed, w_bcdt))
    arrived = exchange(routed, "dp")

    w_near = lax.all_gather(w_bcdt.T, "tp")
    own_columns = n_tp * w_bcdt.shape[1]
    w_near = w_near.reshape(own_columns, 2, n_ctx // 2, n_tp, features)
    w_near = lax.dynamic_index_in_dim(w_near, tp, 3, keepdims=False)
    w_near = jnp.swapaxes(w_near, 1, 2).reshape(own_columns, -1)
    w_near = jnp.concatenate([w_near, w_near], axis=0)
    w_near = jnp.pad(w_near, ((HALF, LANES - HALF - 2 * own_columns), (0, 0)))

    piece = pl.pallas_call(
        columns_kernel,
        out_shape=jax.ShapeDtypeStruct((peers, rows, LANES), BF),
        in_specs=[VM, VM, VM],
        out_specs=HB,
        scratch_shapes=[
            pltpu.VMEM((NEAR_ROWS // 8, 8, LANES), F32),
            pltpu.VMEM((peers, rows, LANES), BF),
            pltpu.SemaphoreType.DMA(()),
        ],
        compiler_params=PARAMS,
        name="columns",
    )(arrived, near_gain, w_near)
    piece, w_zx, w_out = lax.optimization_barrier((piece, w_zx, w_out))
    everyone = exchange(piece, BOTH)
    weights = jnp.concatenate(
        [w_zx.reshape(2 * channels, model), w_out.reshape(channels, model)], axis=0
    )

    outgoing, extra = pl.pallas_call(
        decode_kernel,
        out_shape=(
            jax.ShapeDtypeStruct((peers, rows, LANES), BF),
            jax.ShapeDtypeStruct((24, LANES), F32),
        ),
        in_specs=[VM, VM, HB, HB, HB, HB],
        out_specs=(HB, VM),
        scratch_shapes=[
            pltpu.VMEM((slots, ONE_STATE + TAIL_ROWS, width), BF),
            pltpu.SMEM(decode_prompt.shape, jnp.int32),
            pltpu.VMEM((model // LANES, LANES), F32),
            pltpu.VMEM(small.shape, F32),
            pltpu.VMEM((16, LANES), F32),
            pltpu.VMEM((16, LANES), F32),
            pltpu.VMEM((16, LANES), F32),
            pltpu.VMEM((peers, rows, LANES), BF),
            pltpu.SemaphoreType.DMA((3 + slots,)),
            pltpu.SemaphoreType.DMA((peers // 16,)),
        ],
        compiler_params=PARAMS,
        name="decode",
    )(
        everyone,
        weights,
        in_hbm(arrived),
        in_hbm(decode_prompt),
        in_hbm(norm_gain.reshape(model // LANES, LANES)),
        in_hbm(small),
    )
    incoming = exchange(outgoing, BOTH)

    start = jnp.stack(
        [
            lax.dynamic_index_in_dim(arrived[:, :ONE_STATE], own_slots[s] // slots, 0, keepdims=False)
            for s in range(slots)
        ]
    )
    push = extra[0:8].reshape(steps, slots, channels)
    b_conv = extra[8:16].reshape(steps, slots, width)
    kept = extra[16:18]
    final = kept[:, :, None] * start.astype(F32) + jnp.einsum(
        "tpc,tpn->pcn", push, b_conv, precision=lax.Precision.HIGHEST
    )

    mixed = pl.pallas_call(
        finish_kernel,
        out_shape=jax.ShapeDtypeStruct((rows, features), BF),
        in_specs=[VM],
        out_specs=VM,
        compiler_params=PARAMS,
        name="finish",
    )(incoming)
    return (
        mixed.reshape(steps, slots, features),
        final.reshape(slots, heads, HEAD_DIM, width),
    )


def solution(mesh):
    return jax.shard_map(
        per_device,
        mesh=mesh,
        in_specs=(
            P(),
            P(),
            P("dp", ("ctx", "tp")),
            P(),
            P(None, ("tp", "ctx"), None, None),
            P(None, ("ctx", "tp")),
            P(None, ("tp", "ctx"), None),
            P(("tp", "ctx"), None),
            P(),
            P(),
            P(("tp", "ctx")),
            P(("tp", "ctx")),
            P(("tp", "ctx")),
            P(("tp", "ctx"), None),
            P(("tp", "ctx"), None, None),
            P("ctx", "dp", "tp", None, None),
            P("ctx", "dp", "tp"),
            P("dp", None, ("tp", "ctx"), None),
            P("dp", None, None),
        ),
        out_specs=(P(None, "dp", ("ctx", "tp")), P("dp", ("tp", "ctx"), None, None)),
        check_vma=False,
    )
```

```python
import jax
import jax.numpy as jnp
from jax import lax
from jax.experimental import pallas as pl
from jax.experimental.pallas import tpu as pltpu
from jax.sharding import PartitionSpec as P

HEADS = 128
HEAD_DIM = 64
EPS = 1e-05
BOTH = ("ctx", "tp")
BF = jnp.bfloat16
F32 = jnp.float32
LANES = 128
HALF = 64
VMEM_LIMIT = 12 * 1024 * 1024

STATE_ROWS = 256
RATE_ROWS = 16
TOKEN_ROWS = 32
SIDE_ROWS = RATE_ROWS + TOKEN_ROWS
ONE_STATE = 128
TAIL_ROWS = 16
NEAR_ROWS = 16


def exchange(pieces, axis):
    return lax.all_to_all(pieces, axis, 0, 0, tiled=True)


def in_three(values):
    first = values.astype(BF)
    rest = values - first.astype(F32)
    second = rest.astype(BF)
    third = (rest - second.astype(F32)).astype(BF)
    return first, second, third


def silu(v):
    return v / (1.0 + jnp.exp(-v))


def low_half(shape=(8, LANES)):
    return lax.broadcasted_iota(jnp.int32, shape, 1) < HALF


def send_kernel(
    tokens_hbm, prompt_hbm, rate_hbm, table_hbm, states_hbm, out_ref,
    tokens_ref, prompt_ref, rate_ref, table_ref, states_ref, token_ref, rows_ref, block_ref, side_ref, sems,
):
    pairs = [
        (tokens_hbm, tokens_ref),
        (prompt_hbm, prompt_ref),
        (rate_hbm, rate_ref),
        (table_hbm, table_ref),
        (states_hbm, states_ref),
    ]
    loads = [pltpu.make_async_copy(a, b, sems.at[n]) for n, (a, b) in enumerate(pairs)]
    for load in loads:
        load.start()
    group = lax.axis_index("dp")
    count = out_ref.shape[0]
    slots = states_ref.shape[0]
    heads = rate_ref.shape[1] // count
    steps = tokens_ref.shape[0]
    rows = steps * slots
    groups = prompt_ref.shape[0] // slots
    vocab_rows = table_ref.shape[1]
    first = group * vocab_rows
    loads[0].wait()
    loads[1].wait()
    for g in range(groups):
        for step in range(steps):
            for slot in range(slots):
                token = tokens_ref[step, prompt_ref[g * slots + slot]] - first
                at = g * rows + step * slots + slot
                token_ref[at : at + 1, :] = jnp.full((1, LANES), token, jnp.int32)
    loads[2].wait()
    for c in range(count):
        for p in range(slots):
            for h in range(heads):
                at = (c * slots + p) * heads + h
                rows_ref[at : at + 1, :] = jnp.full((1, LANES), rate_ref[p, c * heads + h], F32)
    each = slots * heads
    parts = [p.astype(F32) for p in in_three(rows_ref[...])]
    for c in range(count):
        for n, part in enumerate(parts):
            block_ref[c, n * each : (n + 1) * each, :] = part[c * each : (c + 1) * each]
        block_ref[c, 3 * each : RATE_ROWS, :] = jnp.zeros((RATE_ROWS - 3 * each, LANES), F32)
        side_ref[c, 0:RATE_ROWS, :] = block_ref[c].astype(BF)
    loads[4].wait()
    stores = []
    for p in range(slots):
        stores.append(
            pltpu.make_async_copy(
                states_ref.at[p], out_ref.at[:, p * ONE_STATE : (p + 1) * ONE_STATE, :], sems.at[5 + p]
            )
        )
        stores[-1].start()
    loads[3].wait()
    tokens = token_ref[:, 0:1]
    found = jnp.zeros((groups * rows, LANES), F32)
    whole = vocab_rows // LANES * LANES
    bounds = [*range(0, whole, 1024), whole, vocab_rows]
    for low_at, high_at in zip(bounds[:-1], bounds[1:]):
        ids = lax.broadcasted_iota(jnp.int32, (groups * rows, high_at - low_at), 1) + low_at
        hot = jnp.where(tokens == ids, 1.0, 0.0).astype(BF)
        table = table_ref[:, low_at:high_at]
        found = found + lax.dot_general(
            hot,
            jnp.concatenate([table, table], axis=0),
            (((1,), (1,)), ((), ())),
            preferred_element_type=F32,
        )
    low = low_half((TOKEN_ROWS, LANES))
    tile = jnp.where(low, found[0:TOKEN_ROWS], found[TOKEN_ROWS : 2 * TOKEN_ROWS]).astype(BF)
    for c in range(count):
        side_ref[c, RATE_ROWS:SIDE_ROWS, :] = tile
    stores.append(
        pltpu.make_async_copy(
            side_ref, out_ref.at[:, STATE_ROWS : STATE_ROWS + SIDE_ROWS, :], sems.at[5 + slots]
        )
    )
    stores[-1].start()
    for store in stores:
        store.wait()


def combine_kernel(
    chosen_ref, got_ref, tails_ref, gain_ref, weight_ref, out_ref, bundle_ref, near_ref, sems
):
    count = got_ref.shape[0]
    groups = out_ref.shape[0]
    own_rows = ONE_STATE + TAIL_ROWS

    low = low_half((TOKEN_ROWS, LANES))
    at = STATE_ROWS + RATE_ROWS
    pieces = []
    for k in range(count // 2):
        one = got_ref[k, at : at + TOKEN_ROWS, :].astype(F32)
        two = got_ref[count // 2 + k, at : at + TOKEN_ROWS, :].astype(F32)
        early = jnp.where(low, one, pltpu.roll(two, HALF, 1))
        late = jnp.where(low, pltpu.roll(one, HALF, 1), two)
        rows = jnp.concatenate([early, late], axis=0)
        pieces.append((rows * gain_ref[k : k + 1, :]).astype(BF))
    partial = lax.dot_general(
        jnp.concatenate(pieces, axis=1),
        weight_ref[...],
        (((1,), (1,)), ((), ())),
        preferred_element_type=F32,
    )
    one = got_ref[lax.axis_index("ctx"), at : at + TOKEN_ROWS, :].astype(F32)
    own = jnp.concatenate([one, pltpu.roll(one, HALF, 1)], axis=0)
    lane = lax.broadcasted_iota(jnp.int32, own.shape, 1)
    first = partial.astype(BF).astype(F32)
    tiles = jnp.where(lane < HALF, own, jnp.where(lane < HALF + 24, first, partial - first))
    for g in range(groups):
        tile = jnp.concatenate([tiles[8 * g : 8 * g + 8], jnp.zeros((8, LANES), F32)], axis=0)
        near_ref[g] = tile.astype(BF)
    move_near = pltpu.make_async_copy(
        near_ref, out_ref.at[:, own_rows : own_rows + NEAR_ROWS, :], sems.at[groups]
    )
    move_near.start()

    rates = []
    for k in range(count):
        parts = got_ref[k, STATE_ROWS : STATE_ROWS + RATE_ROWS, :].astype(F32)
        rates.append(parts[0:4] + parts[4:8] + parts[8:12])
    weights = [None] * count
    later = jnp.zeros_like(rates[0])
    for k in reversed(range(count)):
        weights[k] = jnp.exp(-later)
        later = later + rates[k]
    for part in range(4):
        total = jnp.zeros((HEAD_DIM, LANES), F32)
        for k in range(count):
            own = got_ref[k, part * HEAD_DIM : (part + 1) * HEAD_DIM, :].astype(F32)
            total = total + (own * weights[k][part : part + 1]).astype(BF).astype(F32)
        at = (part % 2) * HEAD_DIM
        bundle_ref[part // 2, at : at + HEAD_DIM, :] = total.astype(BF)
    for p in range(bundle_ref.shape[0]):
        bundle_ref[p, ONE_STATE:own_rows, :] = tails_ref[p]
    moves = [
        pltpu.make_async_copy(
            bundle_ref.at[chosen_ref[g]], out_ref.at[g, 0:own_rows, :], sems.at[g]
        )
        for g in range(groups)
    ]
    for move in moves:
        move.start()
    for move in [*moves, move_near]:
        move.wait()


def spread_kernel(arrived_ref, out_ref, tile_ref, sem):
    at = ONE_STATE + TAIL_ROWS
    total = arrived_ref[0, at : at + NEAR_ROWS, :].astype(F32)
    for g in range(1, arrived_ref.shape[0]):
        total = total + arrived_ref[g, at : at + NEAR_ROWS, :].astype(F32)
    tile_ref[...] = jnp.broadcast_to(total[0:8].astype(BF)[None], tile_ref.shape)
    move = pltpu.make_async_copy(tile_ref, out_ref, sem)
    move.start()
    move.wait()


def decode_kernel(
    everyone_ref, weights_ref, arrived_hbm, prompt_hbm, gain_hbm, small_hbm, out_ref, start_ref, extra_ref,
    arrived_ref, prompt_ref, gain_ref, small_ref, x_ref, b_ref, c_ref, tile_ref, load_sems, sems,
):
    pairs = [(prompt_hbm, prompt_ref), (gain_hbm, gain_ref), (small_hbm, small_ref)]
    loads = [pltpu.make_async_copy(a, b, load_sems.at[n]) for n, (a, b) in enumerate(pairs)]
    for load in loads:
        load.start()
    ctx, group, tp = (lax.axis_index(a) for a in ("ctx", "dp", "tp"))
    head_at = (tp * lax.axis_size("ctx") + ctx) * 2
    peers = everyone_ref.shape[0]
    model = peers * HALF
    lane = lax.broadcasted_iota(jnp.int32, (8, LANES), 1)
    row = lax.broadcasted_iota(jnp.int32, (8, LANES), 0)
    low = lane < HALF

    tiles = [everyone_ref[p].astype(F32) for p in range(peers)]
    rows = [
        jnp.where(low, tiles[2 * n], pltpu.roll(tiles[2 * n + 1], HALF, 1)) for n in range(peers // 2)
    ]
    squares = rows[0] * rows[0]
    for r in rows[1:]:
        squares = squares + r * r
    own_rows = arrived_ref.shape[1]
    loads[0].wait()
    for slot in range(2):
        holder = prompt_ref[group * 2 + slot] // 2
        loads.append(
            pltpu.make_async_copy(
                arrived_hbm.at[holder, 0:own_rows, :], arrived_ref.at[slot], load_sems.at[3 + slot]
            )
        )
        loads[-1].start()
    loads[1].wait()
    inverse = lax.rsqrt(jnp.sum(squares, axis=1, keepdims=True) * (1.0 / model) + EPS)
    normed = jnp.concatenate(
        [(r * inverse * gain_ref[n : n + 1, :]).astype(BF) for n, r in enumerate(rows)], axis=1
    )

    projected = lax.dot_general(
        normed, weights_ref[0 : 2 * LANES, :], (((1,), (1,)), ((), ())), preferred_element_type=F32
    )

    columns = [jnp.zeros((8, LANES), F32) for _ in range(3)]
    for c in range(16):
        part = tiles[4 * c] + tiles[4 * c + 1] + tiles[4 * c + 2] + tiles[4 * c + 3]
        part = part + pltpu.roll(part, LANES - 24, 1)
        part = jnp.where((lane >= HALF) & (lane < HALF + 24), part, 0.0)
        first, offset = divmod(c * 24, LANES)
        part = pltpu.roll(part, (offset - HALF) % LANES, 1)
        if offset + 24 <= LANES:
            columns[first] = columns[first] + part
        else:
            columns[first] = columns[first] + jnp.where(lane >= offset, part, 0.0)
            columns[first + 1] = columns[first + 1] + jnp.where(lane < offset, part, 0.0)
    columns = [v * inverse for v in columns]

    for load in loads[2:]:
        load.wait()

    for slot in range(2):
        tail = arrived_ref[slot, ONE_STATE : ONE_STATE + TAIL_ROWS, :].astype(F32)
        for k in range(3):
            at = 2 * k + slot
            x_ref[at : at + 1, :] = tail[k : k + 1]
            b_ref[at : at + 1, :] = tail[3 + 2 * k : 4 + 2 * k]
            c_ref[at : at + 1, :] = tail[4 + 2 * k : 5 + 2 * k]
    b_ref[6:14, :] = columns[0]
    c_ref[6:14, :] = columns[1]

    def convolved(ref, weight_at, bias_at):
        total = ref[0:8, :] * small_ref[weight_at : weight_at + 1, :]
        for k in range(1, 4):
            total = total + ref[2 * k : 2 * k + 8, :] * small_ref[weight_at + k : weight_at + k + 1, :]
        return silu(total + small_ref[bias_at : bias_at + 1, :])

    b_conv = convolved(b_ref, 4, 13)
    c_conv = convolved(c_ref, 8, 14)

    raw = pltpu.roll(columns[2], lax.rem(LANES - head_at, LANES), 1)
    raw = jnp.where(low, raw[:, 0:1], raw[:, 1:2]) + small_ref[15:16, :]
    step = jnp.maximum(raw, 0.0) + jnp.log1p(jnp.exp(-jnp.abs(raw)))
    log_retain = -step * jnp.exp(small_ref[16:17, :])

    def earlier(v, lag):
        return jnp.where(row >= 2 * lag, pltpu.roll(v, 2 * lag, 0), 0.0)

    log_total = log_retain
    for lag in range(1, 4):
        log_total = log_total + earlier(log_retain, lag)

    c_parts = jnp.concatenate([p.astype(F32) for p in in_three(c_conv)], axis=0).astype(BF)
    from_start = []
    for slot in range(2):
        state = arrived_ref[slot, 0:ONE_STATE, :]
        start_ref[slot] = state
        product = lax.dot_general(
            c_parts, state, (((1,), (1,)), ((), ())), preferred_element_type=F32
        )
        from_start.append(product[0:8] + product[8:16] + product[16:24])
    y = jnp.exp(log_total) * jnp.where(row % 2 == 0, from_start[0], from_start[1])

    gate = projected[:, 0:LANES]
    x_ref[6:14, :] = projected[:, LANES : 2 * LANES]
    x_conv = convolved(x_ref, 0, 12)
    drive = step * x_conv
    y = y + small_ref[17:18, :] * x_conv
    for lag in range(4):
        match = jnp.sum(c_conv * earlier(b_conv, lag), axis=1, keepdims=True)
        if lag == 0:
            y = y + drive * match
        else:
            decay = jnp.exp(log_total - earlier(log_total, lag))
            y = y + decay * earlier(drive, lag) * match
    gated = y * silu(gate)
    total = jnp.sum(gated * gated, axis=1, keepdims=True)
    parts = [p.astype(F32) for p in in_three(total)]
    aside = jnp.where(
        lane == HALF,
        parts[0],
        jnp.where(lane == HALF + 1, parts[1], jnp.where(lane == HALF + 2, parts[2], 0.0)),
    )
    weighted = (gated * small_ref[18:19, :]).astype(BF)

    last = jnp.where(row % 2 == 0, log_total[6:7], log_total[7:8])
    extra_ref[0:8, :] = jnp.exp(last - log_total) * drive
    extra_ref[8:16, :] = b_conv
    extra_ref[16:24, :] = jnp.exp(last)

    moves = []
    for n in range(peers // 16):
        wide = jnp.dot(
            weighted, weights_ref[2 * LANES :, n * 1024 : (n + 1) * 1024], preferred_element_type=F32
        )
        for m in range(8):
            piece = wide[:, m * LANES : (m + 1) * LANES]
            tile_ref[16 * n + 2 * m] = jnp.where(low, piece, aside).astype(BF)
            tile_ref[16 * n + 2 * m + 1] = jnp.where(low, pltpu.roll(piece, HALF, 1), aside).astype(BF)
        part = pl.ds(16 * n, 16)
        moves.append(pltpu.make_async_copy(tile_ref.at[part], out_ref.at[part], sems.at[n]))
        moves[-1].start()
    for move in moves:
        move.wait()


def finish_kernel(incoming_ref, out_ref):
    total = incoming_ref[0].astype(F32)
    for p in range(1, incoming_ref.shape[0]):
        total = total + incoming_ref[p].astype(F32)
    squares = total[:, HALF : HALF + 1] + total[:, HALF + 1 : HALF + 2] + total[:, HALF + 2 : HALF + 3]
    scale = lax.rsqrt(squares * (1.0 / (HEADS * HEAD_DIM)) + EPS)
    out_ref[...] = (total[:, 0:HALF] * scale).astype(BF)


VM = pl.BlockSpec(memory_space=pltpu.VMEM)
SM = pl.BlockSpec(memory_space=pltpu.SMEM)
HB = pl.BlockSpec(memory_space=pltpu.HBM)


def in_hbm(array):
    return pltpu.with_memory_space_constraint(array, pltpu.HBM)


PARAMS = pltpu.CompilerParams(vmem_limit_bytes=VMEM_LIMIT)


def per_device(
    token_ids,
    decode_prompt,
    embedding,
    norm_gain,
    w_zx,
    w_bcdt,
    conv_x_weight,
    conv_x_bias,
    conv_bc_weight,
    conv_bc_bias,
    dt_bias,
    a_log,
    d_skip,
    gate_norm_gain,
    w_out,
    state_parts,
    seg_rate,
    x_tail,
    bc_tail,
):
    ctx, group, tp = (lax.axis_index(a) for a in ("ctx", "dp", "tp"))
    n_ctx, n_dp, n_tp = (lax.axis_size(a) for a in ("ctx", "dp", "tp"))
    peers = n_ctx * n_tp
    slots = state_parts.shape[1]
    heads = w_zx.shape[1]
    width = state_parts.shape[-1]
    steps = token_ids.shape[0]
    vocab_rows, features = embedding.shape
    model = norm_gain.shape[0]
    rows = steps * slots
    channels = heads * HEAD_DIM

    sent = pl.pallas_call(
        send_kernel,
        out_shape=jax.ShapeDtypeStruct((n_ctx, STATE_ROWS + SIDE_ROWS, width), BF),
        in_specs=[HB] * 5,
        out_specs=HB,
        scratch_shapes=[
            pltpu.SMEM(token_ids.shape, jnp.int32),
            pltpu.SMEM(decode_prompt.shape, jnp.int32),
            pltpu.SMEM(seg_rate.shape[1:], F32),
            pltpu.VMEM((features, vocab_rows), BF),
            pltpu.VMEM((slots, n_ctx, ONE_STATE, width), BF),
            pltpu.VMEM((n_dp * rows, LANES), jnp.int32),
            pltpu.VMEM((n_ctx * slots * heads, LANES), F32),
            pltpu.VMEM((n_ctx, RATE_ROWS, LANES), F32),
            pltpu.VMEM((n_ctx, SIDE_ROWS, LANES), BF),
            pltpu.SemaphoreType.DMA((6 + slots,)),
        ],
        compiler_params=PARAMS,
        name="send",
    )(
        in_hbm(token_ids),
        in_hbm(decode_prompt),
        in_hbm(seg_rate[0]),
        in_hbm(embedding.T),
        in_hbm(state_parts.reshape(slots, n_ctx, ONE_STATE, width)),
    )
    got = exchange(sent, "ctx")

    w_near = lax.all_gather(w_bcdt.T, "tp")
    own_columns = n_tp * w_bcdt.shape[1]
    w_near = w_near.reshape(own_columns, 2, n_ctx // 2, n_tp, features)
    w_near = lax.dynamic_index_in_dim(w_near, tp, 3, keepdims=False)
    w_near = jnp.swapaxes(w_near, 1, 2).reshape(own_columns, -1)
    w_near = jnp.concatenate([w_near, w_near], axis=0)
    w_near = jnp.pad(w_near, ((HALF, LANES - HALF - 2 * own_columns), (0, 0)))
    near_gain = norm_gain.reshape(2, n_ctx // 2, n_tp, features)
    near_gain = lax.dynamic_index_in_dim(near_gain, tp, 2, keepdims=False)
    near_gain = jnp.swapaxes(near_gain, 0, 1).reshape(n_ctx // 2, -1)
    tails = jnp.concatenate([x_tail.reshape(slots, 3, LANES), bc_tail.reshape(slots, 6, LANES)], axis=1)
    tails = jnp.pad(tails, ((0, 0), (0, TAIL_ROWS - tails.shape[1]), (0, 0)))
    wanted = decode_prompt.reshape(n_dp, slots) - group * slots
    prompt_for = jnp.any(wanted == 1, axis=1).astype(jnp.int32)

    def spread(values):
        return jnp.broadcast_to(values[:, None], (heads, HEAD_DIM)).reshape(1, channels)

    small = jnp.concatenate(
        [
            conv_x_weight.reshape(4, channels),
            conv_bc_weight[:, :width],
            conv_bc_weight[:, width:],
            conv_x_bias.reshape(1, channels),
            conv_bc_bias.reshape(2, width),
            spread(dt_bias),
            spread(a_log),
            spread(d_skip),
            gate_norm_gain.reshape(1, channels),
        ],
        axis=0,
    )
    small = jnp.pad(small, ((0, -small.shape[0] % 8), (0, 0)))

    routed = pl.pallas_call(
        combine_kernel,
        out_shape=jax.ShapeDtypeStruct((n_dp, ONE_STATE + TAIL_ROWS + NEAR_ROWS, width), BF),
        in_specs=[SM, VM, VM, VM, VM],
        out_specs=HB,
        scratch_shapes=[
            pltpu.VMEM((slots, ONE_STATE + TAIL_ROWS, width), BF),
            pltpu.VMEM((n_dp, NEAR_ROWS, width), BF),
            pltpu.SemaphoreType.DMA((n_dp + 1,)),
        ],
        compiler_params=PARAMS,
        name="combine",
    )(prompt_for, got, tails, near_gain, w_near)
    arrived = exchange(routed, "dp")

    piece = pl.pallas_call(
        spread_kernel,
        out_shape=jax.ShapeDtypeStruct((peers, rows, LANES), BF),
        in_specs=[VM],
        out_specs=HB,
        scratch_shapes=[
            pltpu.VMEM((peers, rows, LANES), BF),
            pltpu.SemaphoreType.DMA(()),
        ],
        compiler_params=PARAMS,
        name="spread",
    )(arrived)
    piece, w_zx, w_out = lax.optimization_barrier((piece, w_zx, w_out))
    everyone = exchange(piece, BOTH)
    weights = jnp.concatenate(
        [w_zx.reshape(2 * channels, model), w_out.reshape(channels, model)], axis=0
    )

    outgoing, start, extra = pl.pallas_call(
        decode_kernel,
        out_shape=(
            jax.ShapeDtypeStruct((peers, rows, LANES), BF),
            jax.ShapeDtypeStruct((slots, ONE_STATE, width), BF),
            jax.ShapeDtypeStruct((24, LANES), F32),
        ),
        in_specs=[VM, VM, HB, HB, HB, HB],
        out_specs=(HB, VM, VM),
        scratch_shapes=[
            pltpu.VMEM((slots, ONE_STATE + TAIL_ROWS, width), BF),
            pltpu.SMEM(decode_prompt.shape, jnp.int32),
            pltpu.VMEM((model // LANES, LANES), F32),
            pltpu.VMEM(small.shape, F32),
            pltpu.VMEM((16, LANES), F32),
            pltpu.VMEM((16, LANES), F32),
            pltpu.VMEM((16, LANES), F32),
            pltpu.VMEM((peers, rows, LANES), BF),
            pltpu.SemaphoreType.DMA((3 + slots,)),
            pltpu.SemaphoreType.DMA((peers // 16,)),
        ],
        compiler_params=PARAMS,
        name="decode",
    )(
        everyone,
        weights,
        in_hbm(arrived),
        in_hbm(decode_prompt),
        in_hbm(norm_gain.reshape(model // LANES, LANES)),
        in_hbm(small),
    )
    incoming = exchange(outgoing, BOTH)

    push = extra[0:8].reshape(steps, slots, channels)
    b_conv = extra[8:16].reshape(steps, slots, width)
    kept = extra[16:18]
    final = kept[:, :, None] * start.astype(F32) + jnp.einsum(
        "tpc,tpn->pcn", push, b_conv, precision=lax.Precision.HIGHEST
    )

    mixed = pl.pallas_call(
        finish_kernel,
        out_shape=jax.ShapeDtypeStruct((rows, features), BF),
        in_specs=[VM],
        out_specs=VM,
        compiler_params=PARAMS,
        name="finish",
    )(incoming)
    return (
        mixed.reshape(steps, slots, features),
        final.reshape(slots, heads, HEAD_DIM, width),
    )


def solution(mesh):
    return jax.shard_map(
        per_device,
        mesh=mesh,
        in_specs=(
            P(),
            P(),
            P("dp", ("ctx", "tp")),
            P(),
            P(None, ("tp", "ctx"), None, None),
            P(None, ("ctx", "tp")),
            P(None, ("tp", "ctx"), None),
            P(("tp", "ctx"), None),
            P(),
            P(),
            P(("tp", "ctx")),
            P(("tp", "ctx")),
            P(("tp", "ctx")),
            P(("tp", "ctx"), None),
            P(("tp", "ctx"), None, None),
            P("ctx", "dp", "tp", None, None),
            P("ctx", "dp", "tp"),
            P("dp", None, ("tp", "ctx"), None),
            P("dp", None, None),
        ),
        out_specs=(P(None, "dp", ("ctx", "tp")), P("dp", ("tp", "ctx"), None, None)),
        check_vma=False,
    )
```

```python
import jax
import jax.numpy as jnp
from jax import lax
from jax.experimental import pallas as pl
from jax.experimental.pallas import tpu as pltpu
from jax.sharding import PartitionSpec as P

HEADS = 128
HEAD_DIM = 64
EPS = 1e-05
BOTH = ("ctx", "tp")
BF = jnp.bfloat16
F32 = jnp.float32
LANES = 128
HALF = 64
VMEM_LIMIT = 12 * 1024 * 1024

STATE_ROWS = 256
RATE_ROWS = 16
TOKEN_ROWS = 32
SIDE_ROWS = RATE_ROWS + TOKEN_ROWS
ONE_STATE = 128
TAIL_ROWS = 16
NEAR_ROWS = 64


def exchange(pieces, axis):
    return lax.all_to_all(pieces, axis, 0, 0, tiled=True)


def in_three(values):
    first = values.astype(BF)
    rest = values - first.astype(F32)
    second = rest.astype(BF)
    third = (rest - second.astype(F32)).astype(BF)
    return first, second, third


def silu(v):
    return v / (1.0 + jnp.exp(-v))


def low_half(shape=(8, LANES)):
    return lax.broadcasted_iota(jnp.int32, shape, 1) < HALF


def send_kernel(
    tokens_hbm, prompt_hbm, rate_hbm, table_hbm, states_hbm, out_ref,
    tokens_ref, prompt_ref, rate_ref, table_ref, states_ref, token_ref, rows_ref, block_ref, side_ref, sems,
):
    pairs = [
        (tokens_hbm, tokens_ref),
        (prompt_hbm, prompt_ref),
        (rate_hbm, rate_ref),
        (table_hbm, table_ref),
        (states_hbm, states_ref),
    ]
    loads = [pltpu.make_async_copy(a, b, sems.at[n]) for n, (a, b) in enumerate(pairs)]
    for load in loads:
        load.start()
    group = lax.axis_index("dp")
    count = out_ref.shape[0]
    slots = states_ref.shape[0]
    heads = rate_ref.shape[1] // count
    steps = tokens_ref.shape[0]
    rows = steps * slots
    groups = prompt_ref.shape[0] // slots
    vocab_rows = table_ref.shape[1]
    first = group * vocab_rows
    loads[0].wait()
    loads[1].wait()
    for g in range(groups):
        for step in range(steps):
            for slot in range(slots):
                token = tokens_ref[step, prompt_ref[g * slots + slot]] - first
                at = g * rows + step * slots + slot
                token_ref[at : at + 1, :] = jnp.full((1, LANES), token, jnp.int32)
    loads[2].wait()
    for c in range(count):
        for p in range(slots):
            for h in range(heads):
                at = (c * slots + p) * heads + h
                rows_ref[at : at + 1, :] = jnp.full((1, LANES), rate_ref[p, c * heads + h], F32)
    each = slots * heads
    parts = [p.astype(F32) for p in in_three(rows_ref[...])]
    for c in range(count):
        for n, part in enumerate(parts):
            block_ref[c, n * each : (n + 1) * each, :] = part[c * each : (c + 1) * each]
        block_ref[c, 3 * each : RATE_ROWS, :] = jnp.zeros((RATE_ROWS - 3 * each, LANES), F32)
        side_ref[c, 0:RATE_ROWS, :] = block_ref[c].astype(BF)
    loads[4].wait()
    stores = []
    for p in range(slots):
        stores.append(
            pltpu.make_async_copy(
                states_ref.at[p], out_ref.at[:, p * ONE_STATE : (p + 1) * ONE_STATE, :], sems.at[5 + p]
            )
        )
        stores[-1].start()
    loads[3].wait()
    tokens = token_ref[:, 0:1]
    found = jnp.zeros((groups * rows, LANES), F32)
    whole = vocab_rows // LANES * LANES
    bounds = [*range(0, whole, 1024), whole, vocab_rows]
    for low_at, high_at in zip(bounds[:-1], bounds[1:]):
        ids = lax.broadcasted_iota(jnp.int32, (groups * rows, high_at - low_at), 1) + low_at
        hot = jnp.where(tokens == ids, 1.0, 0.0).astype(BF)
        table = table_ref[:, low_at:high_at]
        found = found + lax.dot_general(
            hot,
            jnp.concatenate([table, table], axis=0),
            (((1,), (1,)), ((), ())),
            preferred_element_type=F32,
        )
    low = low_half((TOKEN_ROWS, LANES))
    tile = jnp.where(low, found[0:TOKEN_ROWS], found[TOKEN_ROWS : 2 * TOKEN_ROWS]).astype(BF)
    for c in range(count):
        side_ref[c, RATE_ROWS:SIDE_ROWS, :] = tile
    stores.append(
        pltpu.make_async_copy(
            side_ref, out_ref.at[:, STATE_ROWS : STATE_ROWS + SIDE_ROWS, :], sems.at[5 + slots]
        )
    )
    stores[-1].start()
    for store in stores:
        store.wait()


def combine_kernel(chosen_ref, got_ref, tails_ref, out_ref, bundle_ref, near_ref, sems):
    count = got_ref.shape[0]
    groups = out_ref.shape[0]
    own_rows = ONE_STATE + TAIL_ROWS
    low = low_half((TOKEN_ROWS, LANES))
    at = STATE_ROWS + RATE_ROWS
    for pair in range(0, count // 2, 2):
        early, late = [], []
        for k in (pair, pair + 1):
            one = got_ref[k, at : at + TOKEN_ROWS, :].astype(F32)
            two = got_ref[count // 2 + k, at : at + TOKEN_ROWS, :].astype(F32)
            early.append(jnp.where(low, one, pltpu.roll(two, HALF, 1)))
            late.append(jnp.where(low, pltpu.roll(one, HALF, 1), two))
        for g in range(groups):
            source = early if g < groups // 2 else late
            r = (g % (groups // 2)) * 8
            both = jnp.concatenate([s[r : r + 8] for s in source], axis=0)
            near_ref[g, pair * 8 : pair * 8 + 16, :] = both.astype(BF)
    move_near = pltpu.make_async_copy(
        near_ref, out_ref.at[:, own_rows : own_rows + NEAR_ROWS, :], sems.at[groups]
    )
    move_near.start()
    rates = []
    for k in range(count):
        parts = got_ref[k, STATE_ROWS : STATE_ROWS + RATE_ROWS, :].astype(F32)
        rates.append(parts[0:4] + parts[4:8] + parts[8:12])
    weights = [None] * count
    later = jnp.zeros_like(rates[0])
    for k in reversed(range(count)):
        weights[k] = jnp.exp(-later)
        later = later + rates[k]
    for part in range(4):
        total = jnp.zeros((HEAD_DIM, LANES), F32)
        for k in range(count):
            own = got_ref[k, part * HEAD_DIM : (part + 1) * HEAD_DIM, :].astype(F32)
            total = total + (own * weights[k][part : part + 1]).astype(BF).astype(F32)
        at = (part % 2) * HEAD_DIM
        bundle_ref[part // 2, at : at + HEAD_DIM, :] = total.astype(BF)
    for p in range(bundle_ref.shape[0]):
        bundle_ref[p, ONE_STATE:own_rows, :] = tails_ref[p]
    moves = [
        pltpu.make_async_copy(
            bundle_ref.at[chosen_ref[g]], out_ref.at[g, 0:own_rows, :], sems.at[g]
        )
        for g in range(groups)
    ]
    for move in moves:
        move.start()
    for move in [*moves, move_near]:
        move.wait()


def columns_kernel(arrived_ref, gain_ref, weight_ref, out_ref, near_ref, tile_ref, sem):
    groups = arrived_ref.shape[0]
    at = ONE_STATE + TAIL_ROWS
    total = arrived_ref[0, at : at + NEAR_ROWS, :].astype(F32)
    for g in range(1, groups):
        total = total + arrived_ref[g, at : at + NEAR_ROWS, :].astype(F32)
    pieces = []
    for k in range(NEAR_ROWS // 8):
        rows = total[k * 8 : (k + 1) * 8]
        near_ref[k] = rows
        pieces.append((rows * gain_ref[k : k + 1, :]).astype(BF))
    weighted = jnp.concatenate(pieces, axis=1)
    partial = lax.dot_general(
        weighted, weight_ref[...], (((1,), (1,)), ((), ())), preferred_element_type=F32
    )
    ctx = lax.axis_index("ctx")
    half = lax.axis_size("ctx") // 2
    own = pltpu.roll(near_ref[lax.rem(ctx, half)], ctx // half * HALF, 1)
    lane = lax.broadcasted_iota(jnp.int32, (8, LANES), 1)
    first = partial.astype(BF).astype(F32)
    tile = jnp.where(lane < HALF, own, jnp.where(lane < HALF + 24, first, partial - first))
    tile_ref[...] = jnp.broadcast_to(tile.astype(BF)[None], tile_ref.shape)
    move = pltpu.make_async_copy(tile_ref, out_ref, sem)
    move.start()
    move.wait()


def decode_kernel(
    everyone_ref, weights_ref, arrived_hbm, prompt_hbm, gain_hbm, small_hbm, out_ref, start_ref, extra_ref,
    arrived_ref, prompt_ref, gain_ref, small_ref, x_ref, b_ref, c_ref, tile_ref, load_sems, sems,
):
    pairs = [(prompt_hbm, prompt_ref), (gain_hbm, gain_ref), (small_hbm, small_ref)]
    loads = [pltpu.make_async_copy(a, b, load_sems.at[n]) for n, (a, b) in enumerate(pairs)]
    for load in loads:
        load.start()
    ctx, group, tp = (lax.axis_index(a) for a in ("ctx", "dp", "tp"))
    head_at = (tp * lax.axis_size("ctx") + ctx) * 2
    peers = everyone_ref.shape[0]
    model = peers * HALF
    lane = lax.broadcasted_iota(jnp.int32, (8, LANES), 1)
    row = lax.broadcasted_iota(jnp.int32, (8, LANES), 0)
    low = lane < HALF

    tiles = [everyone_ref[p].astype(F32) for p in range(peers)]
    rows = [
        jnp.where(low, tiles[2 * n], pltpu.roll(tiles[2 * n + 1], HALF, 1)) for n in range(peers // 2)
    ]
    squares = rows[0] * rows[0]
    for r in rows[1:]:
        squares = squares + r * r
    own_rows = arrived_ref.shape[1]
    loads[0].wait()
    for slot in range(2):
        holder = prompt_ref[group * 2 + slot] // 2
        loads.append(
            pltpu.make_async_copy(
                arrived_hbm.at[holder, 0:own_rows, :], arrived_ref.at[slot], load_sems.at[3 + slot]
            )
        )
        loads[-1].start()
    loads[1].wait()
    inverse = lax.rsqrt(jnp.sum(squares, axis=1, keepdims=True) * (1.0 / model) + EPS)
    normed = jnp.concatenate(
        [(r * inverse * gain_ref[n : n + 1, :]).astype(BF) for n, r in enumerate(rows)], axis=1
    )

    projected = lax.dot_general(
        normed, weights_ref[0 : 2 * LANES, :], (((1,), (1,)), ((), ())), preferred_element_type=F32
    )

    columns = [jnp.zeros((8, LANES), F32) for _ in range(3)]
    for c in range(16):
        part = tiles[4 * c] + tiles[4 * c + 1] + tiles[4 * c + 2] + tiles[4 * c + 3]
        part = part + pltpu.roll(part, LANES - 24, 1)
        part = jnp.where((lane >= HALF) & (lane < HALF + 24), part, 0.0)
        first, offset = divmod(c * 24, LANES)
        part = pltpu.roll(part, (offset - HALF) % LANES, 1)
        if offset + 24 <= LANES:
            columns[first] = columns[first] + part
        else:
            columns[first] = columns[first] + jnp.where(lane >= offset, part, 0.0)
            columns[first + 1] = columns[first + 1] + jnp.where(lane < offset, part, 0.0)
    columns = [v * inverse for v in columns]

    for load in loads[2:]:
        load.wait()

    for slot in range(2):
        tail = arrived_ref[slot, ONE_STATE : ONE_STATE + TAIL_ROWS, :].astype(F32)
        for k in range(3):
            at = 2 * k + slot
            x_ref[at : at + 1, :] = tail[k : k + 1]
            b_ref[at : at + 1, :] = tail[3 + 2 * k : 4 + 2 * k]
            c_ref[at : at + 1, :] = tail[4 + 2 * k : 5 + 2 * k]
    b_ref[6:14, :] = columns[0]
    c_ref[6:14, :] = columns[1]

    def convolved(ref, weight_at, bias_at):
        total = ref[0:8, :] * small_ref[weight_at : weight_at + 1, :]
        for k in range(1, 4):
            total = total + ref[2 * k : 2 * k + 8, :] * small_ref[weight_at + k : weight_at + k + 1, :]
        return silu(total + small_ref[bias_at : bias_at + 1, :])

    b_conv = convolved(b_ref, 4, 13)
    c_conv = convolved(c_ref, 8, 14)

    raw = pltpu.roll(columns[2], lax.rem(LANES - head_at, LANES), 1)
    raw = jnp.where(low, raw[:, 0:1], raw[:, 1:2]) + small_ref[15:16, :]
    step = jnp.maximum(raw, 0.0) + jnp.log1p(jnp.exp(-jnp.abs(raw)))
    log_retain = -step * jnp.exp(small_ref[16:17, :])

    def earlier(v, lag):
        return jnp.where(row >= 2 * lag, pltpu.roll(v, 2 * lag, 0), 0.0)

    log_total = log_retain
    for lag in range(1, 4):
        log_total = log_total + earlier(log_retain, lag)

    c_parts = jnp.concatenate([p.astype(F32) for p in in_three(c_conv)], axis=0).astype(BF)
    from_start = []
    for slot in range(2):
        state = arrived_ref[slot, 0:ONE_STATE, :]
        start_ref[slot] = state
        product = lax.dot_general(
            c_parts, state, (((1,), (1,)), ((), ())), preferred_element_type=F32
        )
        from_start.append(product[0:8] + product[8:16] + product[16:24])
    y = jnp.exp(log_total) * jnp.where(row % 2 == 0, from_start[0], from_start[1])

    gate = projected[:, 0:LANES]
    x_ref[6:14, :] = projected[:, LANES : 2 * LANES]
    x_conv = convolved(x_ref, 0, 12)
    drive = step * x_conv
    y = y + small_ref[17:18, :] * x_conv
    for lag in range(4):
        match = jnp.sum(c_conv * earlier(b_conv, lag), axis=1, keepdims=True)
        if lag == 0:
            y = y + drive * match
        else:
            decay = jnp.exp(log_total - earlier(log_total, lag))
            y = y + decay * earlier(drive, lag) * match
    gated = y * silu(gate)
    total = jnp.sum(gated * gated, axis=1, keepdims=True)
    parts = [p.astype(F32) for p in in_three(total)]
    aside = jnp.where(
        lane == HALF,
        parts[0],
        jnp.where(lane == HALF + 1, parts[1], jnp.where(lane == HALF + 2, parts[2], 0.0)),
    )
    weighted = (gated * small_ref[18:19, :]).astype(BF)

    last = jnp.where(row % 2 == 0, log_total[6:7], log_total[7:8])
    extra_ref[0:8, :] = jnp.exp(last - log_total) * drive
    extra_ref[8:16, :] = b_conv
    extra_ref[16:24, :] = jnp.exp(last)

    moves = []
    for n in range(peers // 16):
        wide = jnp.dot(
            weighted, weights_ref[2 * LANES :, n * 1024 : (n + 1) * 1024], preferred_element_type=F32
        )
        for m in range(8):
            piece = wide[:, m * LANES : (m + 1) * LANES]
            tile_ref[16 * n + 2 * m] = jnp.where(low, piece, aside).astype(BF)
            tile_ref[16 * n + 2 * m + 1] = jnp.where(low, pltpu.roll(piece, HALF, 1), aside).astype(BF)
        part = pl.ds(16 * n, 16)
        moves.append(pltpu.make_async_copy(tile_ref.at[part], out_ref.at[part], sems.at[n]))
        moves[-1].start()
    for move in moves:
        move.wait()


def finish_kernel(incoming_ref, out_ref):
    total = incoming_ref[0].astype(F32)
    for p in range(1, incoming_ref.shape[0]):
        total = total + incoming_ref[p].astype(F32)
    squares = total[:, HALF : HALF + 1] + total[:, HALF + 1 : HALF + 2] + total[:, HALF + 2 : HALF + 3]
    scale = lax.rsqrt(squares * (1.0 / (HEADS * HEAD_DIM)) + EPS)
    out_ref[...] = (total[:, 0:HALF] * scale).astype(BF)


VM = pl.BlockSpec(memory_space=pltpu.VMEM)
SM = pl.BlockSpec(memory_space=pltpu.SMEM)
HB = pl.BlockSpec(memory_space=pltpu.HBM)


def in_hbm(array):
    return pltpu.with_memory_space_constraint(array, pltpu.HBM)


PARAMS = pltpu.CompilerParams(vmem_limit_bytes=VMEM_LIMIT)


def per_device(
    token_ids,
    decode_prompt,
    embedding,
    norm_gain,
    w_zx,
    w_bcdt,
    conv_x_weight,
    conv_x_bias,
    conv_bc_weight,
    conv_bc_bias,
    dt_bias,
    a_log,
    d_skip,
    gate_norm_gain,
    w_out,
    state_parts,
    seg_rate,
    x_tail,
    bc_tail,
):
    ctx, group, tp = (lax.axis_index(a) for a in ("ctx", "dp", "tp"))
    n_ctx, n_dp, n_tp = (lax.axis_size(a) for a in ("ctx", "dp", "tp"))
    peers = n_ctx * n_tp
    slots = state_parts.shape[1]
    heads = w_zx.shape[1]
    width = state_parts.shape[-1]
    steps = token_ids.shape[0]
    vocab_rows, features = embedding.shape
    model = norm_gain.shape[0]
    rows = steps * slots
    channels = heads * HEAD_DIM

    sent = pl.pallas_call(
        send_kernel,
        out_shape=jax.ShapeDtypeStruct((n_ctx, STATE_ROWS + SIDE_ROWS, width), BF),
        in_specs=[HB] * 5,
        out_specs=HB,
        scratch_shapes=[
            pltpu.SMEM(token_ids.shape, jnp.int32),
            pltpu.SMEM(decode_prompt.shape, jnp.int32),
            pltpu.SMEM(seg_rate.shape[1:], F32),
            pltpu.VMEM((features, vocab_rows), BF),
            pltpu.VMEM((slots, n_ctx, ONE_STATE, width), BF),
            pltpu.VMEM((n_dp * rows, LANES), jnp.int32),
            pltpu.VMEM((n_ctx * slots * heads, LANES), F32),
            pltpu.VMEM((n_ctx, RATE_ROWS, LANES), F32),
            pltpu.VMEM((n_ctx, SIDE_ROWS, LANES), BF),
            pltpu.SemaphoreType.DMA((6 + slots,)),
        ],
        compiler_params=PARAMS,
        name="send",
    )(
        in_hbm(token_ids),
        in_hbm(decode_prompt),
        in_hbm(seg_rate[0]),
        in_hbm(embedding.T),
        in_hbm(state_parts.reshape(slots, n_ctx, ONE_STATE, width)),
    )
    got = exchange(sent, "ctx")

    near_gain = norm_gain.reshape(2, n_ctx // 2, n_tp, features)
    near_gain = lax.dynamic_index_in_dim(near_gain, tp, 2, keepdims=False)
    near_gain = jnp.swapaxes(near_gain, 0, 1).reshape(n_ctx // 2, -1)
    tails = jnp.concatenate([x_tail.reshape(slots, 3, LANES), bc_tail.reshape(slots, 6, LANES)], axis=1)
    tails = jnp.pad(tails, ((0, 0), (0, TAIL_ROWS - tails.shape[1]), (0, 0)))
    wanted = decode_prompt.reshape(n_dp, slots) - group * slots
    prompt_for = jnp.any(wanted == 1, axis=1).astype(jnp.int32)

    def spread(values):
        return jnp.broadcast_to(values[:, None], (heads, HEAD_DIM)).reshape(1, channels)

    small = jnp.concatenate(
        [
            conv_x_weight.reshape(4, channels),
            conv_bc_weight[:, :width],
            conv_bc_weight[:, width:],
            conv_x_bias.reshape(1, channels),
            conv_bc_bias.reshape(2, width),
            spread(dt_bias),
            spread(a_log),
            spread(d_skip),
            gate_norm_gain.reshape(1, channels),
        ],
        axis=0,
    )
    small = jnp.pad(small, ((0, -small.shape[0] % 8), (0, 0)))

    got, near_gain, small = lax.optimization_barrier((got, near_gain, small))
    routed = pl.pallas_call(
        combine_kernel,
        out_shape=jax.ShapeDtypeStruct((n_dp, ONE_STATE + TAIL_ROWS + NEAR_ROWS, width), BF),
        in_specs=[SM, VM, VM],
        out_specs=HB,
        scratch_shapes=[
            pltpu.VMEM((slots, ONE_STATE + TAIL_ROWS, width), BF),
            pltpu.VMEM((n_dp, NEAR_ROWS, width), BF),
            pltpu.SemaphoreType.DMA((n_dp + 1,)),
        ],
        compiler_params=PARAMS,
        name="combine",
    )(prompt_for, got, tails)
    routed, w_bcdt = lax.optimization_barrier((routed, w_bcdt))
    arrived = exchange(routed, "dp")

    w_near = lax.all_gather(w_bcdt.T, "tp")
    own_columns = n_tp * w_bcdt.shape[1]
    w_near = w_near.reshape(own_columns, 2, n_ctx // 2, n_tp, features)
    w_near = lax.dynamic_index_in_dim(w_near, tp, 3, keepdims=False)
    w_near = jnp.swapaxes(w_near, 1, 2).reshape(own_columns, -1)
    w_near = jnp.concatenate([w_near, w_near], axis=0)
    w_near = jnp.pad(w_near, ((HALF, LANES - HALF - 2 * own_columns), (0, 0)))

    piece = pl.pallas_call(
        columns_kernel,
        out_shape=jax.ShapeDtypeStruct((peers, rows, LANES), BF),
        in_specs=[VM, VM, VM],
        out_specs=HB,
        scratch_shapes=[
            pltpu.VMEM((NEAR_ROWS // 8, 8, LANES), F32),
            pltpu.VMEM((peers, rows, LANES), BF),
            pltpu.SemaphoreType.DMA(()),
        ],
        compiler_params=PARAMS,
        name="columns",
    )(arrived, near_gain, w_near)
    piece, w_zx, w_out = lax.optimization_barrier((piece, w_zx, w_out))
    everyone = exchange(piece, BOTH)
    weights = jnp.concatenate(
        [w_zx.reshape(2 * channels, model), w_out.reshape(channels, model)], axis=0
    )

    outgoing, start, extra = pl.pallas_call(
        decode_kernel,
        out_shape=(
            jax.ShapeDtypeStruct((peers, rows, LANES), BF),
            jax.ShapeDtypeStruct((slots, ONE_STATE, width), BF),
            jax.ShapeDtypeStruct((24, LANES), F32),
        ),
        in_specs=[VM, VM, HB, HB, HB, HB],
        out_specs=(HB, VM, VM),
        scratch_shapes=[
            pltpu.VMEM((slots, ONE_STATE + TAIL_ROWS, width), BF),
            pltpu.SMEM(decode_prompt.shape, jnp.int32),
            pltpu.VMEM((model // LANES, LANES), F32),
            pltpu.VMEM(small.shape, F32),
            pltpu.VMEM((16, LANES), F32),
            pltpu.VMEM((16, LANES), F32),
            pltpu.VMEM((16, LANES), F32),
            pltpu.VMEM((peers, rows, LANES), BF),
            pltpu.SemaphoreType.DMA((3 + slots,)),
            pltpu.SemaphoreType.DMA((peers // 16,)),
        ],
        compiler_params=PARAMS,
        name="decode",
    )(
        everyone,
        weights,
        in_hbm(arrived),
        in_hbm(decode_prompt),
        in_hbm(norm_gain.reshape(model // LANES, LANES)),
        in_hbm(small),
    )
    incoming = exchange(outgoing, BOTH)

    push = extra[0:8].reshape(steps, slots, channels)
    b_conv = extra[8:16].reshape(steps, slots, width)
    kept = extra[16:18]
    final = kept[:, :, None] * start.astype(F32) + jnp.einsum(
        "tpc,tpn->pcn", push, b_conv, precision=lax.Precision.HIGHEST
    )

    mixed = pl.pallas_call(
        finish_kernel,
        out_shape=jax.ShapeDtypeStruct((rows, features), BF),
        in_specs=[VM],
        out_specs=VM,
        compiler_params=PARAMS,
        name="finish",
    )(incoming)
    return (
        mixed.reshape(steps, slots, features),
        final.reshape(slots, heads, HEAD_DIM, width),
    )


def solution(mesh):
    return jax.shard_map(
        per_device,
        mesh=mesh,
        in_specs=(
            P(),
            P(),
            P("dp", ("ctx", "tp")),
            P(),
            P(None, ("tp", "ctx"), None, None),
            P(None, ("ctx", "tp")),
            P(None, ("tp", "ctx"), None),
            P(("tp", "ctx"), None),
            P(),
            P(),
            P(("tp", "ctx")),
            P(("tp", "ctx")),
            P(("tp", "ctx")),
            P(("tp", "ctx"), None),
            P(("tp", "ctx"), None, None),
            P("ctx", "dp", "tp", None, None),
            P("ctx", "dp", "tp"),
            P("dp", None, ("tp", "ctx"), None),
            P("dp", None, None),
        ),
        out_specs=(P(None, "dp", ("ctx", "tp")), P("dp", ("tp", "ctx"), None, None)),
        check_vma=False,
    )
```

```python
import jax
import jax.numpy as jnp
from jax import lax
from jax.experimental import pallas as pl
from jax.experimental.pallas import tpu as pltpu
from jax.sharding import PartitionSpec as P

HEADS = 128
HEAD_DIM = 64
EPS = 1e-05
BOTH = ("ctx", "tp")
BF = jnp.bfloat16
F32 = jnp.float32
LANES = 128
HALF = 64
VMEM_LIMIT = 12 * 1024 * 1024

STATE_ROWS = 256
RATE_ROWS = 16
TOKEN_ROWS = 32
SIDE_ROWS = RATE_ROWS + TOKEN_ROWS
ONE_STATE = 128
TAIL_ROWS = 16
NEAR_ROWS = 16


def exchange(pieces, axis):
    return lax.all_to_all(pieces, axis, 0, 0, tiled=True)


def in_three(values):
    first = values.astype(BF)
    rest = values - first.astype(F32)
    second = rest.astype(BF)
    third = (rest - second.astype(F32)).astype(BF)
    return first, second, third


def silu(v):
    return v / (1.0 + jnp.exp(-v))


def low_half(shape=(8, LANES)):
    return lax.broadcasted_iota(jnp.int32, shape, 1) < HALF


def send_kernel(
    tokens_hbm, prompt_hbm, rate_hbm, table_hbm, states_hbm, out_ref,
    tokens_ref, prompt_ref, rate_ref, table_ref, states_ref, token_ref, rows_ref, block_ref, side_ref, sems,
):
    pairs = [
        (tokens_hbm, tokens_ref),
        (prompt_hbm, prompt_ref),
        (rate_hbm, rate_ref),
        (table_hbm, table_ref),
        (states_hbm, states_ref),
    ]
    loads = [pltpu.make_async_copy(a, b, sems.at[n]) for n, (a, b) in enumerate(pairs)]
    for load in loads:
        load.start()
    group = lax.axis_index("dp")
    count = out_ref.shape[0]
    slots = states_ref.shape[0]
    heads = rate_ref.shape[1] // count
    steps = tokens_ref.shape[0]
    rows = steps * slots
    groups = prompt_ref.shape[0] // slots
    vocab_rows = table_ref.shape[1]
    first = group * vocab_rows
    loads[0].wait()
    loads[1].wait()
    for g in range(groups):
        for step in range(steps):
            for slot in range(slots):
                token = tokens_ref[step, prompt_ref[g * slots + slot]] - first
                at = g * rows + step * slots + slot
                token_ref[at : at + 1, :] = jnp.full((1, LANES), token, jnp.int32)
    loads[2].wait()
    for c in range(count):
        for p in range(slots):
            for h in range(heads):
                at = (c * slots + p) * heads + h
                rows_ref[at : at + 1, :] = jnp.full((1, LANES), rate_ref[p, c * heads + h], F32)
    each = slots * heads
    parts = [p.astype(F32) for p in in_three(rows_ref[...])]
    for c in range(count):
        for n, part in enumerate(parts):
            block_ref[c, n * each : (n + 1) * each, :] = part[c * each : (c + 1) * each]
        block_ref[c, 3 * each : RATE_ROWS, :] = jnp.zeros((RATE_ROWS - 3 * each, LANES), F32)
        side_ref[c, 0:RATE_ROWS, :] = block_ref[c].astype(BF)
    loads[4].wait()
    stores = []
    for p in range(slots):
        stores.append(
            pltpu.make_async_copy(
                states_ref.at[p], out_ref.at[:, p * ONE_STATE : (p + 1) * ONE_STATE, :], sems.at[5 + p]
            )
        )
        stores[-1].start()
    loads[3].wait()
    tokens = token_ref[:, 0:1]
    found = jnp.zeros((groups * rows, LANES), F32)
    whole = vocab_rows // LANES * LANES
    bounds = [*range(0, whole, 1024), whole, vocab_rows]
    for low_at, high_at in zip(bounds[:-1], bounds[1:]):
        ids = lax.broadcasted_iota(jnp.int32, (groups * rows, high_at - low_at), 1) + low_at
        hot = jnp.where(tokens == ids, 1.0, 0.0).astype(BF)
        table = table_ref[:, low_at:high_at]
        found = found + lax.dot_general(
            hot,
            jnp.concatenate([table, table], axis=0),
            (((1,), (1,)), ((), ())),
            preferred_element_type=F32,
        )
    low = low_half((TOKEN_ROWS, LANES))
    tile = jnp.where(low, found[0:TOKEN_ROWS], found[TOKEN_ROWS : 2 * TOKEN_ROWS]).astype(BF)
    for c in range(count):
        side_ref[c, RATE_ROWS:SIDE_ROWS, :] = tile
    stores.append(
        pltpu.make_async_copy(
            side_ref, out_ref.at[:, STATE_ROWS : STATE_ROWS + SIDE_ROWS, :], sems.at[5 + slots]
        )
    )
    stores[-1].start()
    for store in stores:
        store.wait()


def combine_kernel(
    chosen_ref, got_ref, tails_ref, gain_ref, weight_ref, out_ref, bundle_ref, near_ref, sems
):
    count = got_ref.shape[0]
    groups = out_ref.shape[0]
    own_rows = ONE_STATE + TAIL_ROWS

    low = low_half((TOKEN_ROWS, LANES))
    at = STATE_ROWS + RATE_ROWS
    pieces = []
    for k in range(count // 2):
        one = got_ref[k, at : at + TOKEN_ROWS, :].astype(F32)
        two = got_ref[count // 2 + k, at : at + TOKEN_ROWS, :].astype(F32)
        early = jnp.where(low, one, pltpu.roll(two, HALF, 1))
        late = jnp.where(low, pltpu.roll(one, HALF, 1), two)
        rows = jnp.concatenate([early, late], axis=0)
        pieces.append((rows * gain_ref[k : k + 1, :]).astype(BF))
    partial = lax.dot_general(
        jnp.concatenate(pieces, axis=1),
        weight_ref[...],
        (((1,), (1,)), ((), ())),
        preferred_element_type=F32,
    )
    one = got_ref[lax.axis_index("ctx"), at : at + TOKEN_ROWS, :].astype(F32)
    own = jnp.concatenate([one, pltpu.roll(one, HALF, 1)], axis=0)
    lane = lax.broadcasted_iota(jnp.int32, own.shape, 1)
    first = partial.astype(BF).astype(F32)
    tiles = jnp.where(lane < HALF, own, jnp.where(lane < HALF + 24, first, partial - first))
    for g in range(groups):
        tile = jnp.concatenate([tiles[8 * g : 8 * g + 8], jnp.zeros((8, LANES), F32)], axis=0)
        near_ref[g] = tile.astype(BF)
    move_near = pltpu.make_async_copy(
        near_ref, out_ref.at[:, own_rows : own_rows + NEAR_ROWS, :], sems.at[groups]
    )
    move_near.start()

    rates = []
    for k in range(count):
        parts = got_ref[k, STATE_ROWS : STATE_ROWS + RATE_ROWS, :].astype(F32)
        rates.append(parts[0:4] + parts[4:8] + parts[8:12])
    weights = [None] * count
    later = jnp.zeros_like(rates[0])
    for k in reversed(range(count)):
        weights[k] = jnp.exp(-later)
        later = later + rates[k]
    for part in range(4):
        total = jnp.zeros((HEAD_DIM, LANES), F32)
        for k in range(count):
            own = got_ref[k, part * HEAD_DIM : (part + 1) * HEAD_DIM, :].astype(F32)
            total = total + (own * weights[k][part : part + 1]).astype(BF).astype(F32)
        at = (part % 2) * HEAD_DIM
        bundle_ref[part // 2, at : at + HEAD_DIM, :] = total.astype(BF)
    for p in range(bundle_ref.shape[0]):
        bundle_ref[p, ONE_STATE:own_rows, :] = tails_ref[p]
    moves = [
        pltpu.make_async_copy(
            bundle_ref.at[chosen_ref[g]], out_ref.at[g, 0:own_rows, :], sems.at[g]
        )
        for g in range(groups)
    ]
    for move in moves:
        move.start()
    for move in [*moves, move_near]:
        move.wait()


def spread_kernel(arrived_ref, out_ref, tile_ref, sem):
    at = ONE_STATE + TAIL_ROWS
    total = arrived_ref[0, at : at + NEAR_ROWS, :].astype(F32)
    for g in range(1, arrived_ref.shape[0]):
        total = total + arrived_ref[g, at : at + NEAR_ROWS, :].astype(F32)
    tile_ref[...] = jnp.broadcast_to(total[0:8].astype(BF)[None], tile_ref.shape)
    move = pltpu.make_async_copy(tile_ref, out_ref, sem)
    move.start()
    move.wait()


def decode_kernel(
    everyone_ref, weights_ref, arrived_hbm, prompt_hbm, gain_hbm, small_hbm, out_ref, start_ref, extra_ref,
    arrived_ref, prompt_ref, gain_ref, small_ref, x_ref, b_ref, c_ref, tile_ref, load_sems, sems,
):
    pairs = [(prompt_hbm, prompt_ref), (gain_hbm, gain_ref), (small_hbm, small_ref)]
    loads = [pltpu.make_async_copy(a, b, load_sems.at[n]) for n, (a, b) in enumerate(pairs)]
    for load in loads:
        load.start()
    ctx, group, tp = (lax.axis_index(a) for a in ("ctx", "dp", "tp"))
    head_at = (tp * lax.axis_size("ctx") + ctx) * 2
    peers = everyone_ref.shape[0]
    model = peers * HALF
    lane = lax.broadcasted_iota(jnp.int32, (8, LANES), 1)
    row = lax.broadcasted_iota(jnp.int32, (8, LANES), 0)
    low = lane < HALF

    tiles = [everyone_ref[p].astype(F32) for p in range(peers)]
    rows = [
        jnp.where(low, tiles[2 * n], pltpu.roll(tiles[2 * n + 1], HALF, 1)) for n in range(peers // 2)
    ]
    squares = rows[0] * rows[0]
    for r in rows[1:]:
        squares = squares + r * r
    own_rows = arrived_ref.shape[1]
    loads[0].wait()
    for slot in range(2):
        holder = prompt_ref[group * 2 + slot] // 2
        loads.append(
            pltpu.make_async_copy(
                arrived_hbm.at[holder, 0:own_rows, :], arrived_ref.at[slot], load_sems.at[3 + slot]
            )
        )
        loads[-1].start()
    loads[1].wait()
    inverse = lax.rsqrt(jnp.sum(squares, axis=1, keepdims=True) * (1.0 / model) + EPS)
    normed = jnp.concatenate(
        [(r * inverse * gain_ref[n : n + 1, :]).astype(BF) for n, r in enumerate(rows)], axis=1
    )

    projected = lax.dot_general(
        normed, weights_ref[0 : 2 * LANES, :], (((1,), (1,)), ((), ())), preferred_element_type=F32
    )

    columns = [jnp.zeros((8, LANES), F32) for _ in range(3)]
    for c in range(16):
        part = tiles[4 * c] + tiles[4 * c + 1] + tiles[4 * c + 2] + tiles[4 * c + 3]
        part = part + pltpu.roll(part, LANES - 24, 1)
        part = jnp.where((lane >= HALF) & (lane < HALF + 24), part, 0.0)
        first, offset = divmod(c * 24, LANES)
        part = pltpu.roll(part, (offset - HALF) % LANES, 1)
        if offset + 24 <= LANES:
            columns[first] = columns[first] + part
        else:
            columns[first] = columns[first] + jnp.where(lane >= offset, part, 0.0)
            columns[first + 1] = columns[first + 1] + jnp.where(lane < offset, part, 0.0)
    columns = [v * inverse for v in columns]

    for load in loads[2:]:
        load.wait()

    for slot in range(2):
        tail = arrived_ref[slot, ONE_STATE : ONE_STATE + TAIL_ROWS, :].astype(F32)
        for k in range(3):
            at = 2 * k + slot
            x_ref[at : at + 1, :] = tail[k : k + 1]
            b_ref[at : at + 1, :] = tail[3 + 2 * k : 4 + 2 * k]
            c_ref[at : at + 1, :] = tail[4 + 2 * k : 5 + 2 * k]
    b_ref[6:14, :] = columns[0]
    c_ref[6:14, :] = columns[1]

    def convolved(ref, weight_at, bias_at):
        total = ref[0:8, :] * small_ref[weight_at : weight_at + 1, :]
        for k in range(1, 4):
            total = total + ref[2 * k : 2 * k + 8, :] * small_ref[weight_at + k : weight_at + k + 1, :]
        return silu(total + small_ref[bias_at : bias_at + 1, :])

    b_conv = convolved(b_ref, 4, 13)
    c_conv = convolved(c_ref, 8, 14)

    raw = pltpu.roll(columns[2], lax.rem(LANES - head_at, LANES), 1)
    raw = jnp.where(low, raw[:, 0:1], raw[:, 1:2]) + small_ref[15:16, :]
    step = jnp.maximum(raw, 0.0) + jnp.log1p(jnp.exp(-jnp.abs(raw)))
    log_retain = -step * jnp.exp(small_ref[16:17, :])

    def earlier(v, lag):
        return jnp.where(row >= 2 * lag, pltpu.roll(v, 2 * lag, 0), 0.0)

    log_total = log_retain
    for lag in range(1, 4):
        log_total = log_total + earlier(log_retain, lag)

    c_parts = jnp.concatenate([p.astype(F32) for p in in_three(c_conv)], axis=0).astype(BF)
    from_start = []
    for slot in range(2):
        state = arrived_ref[slot, 0:ONE_STATE, :]
        start_ref[slot] = state
        product = lax.dot_general(
            c_parts, state, (((1,), (1,)), ((), ())), preferred_element_type=F32
        )
        from_start.append(product[0:8] + product[8:16] + product[16:24])
    y = jnp.exp(log_total) * jnp.where(row % 2 == 0, from_start[0], from_start[1])

    gate = projected[:, 0:LANES]
    x_ref[6:14, :] = projected[:, LANES : 2 * LANES]
    x_conv = convolved(x_ref, 0, 12)
    drive = step * x_conv
    y = y + small_ref[17:18, :] * x_conv
    for lag in range(4):
        match = jnp.sum(c_conv * earlier(b_conv, lag), axis=1, keepdims=True)
        if lag == 0:
            y = y + drive * match
        else:
            decay = jnp.exp(log_total - earlier(log_total, lag))
            y = y + decay * earlier(drive, lag) * match
    gated = y * silu(gate)
    total = jnp.sum(gated * gated, axis=1, keepdims=True)
    parts = [p.astype(F32) for p in in_three(total)]
    aside = jnp.where(
        lane == HALF,
        parts[0],
        jnp.where(lane == HALF + 1, parts[1], jnp.where(lane == HALF + 2, parts[2], 0.0)),
    )
    weighted = (gated * small_ref[18:19, :]).astype(BF)

    last = jnp.where(row % 2 == 0, log_total[6:7], log_total[7:8])
    extra_ref[0:8, :] = jnp.exp(last - log_total) * drive
    extra_ref[8:16, :] = b_conv
    extra_ref[16:24, :] = jnp.exp(last)

    moves = []
    for n in range(peers // 16):
        wide = jnp.dot(
            weighted, weights_ref[2 * LANES :, n * 1024 : (n + 1) * 1024], preferred_element_type=F32
        )
        for m in range(8):
            piece = wide[:, m * LANES : (m + 1) * LANES]
            tile_ref[16 * n + 2 * m] = jnp.where(low, piece, aside).astype(BF)
            tile_ref[16 * n + 2 * m + 1] = jnp.where(low, pltpu.roll(piece, HALF, 1), aside).astype(BF)
        part = pl.ds(16 * n, 16)
        moves.append(pltpu.make_async_copy(tile_ref.at[part], out_ref.at[part], sems.at[n]))
        moves[-1].start()
    for move in moves:
        move.wait()


def finish_kernel(incoming_ref, out_ref):
    total = incoming_ref[0].astype(F32)
    for p in range(1, incoming_ref.shape[0]):
        total = total + incoming_ref[p].astype(F32)
    squares = total[:, HALF : HALF + 1] + total[:, HALF + 1 : HALF + 2] + total[:, HALF + 2 : HALF + 3]
    scale = lax.rsqrt(squares * (1.0 / (HEADS * HEAD_DIM)) + EPS)
    out_ref[...] = (total[:, 0:HALF] * scale).astype(BF)


VM = pl.BlockSpec(memory_space=pltpu.VMEM)
SM = pl.BlockSpec(memory_space=pltpu.SMEM)
HB = pl.BlockSpec(memory_space=pltpu.HBM)


def in_hbm(array):
    return pltpu.with_memory_space_constraint(array, pltpu.HBM)


PARAMS = pltpu.CompilerParams(vmem_limit_bytes=VMEM_LIMIT)


def per_device(
    token_ids,
    decode_prompt,
    embedding,
    norm_gain,
    w_zx,
    w_bcdt,
    conv_x_weight,
    conv_x_bias,
    conv_bc_weight,
    conv_bc_bias,
    dt_bias,
    a_log,
    d_skip,
    gate_norm_gain,
    w_out,
    state_parts,
    seg_rate,
    x_tail,
    bc_tail,
):
    ctx, group, tp = (lax.axis_index(a) for a in ("ctx", "dp", "tp"))
    n_ctx, n_dp, n_tp = (lax.axis_size(a) for a in ("ctx", "dp", "tp"))
    peers = n_ctx * n_tp
    slots = state_parts.shape[1]
    heads = w_zx.shape[1]
    width = state_parts.shape[-1]
    steps = token_ids.shape[0]
    vocab_rows, features = embedding.shape
    model = norm_gain.shape[0]
    rows = steps * slots
    channels = heads * HEAD_DIM

    sent = pl.pallas_call(
        send_kernel,
        out_shape=jax.ShapeDtypeStruct((n_ctx, STATE_ROWS + SIDE_ROWS, width), BF),
        in_specs=[HB] * 5,
        out_specs=HB,
        scratch_shapes=[
            pltpu.SMEM(token_ids.shape, jnp.int32),
            pltpu.SMEM(decode_prompt.shape, jnp.int32),
            pltpu.SMEM(seg_rate.shape[1:], F32),
            pltpu.VMEM((features, vocab_rows), BF),
            pltpu.VMEM((slots, n_ctx, ONE_STATE, width), BF),
            pltpu.VMEM((n_dp * rows, LANES), jnp.int32),
            pltpu.VMEM((n_ctx * slots * heads, LANES), F32),
            pltpu.VMEM((n_ctx, RATE_ROWS, LANES), F32),
            pltpu.VMEM((n_ctx, SIDE_ROWS, LANES), BF),
            pltpu.SemaphoreType.DMA((6 + slots,)),
        ],
        compiler_params=PARAMS,
        name="send",
    )(
        in_hbm(token_ids),
        in_hbm(decode_prompt),
        in_hbm(seg_rate[0]),
        in_hbm(embedding.T),
        in_hbm(state_parts.reshape(slots, n_ctx, ONE_STATE, width)),
    )
    got = exchange(sent, "ctx")

    own_columns = n_tp * w_bcdt.shape[1]
    quarters = w_bcdt.T.reshape(-1, 2, n_ctx // 2, n_tp, features)
    quarters = jnp.transpose(quarters, (3, 0, 2, 1, 4)).reshape(n_tp, w_bcdt.shape[1], -1)
    w_near = jnp.zeros_like(quarters)
    for step in range(n_tp):
        piece = lax.dynamic_index_in_dim(quarters, (tp + step) % n_tp, 0, keepdims=True)
        if step:
            piece = lax.ppermute(piece, "tp", [(t, (t + step) % n_tp) for t in range(n_tp)])
        w_near = lax.dynamic_update_slice_in_dim(w_near, piece, (tp - step) % n_tp, 0)
    w_near = w_near.reshape(own_columns, -1)
    w_near = jnp.concatenate([w_near, w_near], axis=0)
    w_near = jnp.pad(w_near, ((HALF, LANES - HALF - 2 * own_columns), (0, 0)))
    near_gain = norm_gain.reshape(2, n_ctx // 2, n_tp, features)
    near_gain = lax.dynamic_index_in_dim(near_gain, tp, 2, keepdims=False)
    near_gain = jnp.swapaxes(near_gain, 0, 1).reshape(n_ctx // 2, -1)
    tails = jnp.concatenate([x_tail.reshape(slots, 3, LANES), bc_tail.reshape(slots, 6, LANES)], axis=1)
    tails = jnp.pad(tails, ((0, 0), (0, TAIL_ROWS - tails.shape[1]), (0, 0)))
    wanted = decode_prompt.reshape(n_dp, slots) - group * slots
    prompt_for = jnp.any(wanted == 1, axis=1).astype(jnp.int32)

    def spread(values):
        return jnp.broadcast_to(values[:, None], (heads, HEAD_DIM)).reshape(1, channels)

    small = jnp.concatenate(
        [
            conv_x_weight.reshape(4, channels),
            conv_bc_weight[:, :width],
            conv_bc_weight[:, width:],
            conv_x_bias.reshape(1, channels),
            conv_bc_bias.reshape(2, width),
            spread(dt_bias),
            spread(a_log),
            spread(d_skip),
            gate_norm_gain.reshape(1, channels),
        ],
        axis=0,
    )
    small = jnp.pad(small, ((0, -small.shape[0] % 8), (0, 0)))

    routed = pl.pallas_call(
        combine_kernel,
        out_shape=jax.ShapeDtypeStruct((n_dp, ONE_STATE + TAIL_ROWS + NEAR_ROWS, width), BF),
        in_specs=[SM, VM, VM, VM, VM],
        out_specs=HB,
        scratch_shapes=[
            pltpu.VMEM((slots, ONE_STATE + TAIL_ROWS, width), BF),
            pltpu.VMEM((n_dp, NEAR_ROWS, width), BF),
            pltpu.SemaphoreType.DMA((n_dp + 1,)),
        ],
        compiler_params=PARAMS,
        name="combine",
    )(prompt_for, got, tails, near_gain, w_near)
    arrived = exchange(routed, "dp")

    piece = pl.pallas_call(
        spread_kernel,
        out_shape=jax.ShapeDtypeStruct((peers, rows, LANES), BF),
        in_specs=[VM],
        out_specs=HB,
        scratch_shapes=[
            pltpu.VMEM((peers, rows, LANES), BF),
            pltpu.SemaphoreType.DMA(()),
        ],
        compiler_params=PARAMS,
        name="spread",
    )(arrived)
    piece, w_zx, w_out = lax.optimization_barrier((piece, w_zx, w_out))
    everyone = exchange(piece, BOTH)
    weights = jnp.concatenate(
        [w_zx.reshape(2 * channels, model), w_out.reshape(channels, model)], axis=0
    )

    outgoing, start, extra = pl.pallas_call(
        decode_kernel,
        out_shape=(
            jax.ShapeDtypeStruct((peers, rows, LANES), BF),
            jax.ShapeDtypeStruct((slots, ONE_STATE, width), BF),
            jax.ShapeDtypeStruct((24, LANES), F32),
        ),
        in_specs=[VM, VM, HB, HB, HB, HB],
        out_specs=(HB, VM, VM),
        scratch_shapes=[
            pltpu.VMEM((slots, ONE_STATE + TAIL_ROWS, width), BF),
            pltpu.SMEM(decode_prompt.shape, jnp.int32),
            pltpu.VMEM((model // LANES, LANES), F32),
            pltpu.VMEM(small.shape, F32),
            pltpu.VMEM((16, LANES), F32),
            pltpu.VMEM((16, LANES), F32),
            pltpu.VMEM((16, LANES), F32),
            pltpu.VMEM((peers, rows, LANES), BF),
            pltpu.SemaphoreType.DMA((3 + slots,)),
            pltpu.SemaphoreType.DMA((peers // 16,)),
        ],
        compiler_params=PARAMS,
        name="decode",
    )(
        everyone,
        weights,
        in_hbm(arrived),
        in_hbm(decode_prompt),
        in_hbm(norm_gain.reshape(model // LANES, LANES)),
        in_hbm(small),
    )
    incoming = exchange(outgoing, BOTH)

    push = extra[0:8].reshape(steps, slots, channels)
    b_conv = extra[8:16].reshape(steps, slots, width)
    kept = extra[16:18]
    final = kept[:, :, None] * start.astype(F32) + jnp.einsum(
        "tpc,tpn->pcn", push, b_conv, precision=lax.Precision.HIGHEST
    )

    mixed = pl.pallas_call(
        finish_kernel,
        out_shape=jax.ShapeDtypeStruct((rows, features), BF),
        in_specs=[VM],
        out_specs=VM,
        compiler_params=PARAMS,
        name="finish",
    )(incoming)
    return (
        mixed.reshape(steps, slots, features),
        final.reshape(slots, heads, HEAD_DIM, width),
    )


def solution(mesh):
    return jax.shard_map(
        per_device,
        mesh=mesh,
        in_specs=(
            P(),
            P(),
            P("dp", ("ctx", "tp")),
            P(),
            P(None, ("tp", "ctx"), None, None),
            P(None, ("ctx", "tp")),
            P(None, ("tp", "ctx"), None),
            P(("tp", "ctx"), None),
            P(),
            P(),
            P(("tp", "ctx")),
            P(("tp", "ctx")),
            P(("tp", "ctx")),
            P(("tp", "ctx"), None),
            P(("tp", "ctx"), None, None),
            P("ctx", "dp", "tp", None, None),
            P("ctx", "dp", "tp"),
            P("dp", None, ("tp", "ctx"), None),
            P("dp", None, None),
        ),
        out_specs=(P(None, "dp", ("ctx", "tp")), P("dp", ("tp", "ctx"), None, None)),
        check_vma=False,
    )
```
